32 devices in a mesh: grp: 8 (over z, y), seq: 4 (over x, core).
Axes of the slice: x: 2, y: 2, z: 4, core: 2. Of those that a mesh axis runs over, the one named last changes fastest.
Arguments:
- encoded: bfloat16 [8, 4, 1024, 768], P('grp', 'seq'), may hold values from -6 to 6
- destination: int32 [8, 4, 128], replicated, may hold values from 0 to 7, as said below
- expressed: int32 [8, 4, 1024], replicated, may hold values from 0 to 1, as said below
- in_proj: bfloat16 [768, 512], replicated, may hold values from -0.21875 to 0.21875
- gain_one: float32 [512], replicated, may hold values from 0.5 to 1.5
- shift_one: float32 [512], replicated, may hold values from -1 to 1
- query_w: bfloat16 [512, 512], replicated, may hold values from -0.25 to 0.25
- key_w: bfloat16 [512, 512], replicated, may hold values from -0.25 to 0.25
- value_w: bfloat16 [512, 512], replicated, may hold values from -0.25 to 0.25
- out_w: bfloat16 [512, 512], replicated, may hold values from -6 to 6
- gain_two: float32 [512], replicated, may hold values from 0.5 to 1.5
- shift_two: float32 [512], replicated, may hold values from -1 to 1
- up_w: bfloat16 [512, 2048], replicated, may hold values from -0.25 to 0.25
- down_w: bfloat16 [2048, 512], replicated, may hold values from -0.125 to 0.125
- random_features: bfloat16 [64, 256], replicated, may hold values from -4 to 4
- out_cotangent: bfloat16 [8, 4, 2048, 512], P('grp', 'seq'), may hold values from -6 to 6
Outputs:
- layer_out: float32 [8, 4, 2048, 512], P('grp', 'seq')
- encoded_grad: bfloat16 [8, 4, 1024, 768], P('grp', 'seq')
- in_proj_grad: float32 [768, 512], replicated
- gain_one_grad: float32 [512], replicated
- shift_one_grad: float32 [512], replicated
- query_grad: float32 [512, 512], replicated
- key_grad: float32 [512, 512], replicated
- value_grad: float32 [512, 512], replicated
- out_w_grad: float32 [512, 512], replicated
- gain_two_grad: float32 [512], replicated
- shift_two_grad: float32 [512], replicated
- up_grad: float32 [512, 2048], replicated
- down_grad: float32 [2048, 512], replicated
The draws below stay inside these ranges and needn't reach their ends.
Inputs may be any that keep to these rules, and one draw needn't show every extreme that they name: `destination`: each device's 128 blocks name every cell at least once and no cell more than 32 times; for each split index one cell receives exactly 32 blocks from every device of that split index. `expressed`: on source (c', s), the first token of the first block whose destination is c' is 1.
All inputs are finite; a program needn't handle non-finite values.
Results may differ from the reference program's by a relative error of at most 0.03.
Values may be sent and summed in bfloat16 or wider, within the bound.
A program may use at most 256 MiB of HBM per device.

```python
import jax
import jax.numpy as jnp
from jax import lax

D_IN = 768
D = 512
HEADS = 8
DH = 64
FEATS = 256
FF = 2048
BLK = 8
BLK_DEV = 128
TOK_DEV = 1024
CELLS = 8
SPLITS = 4
CAP = 32
ROWS = 2048


def route_helper(key):
    extra_count = BLK_DEV - CELLS - CAP + 1
    spare_slots = jnp.repeat(jnp.arange(CELLS, dtype=jnp.int32), CAP - 1)
    spare_len = spare_slots.shape[0]
    heavy_base = jax.random.fold_in(key, 1)
    source_base = jax.random.fold_in(key, 2)

    def one_source(position):
        split_index = position % SPLITS
        heavy_cell = jax.random.randint(jax.random.fold_in(heavy_base, split_index), (), 0, CELLS).astype(jnp.int32)
        pick_key, order_key = jax.random.split(jax.random.fold_in(source_base, position))
        priority = jax.random.permutation(pick_key, spare_len).astype(jnp.int32) + (spare_slots == heavy_cell).astype(jnp.int32) * spare_len
        chosen = spare_slots[jnp.argsort(priority, stable=True)[:extra_count]]
        listed = jnp.concatenate([jnp.arange(CELLS, dtype=jnp.int32), jnp.full((CAP - 1,), heavy_cell, jnp.int32), chosen])
        return jax.random.permutation(order_key, listed).astype(jnp.int32)
    routed = jax.vmap(one_source)(jnp.arange(CELLS * SPLITS, dtype=jnp.int32))
    return routed.reshape(CELLS, SPLITS, BLK_DEV)


def draw_destination(key, part):
    routed = route_helper(key)
    return routed


def draw_expressed(key, part):
    routed = route_helper(key)
    key = jax.random.fold_in(key, 5)
    kind_key, level_key, coin_key = jax.random.split(key, 3)
    bulk_index = jax.random.randint(kind_key, (), 0, CELLS)
    bulk_cell = jnp.arange(CELLS, dtype=jnp.int32) == bulk_index
    sparse_level = jax.random.randint(level_key, (CELLS,), 26, 101)
    per_mille = jnp.where(bulk_cell, 950, sparse_level).astype(jnp.int32)
    per_token = jnp.repeat(per_mille[routed], BLK, axis=2)
    coin_draw = jax.random.randint(coin_key, (CELLS, SPLITS, BLK_DEV * BLK), 0, 1000)
    own_hits = (routed == jnp.arange(CELLS, dtype=jnp.int32)[:, None, None]).astype(jnp.int32)
    first_own = (own_hits == 1) & (jnp.cumsum(own_hits, axis=2) == 1)
    token_first = jnp.repeat(first_own, BLK, axis=2) & (jnp.arange(BLK_DEV * BLK, dtype=jnp.int32) % BLK == 0)
    return jnp.where(token_first | (coin_draw < per_token), 1, 0).astype(jnp.int32)


def block_scale(key, dims, shards, least, high):
    level = 1.0
    for axis_at, blocks in shards:
        draws = jax.random.uniform(jax.random.fold_in(jax.random.fold_in(key, 6), axis_at), (blocks,), jnp.float32, least / len(shards), high / len(shards))
        level = level * jnp.repeat(jnp.exp(draws), dims[axis_at] // blocks).reshape((-1,) + (1,) * (len(dims) - 1 - axis_at))
    return level


def noise(key, dims, deviation, bound, cuts=(), kind=jnp.bfloat16):
    entries = deviation * jax.random.normal(key, dims, jnp.float32)
    if cuts:
        entries = entries * block_scale(key, dims, cuts, -0.22, 0.18)
    return jnp.clip(entries, -bound, bound).astype(kind)


def setup_inputs(seed: int = 0) -> dict:
    seeds = jax.random.split(jax.random.key(seed), 17)
    encoded = noise(seeds[0], (CELLS, SPLITS, TOK_DEV, D_IN), 1.0, 6.0, ((0, 8), (1, 4)))
    destination = draw_destination(jax.random.fold_in(seeds[16], 71), 0)
    expressed = draw_expressed(jax.random.fold_in(seeds[16], 71), 0)
    in_proj = noise(seeds[3], (D_IN, D), D_IN ** -0.5, 0.21875)
    gain_one = jnp.clip(1.0 + 0.1 * jax.random.normal(seeds[4], (D,), jnp.float32), 0.5, 1.5)
    shift_one = noise(seeds[5], (D,), 0.2, 1.0, (), jnp.float32)
    query_w = noise(seeds[6], (D, D), D ** -0.5, 0.25)
    key_w = noise(seeds[7], (D, D), D ** -0.5, 0.25)
    value_w = noise(seeds[8], (D, D), D ** -0.5, 0.25)
    out_w = noise(seeds[9], (D, D), (max(1, 4 * D // (TOK_DEV * SPLITS))) ** -0.5, 6.0)
    gain_two = jnp.clip(1.0 + 0.1 * jax.random.normal(seeds[10], (D,), jnp.float32), 0.5, 1.5)
    shift_two = noise(seeds[11], (D,), 0.2, 1.0, (), jnp.float32)
    up_w = noise(seeds[12], (D, FF), D ** -0.5, 0.25)
    down_w = noise(seeds[13], (FF, D), FF ** -0.5, 0.125)
    random_features = noise(seeds[14], (DH, FEATS), 1.0, 4.0)
    out_cotangent = noise(seeds[15], (CELLS, SPLITS, ROWS, D), 1.0, 6.0, ((0, 8), (1, 4)))
    return dict(encoded=encoded, destination=destination, expressed=expressed, in_proj=in_proj, gain_one=gain_one, shift_one=shift_one, query_w=query_w, key_w=key_w, value_w=value_w, out_w=out_w, gain_two=gain_two, shift_two=shift_two, up_w=up_w, down_w=down_w, random_features=random_features, out_cotangent=out_cotangent)


@jax.custom_vjp
def lower_precision(v):
    return lax.optimization_barrier(v.astype(jnp.bfloat16)).astype(jnp.float32)

@jax.custom_vjp
def lower_precision_backward(v):
    return v

def low_keep(v):
    return (lower_precision(v), None)

def low_pass(kept, grad):
    return (grad,)

def back_keep(v):
    return (v, None)

def back_low(kept, grad):
    return (lower_precision(grad),)
lower_precision.defvjp(low_keep, low_pass)
lower_precision_backward.defvjp(back_keep, back_low)

def layer_norm(values, gain, shift):
    center = values - lax.optimization_barrier(jnp.mean(values, axis=-1, keepdims=True))
    variance = lax.optimization_barrier(jnp.mean(center * center, axis=-1, keepdims=True))
    return center * lax.rsqrt(variance + 1e-05) * gain + shift

def feature_map(projected, omega_full, key_keep):
    row_count = projected.shape[0]
    pieces = projected.reshape(row_count, HEADS, DH)
    factor = DH ** (-0.25)
    logits = lower_precision_backward(jnp.einsum('nhd,dm->nhm', pieces, omega_full, precision=lax.Precision.HIGHEST) * factor)
    squares = 0.5 * factor * factor * lax.optimization_barrier(jnp.sum(pieces * pieces, axis=-1, keepdims=True))
    return lower_precision_backward(lower_precision(jnp.exp(logits - squares) * FEATS ** (-0.5) * key_keep[:, None, None]))

def matmul_high(left, right):
    return jnp.dot(left, right, precision=lax.Precision.HIGHEST)

def cell_forward(params, omega_full, rows_in, key_keep, valid):
    in_proj, gain_one, shift_one, query_w, key_w, value_w, out_w, gain_two, shift_two, up_w, down_w = params
    row_count = rows_in.shape[0]
    hidden = lower_precision_backward(lower_precision(matmul_high(rows_in, in_proj)))
    normed = lower_precision(layer_norm(hidden, gain_one, shift_one))
    queries = lower_precision_backward(lower_precision(matmul_high(normed, query_w)))
    key_rows = lower_precision_backward(lower_precision(matmul_high(normed, key_w)))
    values = lower_precision_backward(lower_precision(matmul_high(normed, value_w)))
    query_feature_rows = feature_map(queries, omega_full, jnp.ones((row_count,), jnp.float32))
    key_feature_rows = feature_map(key_rows, omega_full, key_keep)
    value_per_head = values.reshape(row_count, HEADS, DH)
    key_value_products = lower_precision_backward(lower_precision(jnp.einsum('pgk,pgz->gkz', key_feature_rows, value_per_head, precision=lax.Precision.HIGHEST)))
    key_total = lax.optimization_barrier(jnp.sum(key_feature_rows, axis=0))
    attention_numerator = lower_precision_backward(jnp.einsum('bli,lie->ble', query_feature_rows, key_value_products, precision=lax.Precision.HIGHEST))
    denominator = lax.optimization_barrier(jnp.sum(query_feature_rows * key_total[None], axis=-1))
    attended = lower_precision((attention_numerator / denominator[:, :, None]).reshape(row_count, HEADS * DH))
    mixed = hidden + lower_precision_backward(matmul_high(attended, out_w))
    normed_two = lower_precision(layer_norm(mixed, gain_two, shift_two))
    expanded = lower_precision_backward(matmul_high(normed_two, up_w))
    activated = lower_precision(jax.nn.gelu(expanded, approximate=True))
    result = mixed + lower_precision_backward(matmul_high(activated, down_w))
    return result * valid[:, None]

def routing_tables(destination):
    targets = jnp.arange(CELLS, dtype=jnp.int32)
    block_hits = (destination[:, :, :, None] == targets).astype(jnp.int32)
    block_rank = lax.optimization_barrier(jnp.sum(jnp.cumsum(block_hits, axis=2) * block_hits, axis=3)) - 1
    slot_ids = jnp.arange(CAP, dtype=jnp.int32)
    matched = ((block_hits[:, :, :, :, None] == 1) & (block_rank[:, :, :, None, None] == slot_ids)).astype(jnp.int32)
    found = lax.optimization_barrier(jnp.sum(matched, axis=2))
    block_at = lax.optimization_barrier(jnp.sum(matched * jnp.arange(BLK_DEV, dtype=jnp.int32)[:, None, None], axis=2))
    return (found, block_at)

def arrange(table):
    moved = jnp.swapaxes(table, 0, 2)
    return moved.reshape((CELLS, SPLITS * ROWS) + table.shape[5:])

def reference(encoded, destination, expressed, in_proj, gain_one, shift_one, query_w, key_w, value_w, out_w, gain_two, shift_two, up_w, down_w, random_features, out_cotangent):
    found, block_at = routing_tables(destination)
    token_index = (block_at[..., None] * BLK + jnp.arange(BLK, dtype=jnp.int32)).astype(jnp.int32)
    source_index = jnp.arange(CELLS, dtype=jnp.int32)[:, None, None, None, None]
    split_index = jnp.arange(SPLITS, dtype=jnp.int32)[None, :, None, None, None]
    present = jnp.broadcast_to(found[..., None], token_index.shape).astype(jnp.float32)
    valid = arrange(present)
    key_keep = arrange(expressed[source_index, split_index, token_index].astype(jnp.float32) * present)
    block_sum = lax.optimization_barrier(jnp.sum(expressed.reshape(CELLS, SPLITS, BLK_DEV, BLK), axis=3)).astype(jnp.float32)
    dest_hits = (destination[..., None] == jnp.arange(CELLS, dtype=jnp.int32)).astype(jnp.float32)
    counts = lax.optimization_barrier(jnp.sum(dest_hits * block_sum[..., None], axis=(0, 1, 2)))
    share = CELLS * counts / jnp.sum(counts)
    weight_list = (in_proj, gain_one, shift_one, query_w, key_w, value_w, out_w, gain_two, shift_two, up_w, down_w)
    params = tuple((item.astype(jnp.float32) for item in weight_list))
    omega_full = random_features.astype(jnp.float32)

    def forward(params, encoded_full):
        gathered = encoded_full[source_index, split_index, token_index] * present[..., None]
        rows_in = arrange(gathered)

        def one_cell(items):
            return jax.checkpoint(cell_forward)(params, omega_full, items[0], items[1], items[2])
        result = lax.map(one_cell, (rows_in, key_keep, valid))
        return result.reshape(CELLS, SPLITS, ROWS, D)
    outputs, pullback = jax.vjp(forward, params, encoded.astype(jnp.float32))
    weighted = out_cotangent.astype(jnp.float32) * share[:, None, None, None]
    grads, encoded_grad = pullback(weighted)
    return (outputs, encoded_grad.astype(jnp.bfloat16), grads[0], grads[1], grads[2], grads[3], grads[4], grads[5], grads[6], grads[7], grads[8], grads[9], grads[10])
```

```python
import functools
import jax, jax.numpy as jnp
from jax import lax
from jax.experimental import pallas as pl
from jax.experimental.pallas import tpu as pltpu
MESH = pl.DeviceIdType.MESH

def bits_of(mesh_shape):
    sb = (mesh_shape["seq"]).bit_length() - 1
    gb = (mesh_shape["grp"]).bit_length() - 1
    return [("seq", i) for i in range(sb)] + [("grp", i) for i in range(gb)]

def partner(bit):
    g = lax.axis_index("grp"); s = lax.axis_index("seq")
    ax, i = bit
    b = 1 << i
    if ax == "seq":
        v = (s // b) % 2
        return (g, s + b - 2 * b * v), v
    v = (g // b) % 2
    return (g + b - 2 * b * v, s), v

class AR:
    def __init__(self, x_ref, out_ref, recv_ref, ss, rs, chunks):
        self.x, self.out, self.recv, self.ss, self.rs = x_ref, out_ref, recv_ref, ss, rs
        self.chunks = chunks
        n = len(chunks[0][2])
        self.n = n
        self.lo = [c[0] for c in chunks]
        self.len = [c[1] for c in chunks]
        self.roff = [c[3] for c in chunks]
        self.hist = [[] for _ in chunks]
        self.pend = [None] * len(chunks)
    def start(self, c, k):
        n = self.n
        order = self.chunks[c][2]
        sem = self.chunks[c][4]
        if k < n:
            dev, v = partner(order[k])
            half = self.len[c] // 2
            keep = self.lo[c] + v * half
            send = self.lo[c] + (1 - v) * half
            cp = pltpu.make_async_remote_copy(src_ref=self.x.at[pl.ds(pl.multiple_of(send, 16), half)], dst_ref=self.recv.at[pl.ds(self.roff[c], half)],
                send_sem=self.ss.at[sem + k], recv_sem=self.rs.at[sem + k], device_id=dev, device_id_type=MESH)
            self.pend[c] = (cp, keep, half, self.roff[c])
            self.hist[c].append((self.lo[c], self.len[c]))
            self.lo[c] = keep; self.len[c] = half
            self.roff[c] += half
            cp.start()
        else:
            dev, v = partner(order[2 * n - 1 - k])
            lo, ln = self.lo[c], self.len[c]
            r = self.out.at[pl.ds(pl.multiple_of(lo, 16), ln)]
            cp = pltpu.make_async_remote_copy(src_ref=r, dst_ref=r, send_sem=self.ss.at[sem + k], recv_sem=self.rs.at[sem + k], device_id=dev, device_id_type=MESH)
            self.pend[c] = (cp, None, None, None)
            self.lo[c], self.len[c] = self.hist[c].pop()
            cp.start()
    def finish(self, c, k):
        cp, keep, half, roff = self.pend[c]
        cp.wait()
        if k < self.n:
            sl = pl.ds(pl.multiple_of(keep, 16), half)
            dst = self.out if k == self.n - 1 else self.x
            step = 128 if half % 128 == 0 else half
            if half <= 256:
                dst[sl] = (self.x[sl].astype(jnp.float32) + self.recv[pl.ds(roff, half)].astype(jnp.float32)).astype(jnp.bfloat16)
            else:
                def body(i, _):
                    o = i * step
                    a = pl.ds(pl.multiple_of(keep + o, 16), step); b = pl.ds(pl.multiple_of(roff + o, 16), step)
                    dst[a] = (self.x[a].astype(jnp.float32) + self.recv[b].astype(jnp.float32)).astype(jnp.bfloat16)
                    return 0
                lax.fori_loop(0, half // step, body, 0)
    def run(self):
        for k in range(2 * self.n):
            for c in range(len(self.chunks)):
                if k: self.finish(c, k - 1)
                self.start(c, k)
        for c in range(len(self.chunks)): self.finish(c, 2 * self.n - 1)

def orders(bits):
    seq = [b for b in bits if b[0] == "seq"]; grp = [b for b in bits if b[0] == "grp"]
    c, xs = seq[:1], seq[1:]
    y, zs = grp[:1], grp[1:]
    return [c + xs + y + zs, c + y + zs + xs, c + zs + xs + y, c + y + xs + zs]

def plan(bits, rows, nchunk, which):
    ods = orders(bits)
    unit = 16 << len(bits)
    assert rows % unit == 0
    units = rows // unit
    out = []; at = 0; ro = 0
    for i in range(nchunk):
        u = units // nchunk + (1 if i < units % nchunk else 0)
        if u == 0: continue
        out.append((at, u * unit, ods[which[i % len(which)]], ro, i * 2 * len(bits)))
        at += u * unit; ro += u * unit
    return out

def barrier(bits):
    bar = pltpu.get_barrier_semaphore()
    for b in bits:
        dev, _ = partner(b)
        pl.semaphore_signal(bar, inc=1, device_id=dev, device_id_type=MESH)
    pl.semaphore_wait(bar, len(bits))

def ar_kernel(bits, chunks, x_ref, o_ref, work, recv, ss, rs):
    barrier(bits)
    work[...] = x_ref[...]
    AR(work, o_ref, recv, ss, rs, chunks).run()

def allreduce(x, mesh, nchunk, which, cid, name):
    bits = bits_of(mesh.shape)
    rows, cols = x.shape
    chunks = plan(bits, rows, nchunk, which)
    ns = len(chunks) * 2 * len(bits)
    return pl.pallas_call(functools.partial(ar_kernel, bits, chunks),
        out_shape=jax.ShapeDtypeStruct(x.shape, x.dtype),
        in_specs=[pl.BlockSpec(memory_space=pltpu.VMEM)], out_specs=pl.BlockSpec(memory_space=pltpu.VMEM),
        scratch_shapes=[pltpu.VMEM((rows, cols), x.dtype), pltpu.VMEM((rows, cols), x.dtype), pltpu.SemaphoreType.DMA((ns,)), pltpu.SemaphoreType.DMA((ns,))],
        compiler_params=pltpu.CompilerParams(collective_id=cid, has_side_effects=True, vmem_limit_bytes=56 << 20),
        name=name)(x)
from jax.sharding import PartitionSpec as P

D_IN = 768
D = 512
HEADS = 8
DH = 64
FEATS = 256


def layer_norm(values, gain, shift):
    center = values - jnp.mean(values, axis=-1, keepdims=True)
    variance = jnp.mean(center * center, axis=-1, keepdims=True)
    return center * lax.rsqrt(variance + 1e-05) * gain + shift


def feature_map(projected, omega_b, key_keep):
    row_count = projected.shape[0]
    pieces = projected.reshape(row_count, HEADS, DH)
    factor = DH ** (-0.25)
    logits = jnp.einsum("nhd,dm->nhm", pieces, omega_b, preferred_element_type=jnp.float32) * factor
    squares = (
        0.5
        * factor
        * factor
        * jnp.sum(jnp.square(pieces.astype(jnp.float32)), axis=-1, keepdims=True)
    )
    return jnp.exp(logits - squares) * FEATS ** (-0.5) * key_keep[:, None, None]


def feature_grad(grad_feat, feat_full, projected, omega_b):
    row_count = projected.shape[0]
    factor = DH ** (-0.25)
    scaled = grad_feat.astype(jnp.float32) * feat_full
    logit_grad = scaled.astype(jnp.bfloat16)
    pieces = projected.reshape(row_count, HEADS, DH).astype(jnp.float32)
    through = (
        jnp.einsum("nhm,dm->nhd", logit_grad, omega_b, preferred_element_type=jnp.float32) * factor
    )
    direct = pieces * (factor * factor) * jnp.sum(scaled, axis=-1, keepdims=True)
    return (through - direct).reshape(row_count, HEADS * DH).astype(jnp.bfloat16)


def weight_term(left, right):
    return jnp.einsum("nk,nd->kd", left, right, preferred_element_type=jnp.float32)


def shards(
    mesh,
    encoded,
    destination,
    expressed,
    in_proj,
    gain_one,
    shift_one,
    query_w,
    key_w,
    value_w,
    out_w,
    gain_two,
    shift_two,
    up_w,
    down_w,
    random_features,
    out_cotangent,
):
    cell_count = destination.shape[0]
    split_count = destination.shape[1]
    blocks = destination.shape[2]
    tokens = encoded.shape[2]
    block_len = tokens // blocks
    row_total = out_cotangent.shape[2]
    slot_count = row_total // (cell_count * block_len)
    pair_rows = slot_count * block_len
    group_index = lax.axis_index("grp")
    split_index = lax.axis_index("seq")
    targets = jnp.arange(cell_count, dtype=jnp.int32)
    slot_ids = jnp.arange(slot_count, dtype=jnp.int32)
    within = jnp.arange(block_len, dtype=jnp.int32)
    block_ids = jnp.arange(blocks, dtype=jnp.int32)
    column = lax.dynamic_index_in_dim(destination, split_index, 1, keepdims=False)
    block_hits = (column[:, :, None] == targets).astype(jnp.int32)
    block_rank = jnp.sum(jnp.cumsum(block_hits, axis=1) * block_hits, axis=2) - 1
    own_dest = lax.dynamic_index_in_dim(column, group_index, 0, keepdims=False)
    own_rank = lax.dynamic_index_in_dim(block_rank, group_index, 0, keepdims=False)
    send_match = (
        (own_dest[:, None, None] == targets[:, None]) & (own_rank[:, None, None] == slot_ids)
    ).astype(jnp.int32)
    send_found = jnp.sum(send_match, axis=0)
    send_block = jnp.sum(send_match * block_ids[:, None, None], axis=0)
    send_index = (send_block[:, :, None] * block_len + within).reshape(-1)
    send_keep = jnp.repeat(send_found.reshape(-1), block_len).astype(jnp.bfloat16)
    back_index = ((own_dest * slot_count + own_rank)[:, None] * block_len + within).reshape(-1)
    recv_match = (
        (column[:, :, None] == group_index) & (block_rank[:, :, None] == slot_ids)
    ).astype(jnp.int32)
    recv_found = jnp.sum(recv_match, axis=1)
    recv_block = jnp.sum(recv_match * block_ids[:, None], axis=1)
    recv_token = (recv_block[:, :, None] * block_len + within).reshape(cell_count, pair_rows)
    expressed_col = lax.dynamic_index_in_dim(expressed, split_index, 1, keepdims=False)
    valid = jnp.repeat(recv_found.reshape(-1), block_len).astype(jnp.float32)
    key_keep = (
        jnp.take_along_axis(expressed_col, recv_token, axis=1).reshape(-1).astype(jnp.float32)
        * valid
    )
    block_sum = jnp.sum(expressed.reshape(cell_count, split_count, blocks, block_len), axis=3)
    dest_hits = destination[..., None] == targets
    counts = jnp.sum(jnp.where(dest_hits, block_sum[..., None], 0), axis=(0, 1, 2)).astype(
        jnp.float32
    )
    own_count = lax.dynamic_index_in_dim(counts, group_index, 0, keepdims=False)
    share = cell_count * own_count / jnp.sum(counts)
    token_rows = encoded.reshape(tokens, D_IN)
    token_hidden = jnp.dot(token_rows, in_proj, preferred_element_type=jnp.float32).astype(
        jnp.bfloat16
    )
    outgoing = jnp.take(token_hidden, send_index, axis=0) * send_keep[:, None]
    hidden_b = lax.all_to_all(
        outgoing.reshape(cell_count, pair_rows, D),
        "grp",
        split_axis=0,
        concat_axis=0,
        tiled=True,
    ).reshape(row_total, D)
    hidden_f = hidden_b.astype(jnp.float32)
    normed_f, norm_one_pull = jax.vjp(layer_norm, hidden_f, gain_one, shift_one)
    normed_b = normed_f.astype(jnp.bfloat16)
    queries_b = jnp.dot(normed_b, query_w, preferred_element_type=jnp.float32).astype(jnp.bfloat16)
    keys_b = jnp.dot(normed_b, key_w, preferred_element_type=jnp.float32).astype(jnp.bfloat16)
    values_b = jnp.dot(normed_b, value_w, preferred_element_type=jnp.float32).astype(jnp.bfloat16)
    query_full = feature_map(queries_b, random_features, jnp.ones((row_total,), jnp.float32))
    key_full = feature_map(keys_b, random_features, key_keep)
    query_feature_rows = query_full.astype(jnp.bfloat16)
    key_feature_rows = key_full.astype(jnp.bfloat16)
    value_per_head = values_b.reshape(row_total, HEADS, DH)
    value_part = jnp.einsum(
        "pgk,pgz->gkz", key_feature_rows, value_per_head, preferred_element_type=jnp.float32
    )
    total_part = jnp.sum(key_feature_rows, axis=0, dtype=jnp.float32)
    key_value_products, key_total = lax.psum((value_part, total_part), "seq")
    key_value_batched = key_value_products.astype(jnp.bfloat16)
    attention_numerator = jnp.einsum(
        "bli,lie->ble", query_feature_rows, key_value_batched, preferred_element_type=jnp.float32
    )
    denominator = jnp.sum(query_feature_rows.astype(jnp.float32) * key_total[None], axis=-1)
    attended_b = (
        (attention_numerator / denominator[:, :, None]).reshape(row_total, D).astype(jnp.bfloat16)
    )
    mixed = hidden_f + jnp.dot(attended_b, out_w, preferred_element_type=jnp.float32)
    normed_two_f, norm_two_pull = jax.vjp(layer_norm, mixed, gain_two, shift_two)
    normed_two_b = normed_two_f.astype(jnp.bfloat16)
    expanded = jnp.dot(normed_two_b, up_w, preferred_element_type=jnp.float32)
    activated_f, gelu_pull = jax.vjp(partial_gelu, expanded)
    activated_b = activated_f.astype(jnp.bfloat16)
    layer_out = (mixed + jnp.dot(activated_b, down_w, preferred_element_type=jnp.float32)) * valid[
        :, None
    ]
    grad_out = out_cotangent.reshape(row_total, D).astype(jnp.float32) * (valid * share)[:, None]
    grad_mlp = grad_out.astype(jnp.bfloat16)
    down_term = weight_term(activated_b, grad_mlp)
    grad_activated = jnp.dot(grad_mlp, down_w.T, preferred_element_type=jnp.float32)
    grad_up = gelu_pull(grad_activated)[0].astype(jnp.bfloat16)
    up_term = weight_term(normed_two_b, grad_up)
    grad_normed_two = jnp.dot(grad_up, up_w.T, preferred_element_type=jnp.float32)
    mixed_back, gain_two_term, shift_two_term = norm_two_pull(grad_normed_two)
    grad_mixed = grad_out + mixed_back
    grad_att = grad_mixed.astype(jnp.bfloat16)
    out_term = weight_term(attended_b, grad_att)
    grad_attended = jnp.dot(grad_att, out_w.T, preferred_element_type=jnp.float32).reshape(
        row_total, HEADS, DH
    )
    numerator_gradient = (grad_attended / denominator[:, :, None]).astype(jnp.bfloat16)
    grad_den = -jnp.sum(grad_attended * attention_numerator, axis=-1) / (denominator * denominator)
    value_grad_part = jnp.einsum(
        "pgk,pgz->gkz", query_feature_rows, numerator_gradient, preferred_element_type=jnp.float32
    )
    total_grad_part = jnp.sum(query_feature_rows.astype(jnp.float32) * grad_den[:, :, None], axis=0)
    grad_query_feat = (
        jnp.einsum(
            "pao,ajo->paj",
            numerator_gradient,
            key_value_batched,
            preferred_element_type=jnp.float32,
        )
        + grad_den[:, :, None] * key_total[None]
    ).astype(jnp.bfloat16)
    grad_kv, grad_total = lax.psum((value_grad_part, total_grad_part), "seq")
    key_value_gradient_batched = grad_kv.astype(jnp.bfloat16)
    grad_key_feat = (
        jnp.einsum(
            "pao,ajo->paj",
            value_per_head,
            key_value_gradient_batched,
            preferred_element_type=jnp.float32,
        )
        + grad_total[None]
    ).astype(jnp.bfloat16)
    grad_values = (
        jnp.einsum(
            "bli,lie->ble",
            key_feature_rows,
            key_value_gradient_batched,
            preferred_element_type=jnp.float32,
        )
        .reshape(row_total, D)
        .astype(jnp.bfloat16)
    )
    grad_queries = feature_grad(grad_query_feat, query_full, queries_b, random_features)
    grad_keys = feature_grad(grad_key_feat, key_full, keys_b, random_features)
    query_term = weight_term(normed_b, grad_queries)
    key_term = weight_term(normed_b, grad_keys)
    value_term = weight_term(normed_b, grad_values)
    grad_normed = jnp.dot(grad_queries, query_w.T, preferred_element_type=jnp.float32)
    grad_normed = grad_normed + jnp.dot(grad_keys, key_w.T, preferred_element_type=jnp.float32)
    grad_normed = grad_normed + jnp.dot(grad_values, value_w.T, preferred_element_type=jnp.float32)
    hidden_back, gain_one_term, shift_one_term = norm_one_pull(grad_normed)
    grad_hidden = (grad_mixed + hidden_back).astype(jnp.bfloat16)
    returned = lax.all_to_all(
        grad_hidden.reshape(cell_count, pair_rows, D),
        "grp",
        split_axis=0,
        concat_axis=0,
        tiled=True,
    )
    token_grad = jnp.take(returned.reshape(row_total, D), back_index, axis=0)
    encoded_grad = jnp.dot(token_grad, in_proj.T, preferred_element_type=jnp.float32).astype(
        jnp.bfloat16
    )
    in_term = weight_term(token_rows, token_grad)
    pieces = [in_term, query_term, key_term, value_term, out_term]
    pieces += [up_term[:, i : i + D] for i in range(0, up_term.shape[1], D)]
    pieces += [down_term]
    pieces += [gain_one_term[None], shift_one_term[None], gain_two_term[None], shift_two_term[None]]
    flat = jnp.concatenate([p.astype(jnp.bfloat16) for p in pieces])
    unit = 16 << len(bits_of(mesh.shape))
    rows = -(-flat.shape[0] // unit) * unit
    flat = jnp.pad(flat, ((0, rows - flat.shape[0]), (0, 0)))
    total = allreduce(flat, mesh, max(1, min(14, rows // unit)), [0, 1, 2], 0, "weights_sum").astype(jnp.float32)
    cut, at = [], 0
    for p in pieces:
        cut.append(total[at : at + p.shape[0]])
        at += p.shape[0]
    in_sum, query_sum, key_sum, value_sum, out_sum = cut[:5]
    up_sum = jnp.concatenate(cut[5:-5], axis=1)
    down_sum = cut[-5]
    gain_one_sum, shift_one_sum, gain_two_sum, shift_two_sum = [c[0] for c in cut[-4:]]
    return (
        layer_out.reshape(1, 1, row_total, D),
        encoded_grad.reshape(1, 1, tokens, D_IN),
        in_sum,
        gain_one_sum,
        shift_one_sum,
        query_sum,
        key_sum,
        value_sum,
        out_sum,
        gain_two_sum,
        shift_two_sum,
        up_sum,
        down_sum,
    )


def partial_gelu(values):
    return jax.nn.gelu(values, approximate=True)


def solution(mesh):
    in_specs = (
        P("grp", "seq", None, None),
        P(),
        P(),
        P(),
        P(),
        P(),
        P(),
        P(),
        P(),
        P(),
        P(),
        P(),
        P(),
        P(),
        P(),
        P("grp", "seq", None, None),
    )
    out_specs = (
        P("grp", "seq", None, None),
        P("grp", "seq", None, None),
        P(),
        P(),
        P(),
        P(),
        P(),
        P(),
        P(),
        P(),
        P(),
        P(),
        P(),
    )
    return jax.shard_map(functools.partial(shards, mesh), mesh=mesh, in_specs=in_specs, out_specs=out_specs, check_vma=False)
```

```python
import functools

import jax
import jax.numpy as jnp
from jax import lax
from jax.experimental import pallas as pl
from jax.experimental.pallas import tpu as pltpu
from jax.sharding import PartitionSpec as P

D_IN = 768
D = 512
HEADS = 8
DH = 64
FEATS = 256
FF = 2048
BLK = 8
LANES = 128
TILE = 128
FUSED_CELLS = 8
VMEM_LIMIT = 62 << 20
LOG2E = 1.4426950408889634
GELU_A = 0.7978845608028654
GELU_B = 0.044715
F32, BF16 = jnp.float32, jnp.bfloat16
MESH = pl.DeviceIdType.MESH


def dot(a, b):
    return jnp.dot(a, b, preferred_element_type=F32)


def dot_nt(a, b):
    return lax.dot_general(a, b, (((1,), (1,)), ((), ())), preferred_element_type=F32)


def dot_tn(a, b):
    return lax.dot_general(a, b, (((0,), (0,)), ((), ())), preferred_element_type=F32)


def iota(shape, axis):
    return lax.broadcasted_iota(jnp.int32, shape, axis)


def hot(condition):
    return jnp.where(condition, 1.0, 0.0)


def moments(x):
    center = x - jnp.mean(x, axis=-1, keepdims=True)
    scale = lax.rsqrt(jnp.mean(center * center, axis=-1, keepdims=True) + 1e-05)
    return center * scale, scale


def norm_back(grad, gain, unit, scale):
    inner = grad * gain
    return scale * (
        inner
        - jnp.mean(inner, axis=-1, keepdims=True)
        - unit * jnp.mean(inner * unit, axis=-1, keepdims=True)
    )


def axis_bits(sizes):
    return [
        (axis, i) for axis in ("seq", "grp") for i in range(sizes[axis].bit_length() - 1)
    ]


def partner(bit):
    grp, seq = lax.axis_index("grp"), lax.axis_index("seq")
    axis, i = bit
    step = 1 << i
    if axis == "seq":
        own = (seq // step) % 2
        return (grp, seq + step - 2 * step * own), own
    own = (grp // step) % 2
    return (grp + step - 2 * step * own, seq), own


def bit_orders(bits):
    seq = [b for b in bits if b[0] == "seq"]
    grp = [b for b in bits if b[0] == "grp"]
    core, xs, y, zs = seq[:1], seq[1:], grp[:1], grp[1:]
    return [core + xs + y + zs, core + y + zs + xs, core + zs + xs + y]


class Sum:
    def __init__(self, bits, pieces, send, recv, base):
        self.bits, self.pieces, self.send, self.recv, self.base = bits, pieces, send, recv, base
        orders = bit_orders(bits)
        self.orders = [orders[i % len(orders)] for i in range(len(pieces))]
        self.at = [p[3] for p in pieces]
        self.rows = [p[4] for p in pieces]
        self.inbox_at = [p[5] for p in pieces]
        self.kept = [[] for _ in pieces]
        self.flight = [None] * len(pieces)
        self.steps = 2 * len(bits)

    def start(self, c, k):
        part, total, inbox = self.pieces[c][:3]
        n = len(self.bits)
        sem = self.base + c * self.steps + k
        if k < n:
            device, own = partner(self.orders[c][k])
            half = self.rows[c] // 2
            keep = self.at[c] + own * half
            give = self.at[c] + (1 - own) * half
            source = part.at[pl.ds(pl.multiple_of(give, 16), half)]
            target = inbox.at[pl.ds(self.inbox_at[c], half)]
            self.kept[c].append((self.at[c], self.rows[c]))
            self.flight[c] = (None, keep, half, self.inbox_at[c])
            self.at[c], self.rows[c] = keep, half
            self.inbox_at[c] += half
        else:
            device, _ = partner(self.orders[c][2 * n - 1 - k])
            source = target = total.at[pl.ds(pl.multiple_of(self.at[c], 16), self.rows[c])]
            self.flight[c] = (None, None, None, None)
            self.at[c], self.rows[c] = self.kept[c].pop()
        copy = pltpu.make_async_remote_copy(
            src_ref=source,
            dst_ref=target,
            send_sem=self.send.at[sem],
            recv_sem=self.recv.at[sem],
            device_id=device,
            device_id_type=MESH,
        )
        self.flight[c] = (copy,) + self.flight[c][1:]
        copy.start()

    def finish(self, c, k):
        part, total, inbox = self.pieces[c][:3]
        copy, keep, half, inbox_at = self.flight[c]
        copy.wait()
        if k >= len(self.bits):
            return
        target = total if k == len(self.bits) - 1 else part
        step = min(half, 256)

        def add(i, carry):
            rows = pl.ds(pl.multiple_of(keep + i * step, 16), step)
            came = pl.ds(pl.multiple_of(inbox_at + i * step, 16), step)
            target[rows] = (part[rows].astype(F32) + inbox[came].astype(F32)).astype(BF16)
            return carry

        if half == step:
            add(0, 0)
        else:
            lax.fori_loop(0, half // step, add, 0)

    def advance(self, k):
        for c in range(len(self.pieces)):
            if k > 0:
                self.finish(c, k - 1)
            if k < self.steps:
                self.start(c, k)


def fused_kernel(
    sizes,
    cap,
    dest_ref,
    expr_ref,
    gain_one_ref,
    shift_one_ref,
    gain_two_ref,
    shift_two_ref,
    omega_ref,
    enc_hbm,
    in_hbm,
    query_hbm,
    key_hbm,
    value_hbm,
    out_hbm,
    up_hbm,
    down_hbm,
    cot_hbm,
    layer_hbm,
    enc_grad_hbm,
    early_hbm,
    late_hbm,
    enc,
    in_w,
    query_w,
    key_w,
    value_w,
    out_w,
    up_w,
    down_w,
    slots,
    cot,
    hidden,
    normed,
    queries,
    keys,
    values,
    query_feat,
    key_feat,
    kv_part,
    kv_inbox,
    kv,
    kv_grad,
    kt_part,
    kt_inbox,
    kt,
    kt_grad,
    attended,
    normed_two,
    big,
    grad_att,
    grad_num,
    layer,
    den_grad,
    early_part,
    early_inbox,
    feat_w,
    cell_x,
    cell_64,
    keep_col,
    share_col,
    slot_row,
    total_rows,
    spread,
    sums,
    load_sem,
    slot_send,
    slot_recv,
    layer_send,
    layer_recv,
    copy_sem,
    sum_send,
    sum_recv,
):
    grp, seq = lax.axis_index("grp"), lax.axis_index("seq")
    cells, splits = sizes["grp"], sizes["seq"]
    bits = axis_bits(sizes)
    tokens, tile = enc.shape[0], TILE
    tiles = tokens // tile
    blocks = dest_ref.shape[1]
    width = cells * DH
    pair_rows = slots.shape[0] // cells
    me = grp * splits + seq
    factor = DH ** (-0.25)

    loads = []
    for i, (a, b) in enumerate(
        (
            (enc_hbm, enc),
            (in_hbm, in_w),
            (key_hbm, key_w),
            (value_hbm, value_w),
            (query_hbm, query_w),
            (out_hbm, out_w),
            (up_hbm, up_w),
            (down_hbm, down_w),
            (cot_hbm.at[pl.ds(grp * pair_rows, pair_rows)], slots.at[pl.ds(grp * pair_rows, pair_rows)]),
        )
    ):
        load = pltpu.make_async_copy(a, b, load_sem.at[i])
        load.start()
        loads.append(load)

    barrier = pltpu.get_barrier_semaphore()
    others = [(lax.rem(grp + k, cells), seq) for k in range(1, cells)]
    mates = [partner(b)[0] for b in bits if b[0] == "seq"]
    for device in others + mates:
        pl.semaphore_signal(barrier, inc=1, device_id=device, device_id_type=MESH)
    pl.semaphore_wait(barrier, len(others) + len(mates))

    slot_copies = []
    for k, device in enumerate(others):
        copy = pltpu.make_async_remote_copy(
            src_ref=cot_hbm.at[pl.ds(device[0] * pair_rows, pair_rows)],
            dst_ref=slots.at[pl.ds(grp * pair_rows, pair_rows)],
            send_sem=slot_send.at[k],
            recv_sem=slot_recv.at[k],
            device_id=device,
            device_id_type=MESH,
        )
        copy.start()
        slot_copies.append(copy)

    own = dest_ref[pl.ds(me, 1), :]
    cell_x[...] = hot(iota((width, blocks), 0) >> 6 == own).astype(BF16)
    cell_64[...] = hot((iota((HEADS * cells, blocks), 0) & (cells - 1)) == own).astype(BF16)
    cell_hot = hot(iota((cells, blocks), 0) == own)
    earlier = hot(iota((blocks, blocks), 0) < iota((blocks, blocks), 1)).astype(BF16)
    rank = jnp.sum(dot(cell_hot.astype(BF16), earlier) * cell_hot, axis=0, keepdims=True)
    slot_block = own.astype(F32) * cap + rank
    block_of = hot(iota((blocks, tokens), 1) >> 3 == iota((blocks, tokens), 0)).astype(BF16)
    in_block = iota((8, tokens), 1) & (BLK - 1)
    slot_row[...] = (
        dot(jnp.broadcast_to(slot_block, (8, blocks)).astype(BF16), block_of) * BLK
        + in_block.astype(F32)
    )
    expressed = expr_ref[pl.ds(me, 1), :].astype(F32)
    keep_col[...] = jnp.broadcast_to(expressed, (LANES, tokens)).T
    cell_rows = dot(hot(iota((cells, blocks), 0) == own).astype(BF16), block_of)
    keep_rows = cell_rows * expressed
    block_sum = dot_nt(expr_ref[...].astype(F32).astype(BF16), block_of)
    share = jnp.zeros((1, blocks), F32)
    for c in range(cells):
        count = jnp.sum(jnp.where(dest_ref[...] == c, block_sum, 0.0), keepdims=True)
        share += jnp.where(own == c, count, 0.0)
    share = share * cells / jnp.sum(block_sum, keepdims=True)
    share_col[...] = lax.dot_general(
        hot(iota((tokens, blocks), 0) >> 3 == iota((tokens, blocks), 1)),
        jnp.broadcast_to(share, (LANES, blocks)),
        (((1,), (1,)), ((), ())),
        precision=lax.Precision.HIGHEST,
        preferred_element_type=F32,
    )
    head_lanes = iota((HEADS * cells * 2, D), 1) >> 6
    spread[...] = hot(
        (iota((HEADS * cells * 2, D), 0) & (HEADS * cells - 1)) >> cells.bit_length() - 1 == head_lanes
    ).astype(
        BF16
    )
    omega = omega_ref[...]
    zero = jnp.zeros_like(omega)
    one = jnp.ones_like(omega)
    feat_w[...] = jnp.concatenate(
        [
            jnp.concatenate([omega, zero], axis=1),
            jnp.concatenate([zero, omega], axis=1),
            jnp.concatenate([-one, zero], axis=1),
            jnp.concatenate([zero, -one], axis=1),
        ],
        axis=0,
    )
    sums[...] = jnp.zeros_like(sums)

    left = iota((tile, LANES), 1) < DH

    def rows_at(t):
        return pl.ds(pl.multiple_of(t * tile, tile), tile)

    def block_hot(t):
        return hot((iota((tile, blocks), 0) + t * tile) >> 3 == iota((tile, blocks), 1)).astype(BF16)

    def fold(a, b, mask):
        a, b = a * mask, b * mask
        sum_a = sum(a[:, i : i + LANES] for i in range(0, width, LANES))
        sum_b = sum(b[:, i : i + LANES] for i in range(0, width, LANES))
        return jnp.where(left, sum_a, sum_b) + pltpu.roll(jnp.where(left, sum_b, sum_a), DH, 1)

    def unfold(x, mask):
        turned = pltpu.roll(x, DH, 1)
        a, b = jnp.where(left, x, turned), jnp.where(left, turned, x)
        copies = width // LANES
        return (
            (jnp.concatenate([a] * copies, axis=1) * mask).astype(BF16),
            (jnp.concatenate([b] * copies, axis=1) * mask).astype(BF16),
        )

    def features(x):
        xf = x.astype(F32)
        squares = (xf * xf * (0.0625 / factor)).astype(BF16)
        inner = dot(jnp.concatenate([x, squares], axis=1), feat_w[...])
        return jnp.exp2(inner * (factor * LOG2E) - 4.0)

    def feature_back(grad, feat, x):
        scaled = (grad.astype(BF16).astype(F32) * feat.astype(F32)).astype(BF16)
        through = dot_nt(scaled, feat_w[...])
        return through[:, :LANES] * factor + through[:, LANES:] * x.astype(F32) * (factor * factor)

    def total_table(ref):
        flat = ref[: cells * HEADS * FEATS // LANES].astype(F32)
        row = jnp.concatenate(
            [flat[i * cells : (i + 1) * cells] for i in range(HEADS * FEATS // LANES)], axis=1
        )
        full = jnp.concatenate([row] * HEADS, axis=0)
        shape = (HEADS * cells, HEADS * FEATS)
        return (full * hot(iota(shape, 0) >> cells.bit_length() - 1 == iota(shape, 1) >> 8)).astype(BF16)

    def pair_sums(turned, mask_rows, extra, feat_ref, j):
        totals = []
        for i in range(2):
            head = 2 * j + i
            own_rows = turned[i * DH : (i + 1) * DH]
            tall = jnp.concatenate(
                [own_rows * mask_rows[c : c + 1] for c in range(cells)] + [extra(head)], axis=0
            ).astype(BF16)
            both = dot(tall, feat_ref[:, head * FEATS : (head + 1) * FEATS])
            kv_part[j * width : (j + 1) * width, i * FEATS : (i + 1) * FEATS] = both[:width].astype(BF16)
            totals.append(both[width : width + cells])
        return totals

    def store_totals(totals):
        for i in range(0, len(totals), 2):
            tall = jnp.concatenate(
                [x[:, at : at + LANES] for x in totals[i : i + 2] for at in range(0, FEATS, LANES)], axis=0
            )
            kt_part[i * 2 * cells : (i + 2) * 2 * cells] = tall.astype(BF16)

    loads[0].wait()
    loads[1].wait()
    loads[2].wait()
    loads[3].wait()

    def project(t, carry):
        rows = rows_at(t)
        hid = dot(enc[rows], in_w[...]).astype(BF16)
        hidden[rows] = hid
        unit, _ = moments(hid.astype(F32))
        nor = (unit * gain_one_ref[...] + shift_one_ref[...]).astype(BF16)
        normed[rows] = nor
        key = dot(nor, key_w[...]).astype(BF16)
        keys[rows] = key
        values[rows] = dot(nor, value_w[...]).astype(BF16)
        for j in range(HEADS // 2):
            pair = features(key[:, j * LANES : (j + 1) * LANES])
            key_feat[rows, j * 2 * FEATS : (j + 1) * 2 * FEATS] = pair.astype(BF16)
        return carry

    lax.fori_loop(0, tiles, project, 0)

    kt_part[...] = jnp.zeros_like(kt_part)

    def kv_pieces(total, small):
        unit = kv_part.shape[0] // (HEADS // 2)
        pieces = [(kv_part, total, kv_inbox, i * unit, unit, i * unit) for i in range(HEADS // 2)]
        return pieces + [(kt_part, small, kt_inbox, 0, kt_part.shape[0], 0)]

    forward_sum = Sum(bits, kv_pieces(kv, kt), sum_send, sum_recv, 0)
    totals = []
    for j in range(HEADS // 2):
        turned = lax.dot_general(
            value_w[:, j * LANES : (j + 1) * LANES],
            normed[...],
            (((0,), (1,)), ((), ())),
            preferred_element_type=F32,
        )
        totals += pair_sums(turned, keep_rows, lambda head: keep_rows, key_feat, j)
        forward_sum.start(j, 0)
    store_totals(totals)
    forward_sum.start(HEADS // 2, 0)

    def query_side(t, carry):
        rows = rows_at(t)
        query = dot(normed[rows], query_w[...]).astype(BF16)
        queries[rows] = query
        for j in range(HEADS // 2):
            pair = features(query[:, j * LANES : (j + 1) * LANES])
            query_feat[rows, j * 2 * FEATS : (j + 1) * 2 * FEATS] = pair.astype(BF16)
        return carry

    loads[4].wait()
    lax.fori_loop(0, tiles, query_side, 0)
    for k in range(1, forward_sum.steps + 1):
        forward_sum.advance(k)

    for i in range(5, 9):
        loads[i].wait()
    for copy in slot_copies:
        copy.wait()

    total_rows[...] = total_table(kt)

    def middle(t, carry):
        rows = rows_at(t)
        here = block_hot(t)
        mask = dot_nt(here, cell_x[...])
        mask_64 = dot_nt(here, cell_64[...])
        slot_col = dot_nt(here, jnp.broadcast_to(slot_block, (LANES, blocks)).astype(BF16)) * BLK + (
            iota((tile, LANES), 0) & (BLK - 1)
        ).astype(F32)
        pick = jnp.concatenate(
            [
                hot(slot_col == (iota((tile, LANES), 1) + i).astype(F32)).astype(BF16)
                for i in range(0, slots.shape[0], LANES)
            ],
            axis=1,
        )
        grad_out = dot(pick, slots[...]) * jnp.concatenate([share_col[rows]] * (D // LANES), axis=1)
        grad_mlp = grad_out.astype(BF16)
        cot[rows] = grad_mlp

        den = dot_nt(query_feat[rows], total_rows[...]) * mask_64
        den_high = den.astype(BF16)
        den_low = (den - den_high.astype(F32)).astype(BF16)
        over = 1.0 / dot(jnp.concatenate([den_high, den_low], axis=1), spread[...])
        for j in range(HEADS // 2):
            at = pl.ds(j * width, width)
            num = fold(
                dot_nt(query_feat[rows, j * 2 * FEATS : j * 2 * FEATS + FEATS], kv[at, :FEATS]),
                dot_nt(query_feat[rows, j * 2 * FEATS + FEATS : (j + 1) * 2 * FEATS], kv[at, FEATS:]),
                mask,
            )
            lanes = slice(j * LANES, (j + 1) * LANES)
            attended[rows, lanes] = (num * over[:, lanes]).astype(BF16)
        att = attended[rows]
        mixed = hidden[rows].astype(F32) + dot(att, out_w[...])
        unit, scale = moments(mixed)
        nor = (unit * gain_two_ref[...] + shift_two_ref[...]).astype(BF16)
        normed_two[rows] = nor
        out = mixed
        grad_nor = jnp.zeros((tile, D), F32)
        for j in range(FF // D):
            ff = slice(j * D, (j + 1) * D)
            x = dot(nor, up_w[:, ff])
            square = x * x
            bent = jnp.tanh(x * (GELU_A + (GELU_A * GELU_B) * square))
            ramp = 0.5 + 0.5 * bent
            act = (x * ramp).astype(BF16)
            slope = ramp + (0.5 * x) * (1.0 - bent * bent) * (GELU_A + (3.0 * GELU_A * GELU_B) * square)
            big[pl.ds(pl.multiple_of(j * tokens + t * tile, tile), tile)] = act
            out += dot(act, down_w[ff])
            gu = (slope * dot_nt(grad_mlp, down_w[ff])).astype(BF16)
            big[pl.ds(pl.multiple_of((FF // D + j) * tokens + t * tile, tile), tile)] = gu
            grad_nor += dot_nt(gu, up_w[:, ff])
        layer[rows] = out.astype(BF16)
        sums[0:8] += jnp.sum((grad_nor * unit).reshape(tile // 8, 8, D), axis=0)
        sums[8:16] += jnp.sum(grad_nor.reshape(tile // 8, 8, D), axis=0)
        grad_mix = (grad_out + norm_back(grad_nor, gain_two_ref[...], unit, scale)).astype(BF16)
        grad_att[rows] = grad_mix
        grad = dot_nt(grad_mix, out_w[...]) * over
        grad_num[rows] = grad.astype(BF16)
        den_grad[rows] = (
            dot_nt((grad * att.astype(F32)).astype(BF16), spread[: HEADS * cells]) * mask_64 * -1.0
        )
        return carry

    lax.fori_loop(0, tiles, middle, 0)

    den_rows = jnp.concatenate(
        [den_grad[...], jnp.zeros((tokens, LANES - HEADS * cells), F32)], axis=1
    ).T
    backward_sum = Sum(bits, kv_pieces(kv_grad, kt_grad), sum_send, sum_recv, 0)
    totals = []
    for j in range(HEADS // 2):
        turned = grad_num[:, j * LANES : (j + 1) * LANES].astype(F32).T
        totals += pair_sums(
            turned, cell_rows, lambda head: den_rows[head * cells : (head + 1) * cells], query_feat, j
        )
        backward_sum.start(j, 0)
    store_totals(totals)
    backward_sum.start(HEADS // 2, 0)

    layer_copies = []
    for k in range(cells):
        cell = lax.rem(grp + k, cells)
        pick = hot(
            slot_row[0:1] == (iota((pair_rows, tokens), 0) + cell * pair_rows).astype(F32)
        ).astype(BF16)
        here = pl.ds(pl.multiple_of(cell * pair_rows, pair_rows), pair_rows)
        there = pl.ds(pl.multiple_of(grp * pair_rows, pair_rows), pair_rows)
        slots[here] = dot(pick, layer[...]).astype(BF16)
        if k == 0:
            copy = pltpu.make_async_copy(slots.at[here], layer_hbm.at[there], copy_sem.at[0])
        else:
            copy = pltpu.make_async_remote_copy(
                src_ref=slots.at[here],
                dst_ref=layer_hbm.at[there],
                send_sem=layer_send.at[k - 1],
                recv_sem=layer_recv.at[k - 1],
                device_id=others[k - 1],
                device_id_type=MESH,
            )
        copy.start()
        layer_copies.append(copy)
    backward_sum.advance(1)

    for j in range(FF // D):
        early_part[j * D : (j + 1) * D] = dot_tn(big[j * tokens : (j + 1) * tokens], cot[...]).astype(BF16)
    backward_sum.advance(2)
    for j in range(FF // D):
        at = FF // D + j
        early_part[FF + j * D : FF + (j + 1) * D] = dot_tn(
            normed_two[...], big[at * tokens : (at + 1) * tokens]
        ).astype(BF16)
    backward_sum.advance(3)
    early_part[2 * FF : 2 * FF + D] = dot_tn(attended[...], grad_att[...]).astype(BF16)

    def query_back(t, carry):
        rows = rows_at(t)
        mask = dot_nt(block_hot(t), cell_x[...])
        den = den_grad[rows].astype(BF16)
        for j in range(HEADS // 2):
            lanes = slice(j * LANES, (j + 1) * LANES)
            feats = slice(j * 2 * FEATS, (j + 1) * 2 * FEATS)
            a, b = unfold(grad_num[rows, lanes].astype(F32), mask)
            at = pl.ds(j * width, width)
            grad = jnp.concatenate([dot(a, kv[at, :FEATS]), dot(b, kv[at, FEATS:])], axis=1)
            grad += dot(den, total_rows[:, feats])
            queries[rows, lanes] = feature_back(grad, query_feat[rows, feats], queries[rows, lanes]).astype(
                BF16
            )
        return carry

    lax.fori_loop(0, tiles, query_back, 0)
    early_part[2 * FF + D : 2 * FF + 2 * D] = dot_tn(normed[...], queries[...]).astype(BF16)
    for k in range(4, backward_sum.steps + 1):
        backward_sum.advance(k)

    unit_rows = 16 << len(bits)
    early_sum = Sum(
        bits,
        [
            (early_part, big, down_w, i, unit_rows, i)
            if i < FF
            else (early_part, big, early_inbox, i, unit_rows, i - FF)
            for i in range(0, early_part.shape[0], unit_rows)
        ],
        sum_send,
        sum_recv,
        5 * forward_sum.steps,
    )
    early_sum.advance(0)

    total_rows[...] = total_table(kt_grad)

    def last(t, carry):
        rows = rows_at(t)
        here = block_hot(t)
        keep = keep_col[rows]
        mask = dot_nt(here, cell_x[...]) * jnp.concatenate([keep] * (width // LANES), axis=1)
        mask_64 = (dot_nt(here, cell_64[...]) * keep[:, : HEADS * cells]).astype(BF16)
        for j in range(HEADS // 2):
            lanes = slice(j * LANES, (j + 1) * LANES)
            feats = slice(j * 2 * FEATS, (j + 1) * 2 * FEATS)
            a, b = unfold(values[rows, lanes].astype(F32), mask)
            at = pl.ds(j * width, width)
            feat = key_feat[rows, feats]
            grad = jnp.concatenate([dot(a, kv_grad[at, :FEATS]), dot(b, kv_grad[at, FEATS:])], axis=1)
            grad += dot(mask_64, total_rows[:, feats])
            keys[rows, lanes] = feature_back(grad, feat, keys[rows, lanes]).astype(BF16)
            values[rows, lanes] = fold(
                dot_nt(feat[:, :FEATS], kv_grad[at, :FEATS]),
                dot_nt(feat[:, FEATS:], kv_grad[at, FEATS:]),
                mask,
            ).astype(BF16)
        grad_nor = (
            dot_nt(queries[rows], query_w[...])
            + dot_nt(keys[rows], key_w[...])
            + dot_nt(values[rows], value_w[...])
        )
        unit, scale = moments(hidden[rows].astype(F32))
        sums[16:24] += jnp.sum((grad_nor * unit).reshape(tile // 8, 8, D), axis=0)
        sums[24:32] += jnp.sum(grad_nor.reshape(tile // 8, 8, D), axis=0)
        grad_hid = (
            grad_att[rows].astype(F32) + norm_back(grad_nor, gain_one_ref[...], unit, scale)
        ).astype(BF16)
        cot[rows] = grad_hid
        hidden[rows] = grad_hid
        return carry

    lax.fori_loop(0, tiles, last, 0)
    early_sum.advance(1)

    kv_part[0:D] = dot_tn(normed[...], keys[...]).astype(BF16)
    kv_part[D : 2 * D] = dot_tn(normed[...], values[...]).astype(BF16)
    kv_part[2 * D : 2 * D + D_IN] = dot_tn(enc[...], cot[...]).astype(BF16)
    small = jnp.concatenate(
        [jnp.sum(sums[8 * i : 8 * i + 8], axis=0, keepdims=True) for i in range(4)]
        + [jnp.zeros((12, D), F32)],
        axis=0,
    )
    at = 2 * D + D_IN
    kv_part[at : at + 16] = small.astype(BF16)
    kv_part[at + 16 :] = jnp.zeros((kv_part.shape[0] - at - 16, D), BF16)
    late_sum = Sum(
        bits,
        [
            (kv_part, big.at[pl.ds(early_part.shape[0], kv_part.shape[0])], kv_inbox, i, unit_rows, i)
            for i in range(0, kv_part.shape[0], unit_rows)
        ],
        sum_send,
        sum_recv,
        0,
    )
    late_sum.advance(0)

    def encoder_grad(t, carry):
        rows = rows_at(t)
        enc[rows] = dot_nt(hidden[rows], in_w[...]).astype(BF16)
        return carry

    lax.fori_loop(0, tiles, encoder_grad, 0)
    enc_copy = pltpu.make_async_copy(enc, enc_grad_hbm, copy_sem.at[1])
    enc_copy.start()
    for k in range(2, early_sum.steps + 1):
        early_sum.advance(k)
        late_sum.advance(k - 1)
    early_copy = pltpu.make_async_copy(big.at[pl.ds(0, early_part.shape[0])], early_hbm, copy_sem.at[2])
    early_copy.start()
    late_sum.advance(late_sum.steps)
    late_copy = pltpu.make_async_copy(
        big.at[pl.ds(early_part.shape[0], kv_part.shape[0])], late_hbm, copy_sem.at[3]
    )
    late_copy.start()
    for copy in layer_copies:
        copy.wait()
    enc_copy.wait()
    early_copy.wait()
    late_copy.wait()


def fused(
    mesh,
    encoded,
    destination,
    expressed,
    in_proj,
    gain_one,
    shift_one,
    query_w,
    key_w,
    value_w,
    out_w,
    gain_two,
    shift_two,
    up_w,
    down_w,
    random_features,
    out_cotangent,
):
    sizes = {"grp": mesh.shape["grp"], "seq": mesh.shape["seq"]}
    cells, splits, blocks = destination.shape
    tokens = encoded.shape[2]
    slot_total = out_cotangent.shape[2]
    cap = slot_total // (cells * BLK)
    width = cells * DH
    bits = axis_bits(sizes)
    unit = 16 << len(bits)
    steps = 2 * len(bits)
    early = 2 * FF + 2 * D
    late = -(-(2 * D + D_IN + 16) // unit) * unit
    count = 5 + early // unit

    def vmem(shape, kind=BF16):
        return pltpu.VMEM(shape, kind)

    spec, rest = pl.BlockSpec(memory_space=pltpu.VMEM), pl.BlockSpec(memory_space=pl.ANY)
    layer_b, enc_grad, early_b, late_b = pl.pallas_call(
        functools.partial(fused_kernel, sizes, cap),
        out_shape=(
            jax.ShapeDtypeStruct((slot_total, D), BF16),
            jax.ShapeDtypeStruct((tokens, D_IN), BF16),
            jax.ShapeDtypeStruct((early, D), BF16),
            jax.ShapeDtypeStruct((late, D), BF16),
        ),
        in_specs=[spec] * 7 + [rest] * 9,
        out_specs=(rest,) * 4,
        scratch_shapes=[
            vmem((tokens, D_IN)),
            vmem((D_IN, D)),
            vmem((D, D)),
            vmem((D, D)),
            vmem((D, D)),
            vmem((D, D)),
            vmem((D, FF)),
            vmem((FF, D)),
            vmem((slot_total, D)),
            vmem((tokens, D)),
            vmem((tokens, D)),
            vmem((tokens, D)),
            vmem((tokens, D)),
            vmem((tokens, D)),
            vmem((tokens, D)),
            vmem((tokens, HEADS * FEATS)),
            vmem((tokens, HEADS * FEATS)),
            vmem((HEADS // 2 * width, 2 * FEATS)),
            vmem((HEADS // 2 * width, 2 * FEATS)),
            vmem((HEADS // 2 * width, 2 * FEATS)),
            vmem((HEADS // 2 * width, 2 * FEATS)),
            vmem((unit, LANES)),
            vmem((unit, LANES)),
            vmem((unit, LANES)),
            vmem((unit, LANES)),
            vmem((tokens, D)),
            vmem((tokens, D)),
            vmem((2 * FF // D * tokens, D)),
            vmem((tokens, D)),
            vmem((tokens, D)),
            vmem((tokens, D)),
            vmem((tokens, HEADS * cells), F32),
            vmem((early, D)),
            vmem((early - FF, D)),
            vmem((4 * DH, 2 * FEATS)),
            vmem((width, blocks)),
            vmem((HEADS * cells, blocks)),
            vmem((tokens, LANES), F32),
            vmem((tokens, LANES), F32),
            vmem((8, tokens), F32),
            vmem((HEADS * cells, HEADS * FEATS)),
            vmem((2 * HEADS * cells, D)),
            vmem((32, D), F32),
            pltpu.SemaphoreType.DMA((9,)),
            pltpu.SemaphoreType.DMA((cells - 1,)),
            pltpu.SemaphoreType.DMA((cells - 1,)),
            pltpu.SemaphoreType.DMA((cells - 1,)),
            pltpu.SemaphoreType.DMA((cells - 1,)),
            pltpu.SemaphoreType.DMA((4,)),
            pltpu.SemaphoreType.DMA((count * steps,)),
            pltpu.SemaphoreType.DMA((count * steps,)),
        ],
        compiler_params=pltpu.CompilerParams(
            collective_id=1, has_side_effects=True, vmem_limit_bytes=VMEM_LIMIT
        ),
        name="layer_and_gradients",
    )(
        destination.reshape(cells * splits, blocks),
        expressed.reshape(cells * splits, tokens),
        gain_one.reshape(1, D),
        shift_one.reshape(1, D),
        gain_two.reshape(1, D),
        shift_two.reshape(1, D),
        random_features,
        encoded.reshape(tokens, D_IN),
        in_proj,
        query_w,
        key_w,
        value_w,
        out_w,
        up_w,
        down_w,
        out_cotangent.reshape(slot_total, D),
    )
    early_f, late_f = early_b.astype(F32), late_b.astype(F32)
    up_sum = jnp.concatenate([early_f[FF + i : FF + i + D] for i in range(0, FF, D)], axis=1)
    at = 2 * D + D_IN
    return (
        layer_b.astype(F32).reshape(1, 1, slot_total, D),
        enc_grad.reshape(1, 1, tokens, D_IN),
        late_f[2 * D : at],
        late_f[at + 2],
        late_f[at + 3],
        early_f[2 * FF + D :],
        late_f[:D],
        late_f[D : 2 * D],
        early_f[2 * FF : 2 * FF + D],
        late_f[at],
        late_f[at + 1],
        up_sum,
        early_f[:FF],
    )


def layer_norm(values, gain, shift):
    center = values - jnp.mean(values, axis=-1, keepdims=True)
    variance = jnp.mean(center * center, axis=-1, keepdims=True)
    return center * lax.rsqrt(variance + 1e-05) * gain + shift


def feature_map(projected, omega_b, key_keep):
    row_count = projected.shape[0]
    pieces = projected.reshape(row_count, HEADS, DH)
    factor = DH ** (-0.25)
    logits = jnp.einsum("nhd,dm->nhm", pieces, omega_b, preferred_element_type=jnp.float32) * factor
    squares = (
        0.5
        * factor
        * factor
        * jnp.sum(jnp.square(pieces.astype(jnp.float32)), axis=-1, keepdims=True)
    )
    return jnp.exp(logits - squares) * FEATS ** (-0.5) * key_keep[:, None, None]


def feature_grad(grad_feat, feat_full, projected, omega_b):
    row_count = projected.shape[0]
    factor = DH ** (-0.25)
    scaled = grad_feat.astype(jnp.float32) * feat_full
    logit_grad = scaled.astype(jnp.bfloat16)
    pieces = projected.reshape(row_count, HEADS, DH).astype(jnp.float32)
    through = (
        jnp.einsum("nhm,dm->nhd", logit_grad, omega_b, preferred_element_type=jnp.float32) * factor
    )
    direct = pieces * (factor * factor) * jnp.sum(scaled, axis=-1, keepdims=True)
    return (through - direct).reshape(row_count, HEADS * DH).astype(jnp.bfloat16)


def weight_term(left, right):
    return jnp.einsum("nk,nd->kd", left, right, preferred_element_type=jnp.float32)


def plain(
    encoded,
    destination,
    expressed,
    in_proj,
    gain_one,
    shift_one,
    query_w,
    key_w,
    value_w,
    out_w,
    gain_two,
    shift_two,
    up_w,
    down_w,
    random_features,
    out_cotangent,
):
    cell_count = destination.shape[0]
    split_count = destination.shape[1]
    blocks = destination.shape[2]
    tokens = encoded.shape[2]
    block_len = tokens // blocks
    row_total = out_cotangent.shape[2]
    slot_count = row_total // (cell_count * block_len)
    pair_rows = slot_count * block_len
    group_index = lax.axis_index("grp")
    split_index = lax.axis_index("seq")
    targets = jnp.arange(cell_count, dtype=jnp.int32)
    slot_ids = jnp.arange(slot_count, dtype=jnp.int32)
    within = jnp.arange(block_len, dtype=jnp.int32)
    block_ids = jnp.arange(blocks, dtype=jnp.int32)
    column = lax.dynamic_index_in_dim(destination, split_index, 1, keepdims=False)
    block_hits = (column[:, :, None] == targets).astype(jnp.int32)
    block_rank = jnp.sum(jnp.cumsum(block_hits, axis=1) * block_hits, axis=2) - 1
    own_dest = lax.dynamic_index_in_dim(column, group_index, 0, keepdims=False)
    own_rank = lax.dynamic_index_in_dim(block_rank, group_index, 0, keepdims=False)
    send_match = (
        (own_dest[:, None, None] == targets[:, None]) & (own_rank[:, None, None] == slot_ids)
    ).astype(jnp.int32)
    send_found = jnp.sum(send_match, axis=0)
    send_block = jnp.sum(send_match * block_ids[:, None, None], axis=0)
    send_index = (send_block[:, :, None] * block_len + within).reshape(-1)
    send_keep = jnp.repeat(send_found.reshape(-1), block_len).astype(jnp.bfloat16)
    back_index = ((own_dest * slot_count + own_rank)[:, None] * block_len + within).reshape(-1)
    recv_match = (
        (column[:, :, None] == group_index) & (block_rank[:, :, None] == slot_ids)
    ).astype(jnp.int32)
    recv_found = jnp.sum(recv_match, axis=1)
    recv_block = jnp.sum(recv_match * block_ids[:, None], axis=1)
    recv_token = (recv_block[:, :, None] * block_len + within).reshape(cell_count, pair_rows)
    expressed_col = lax.dynamic_index_in_dim(expressed, split_index, 1, keepdims=False)
    valid = jnp.repeat(recv_found.reshape(-1), block_len).astype(jnp.float32)
    key_keep = (
        jnp.take_along_axis(expressed_col, recv_token, axis=1).reshape(-1).astype(jnp.float32)
        * valid
    )
    block_sum = jnp.sum(expressed.reshape(cell_count, split_count, blocks, block_len), axis=3)
    dest_hits = destination[..., None] == targets
    counts = jnp.sum(jnp.where(dest_hits, block_sum[..., None], 0), axis=(0, 1, 2)).astype(
        jnp.float32
    )
    own_count = lax.dynamic_index_in_dim(counts, group_index, 0, keepdims=False)
    share = cell_count * own_count / jnp.sum(counts)
    token_rows = encoded.reshape(tokens, D_IN)
    token_hidden = jnp.dot(token_rows, in_proj, preferred_element_type=jnp.float32).astype(
        jnp.bfloat16
    )
    outgoing = jnp.take(token_hidden, send_index, axis=0) * send_keep[:, None]
    hidden_b = lax.all_to_all(
        outgoing.reshape(cell_count, pair_rows, D),
        "grp",
        split_axis=0,
        concat_axis=0,
        tiled=True,
    ).reshape(row_total, D)
    hidden_f = hidden_b.astype(jnp.float32)
    normed_f, norm_one_pull = jax.vjp(layer_norm, hidden_f, gain_one, shift_one)
    normed_b = normed_f.astype(jnp.bfloat16)
    queries_b = jnp.dot(normed_b, query_w, preferred_element_type=jnp.float32).astype(jnp.bfloat16)
    keys_b = jnp.dot(normed_b, key_w, preferred_element_type=jnp.float32).astype(jnp.bfloat16)
    values_b = jnp.dot(normed_b, value_w, preferred_element_type=jnp.float32).astype(jnp.bfloat16)
    query_full = feature_map(queries_b, random_features, jnp.ones((row_total,), jnp.float32))
    key_full = feature_map(keys_b, random_features, key_keep)
    query_feature_rows = query_full.astype(jnp.bfloat16)
    key_feature_rows = key_full.astype(jnp.bfloat16)
    value_per_head = values_b.reshape(row_total, HEADS, DH)
    value_part = jnp.einsum(
        "pgk,pgz->gkz", key_feature_rows, value_per_head, preferred_element_type=jnp.float32
    )
    total_part = jnp.sum(key_feature_rows, axis=0, dtype=jnp.float32)
    key_value_products, key_total = lax.psum((value_part, total_part), "seq")
    key_value_batched = key_value_products.astype(jnp.bfloat16)
    attention_numerator = jnp.einsum(
        "bli,lie->ble", query_feature_rows, key_value_batched, preferred_element_type=jnp.float32
    )
    denominator = jnp.sum(query_feature_rows.astype(jnp.float32) * key_total[None], axis=-1)
    attended_b = (
        (attention_numerator / denominator[:, :, None]).reshape(row_total, D).astype(jnp.bfloat16)
    )
    mixed = hidden_f + jnp.dot(attended_b, out_w, preferred_element_type=jnp.float32)
    normed_two_f, norm_two_pull = jax.vjp(layer_norm, mixed, gain_two, shift_two)
    normed_two_b = normed_two_f.astype(jnp.bfloat16)
    expanded = jnp.dot(normed_two_b, up_w, preferred_element_type=jnp.float32)
    activated_f, gelu_pull = jax.vjp(partial_gelu, expanded)
    activated_b = activated_f.astype(jnp.bfloat16)
    layer_out = (mixed + jnp.dot(activated_b, down_w, preferred_element_type=jnp.float32)) * valid[
        :, None
    ]
    grad_out = out_cotangent.reshape(row_total, D).astype(jnp.float32) * (valid * share)[:, None]
    grad_mlp = grad_out.astype(jnp.bfloat16)
    down_term = weight_term(activated_b, grad_mlp)
    grad_activated = jnp.dot(grad_mlp, down_w.T, preferred_element_type=jnp.float32)
    grad_up = gelu_pull(grad_activated)[0].astype(jnp.bfloat16)
    up_term = weight_term(normed_two_b, grad_up)
    grad_normed_two = jnp.dot(grad_up, up_w.T, preferred_element_type=jnp.float32)
    mixed_back, gain_two_term, shift_two_term = norm_two_pull(grad_normed_two)
    grad_mixed = grad_out + mixed_back
    grad_att = grad_mixed.astype(jnp.bfloat16)
    out_term = weight_term(attended_b, grad_att)
    grad_attended = jnp.dot(grad_att, out_w.T, preferred_element_type=jnp.float32).reshape(
        row_total, HEADS, DH
    )
    numerator_gradient = (grad_attended / denominator[:, :, None]).astype(jnp.bfloat16)
    grad_den = -jnp.sum(grad_attended * attention_numerator, axis=-1) / (denominator * denominator)
    value_grad_part = jnp.einsum(
        "pgk,pgz->gkz", query_feature_rows, numerator_gradient, preferred_element_type=jnp.float32
    )
    total_grad_part = jnp.sum(query_feature_rows.astype(jnp.float32) * grad_den[:, :, None], axis=0)
    grad_query_feat = (
        jnp.einsum(
            "pao,ajo->paj",
            numerator_gradient,
            key_value_batched,
            preferred_element_type=jnp.float32,
        )
        + grad_den[:, :, None] * key_total[None]
    ).astype(jnp.bfloat16)
    grad_kv, grad_total = lax.psum((value_grad_part, total_grad_part), "seq")
    key_value_gradient_batched = grad_kv.astype(jnp.bfloat16)
    grad_key_feat = (
        jnp.einsum(
            "pao,ajo->paj",
            value_per_head,
            key_value_gradient_batched,
            preferred_element_type=jnp.float32,
        )
        + grad_total[None]
    ).astype(jnp.bfloat16)
    grad_values = (
        jnp.einsum(
            "bli,lie->ble",
            key_feature_rows,
            key_value_gradient_batched,
            preferred_element_type=jnp.float32,
        )
        .reshape(row_total, D)
        .astype(jnp.bfloat16)
    )
    grad_queries = feature_grad(grad_query_feat, query_full, queries_b, random_features)
    grad_keys = feature_grad(grad_key_feat, key_full, keys_b, random_features)
    query_term = weight_term(normed_b, grad_queries)
    key_term = weight_term(normed_b, grad_keys)
    value_term = weight_term(normed_b, grad_values)
    grad_normed = jnp.dot(grad_queries, query_w.T, preferred_element_type=jnp.float32)
    grad_normed = grad_normed + jnp.dot(grad_keys, key_w.T, preferred_element_type=jnp.float32)
    grad_normed = grad_normed + jnp.dot(grad_values, value_w.T, preferred_element_type=jnp.float32)
    hidden_back, gain_one_term, shift_one_term = norm_one_pull(grad_normed)
    grad_hidden = (grad_mixed + hidden_back).astype(jnp.bfloat16)
    returned = lax.all_to_all(
        grad_hidden.reshape(cell_count, pair_rows, D),
        "grp",
        split_axis=0,
        concat_axis=0,
        tiled=True,
    )
    token_grad = jnp.take(returned.reshape(row_total, D), back_index, axis=0)
    encoded_grad = jnp.dot(token_grad, in_proj.T, preferred_element_type=jnp.float32).astype(
        jnp.bfloat16
    )
    in_term = weight_term(token_rows, token_grad)
    (
        in_sum,
        query_sum,
        key_sum,
        value_sum,
        out_sum,
        up_sum,
        down_sum,
        gain_one_sum,
        shift_one_sum,
        gain_two_sum,
        shift_two_sum,
    ) = lax.psum(
        (
            in_term,
            query_term,
            key_term,
            value_term,
            out_term,
            up_term,
            down_term,
            gain_one_term,
            shift_one_term,
            gain_two_term,
            shift_two_term,
        ),
        ("grp", "seq"),
    )
    return (
        layer_out.reshape(1, 1, row_total, D),
        encoded_grad.reshape(1, 1, tokens, D_IN),
        in_sum,
        gain_one_sum,
        shift_one_sum,
        query_sum,
        key_sum,
        value_sum,
        out_sum,
        gain_two_sum,
        shift_two_sum,
        up_sum,
        down_sum,
    )


def partial_gelu(values):
    return jax.nn.gelu(values, approximate=True)


def solution(mesh):
    in_specs = (
        P("grp", "seq", None, None),
        P(),
        P(),
        P(),
        P(),
        P(),
        P(),
        P(),
        P(),
        P(),
        P(),
        P(),
        P(),
        P(),
        P(),
        P("grp", "seq", None, None),
    )
    out_specs = (
        P("grp", "seq", None, None),
        P("grp", "seq", None, None),
        P(),
        P(),
        P(),
        P(),
        P(),
        P(),
        P(),
        P(),
        P(),
        P(),
        P(),
    )
    body = functools.partial(fused, mesh) if mesh.shape["grp"] <= FUSED_CELLS else plain
    return jax.shard_map(body, mesh=mesh, in_specs=in_specs, out_specs=out_specs, check_vma=False)
```

```python
import functools

import jax
import jax.numpy as jnp
from jax import lax
from jax.experimental import pallas as pl
from jax.experimental.pallas import tpu as pltpu
from jax.sharding import PartitionSpec as P

D_IN = 768
D = 512
HEADS = 8
DH = 64
FEATS = 256
FF = 2048
BLK = 8
LANES = 128
TILE = 256
WIDE = 512
PARTS = 4
SLOTS_FIRST = 9
SLOTS_STEP = 2
LAYER_STEP = 1
LAYER_LATE = 2
FUSED_CELLS = 8
VMEM_LIMIT = 62 << 20
LOG2E = 1.4426950408889634
GELU_A = 0.7978845608028654
GELU_B = 0.044715
F32, BF16 = jnp.float32, jnp.bfloat16
MESH = pl.DeviceIdType.MESH


def dot(a, b):
    return jnp.dot(a, b, preferred_element_type=F32)


def dot_nt(a, b):
    return lax.dot_general(a, b, (((1,), (1,)), ((), ())), preferred_element_type=F32)


def dot_tn(a, b):
    return lax.dot_general(a, b, (((0,), (0,)), ((), ())), preferred_element_type=F32)


def iota(shape, axis):
    return lax.broadcasted_iota(jnp.int32, shape, axis)


def hot(condition):
    return jnp.where(condition, 1.0, 0.0)


def moments(x):
    center = x - jnp.mean(x, axis=-1, keepdims=True)
    scale = lax.rsqrt(jnp.mean(center * center, axis=-1, keepdims=True) + 1e-05)
    return center * scale, scale


def norm_back(grad, gain, unit, scale):
    inner = grad * gain
    return scale * (
        inner
        - jnp.mean(inner, axis=-1, keepdims=True)
        - unit * jnp.mean(inner * unit, axis=-1, keepdims=True)
    )


def digits_of(sizes):
    digits = []
    for axis in ("seq", "grp"):
        if sizes[axis] > 1:
            digits.append((axis, 1, 2))
        if sizes[axis] > 2:
            digits.append((axis, 2, sizes[axis] // 2))
    return digits


def peers(digit):
    grp, seq = lax.axis_index("grp"), lax.axis_index("seq")
    axis, step, radix = digit
    index = seq if axis == "seq" else grp
    value = (index // step) % radix
    found = []
    for m in range(1, radix):
        other = index + ((value + m) % radix - value) * step
        found.append((grp, other) if axis == "seq" else (other, seq))
    return value, found


def digit_orders(digits):
    first, second = list(digits), list(digits)
    if len(digits) > 2:
        second[1], second[2] = second[2], second[1]
    return first, second


class Sum:
    def __init__(self, digits, pieces, send, recv, base, settle=None):
        self.pieces, self.send, self.recv, self.base, self.settle = pieces, send, recv, base, settle
        self.half_steps, self.steps = len(digits), 2 * len(digits)
        self.copies = 2 * sum(radix - 1 for _, _, radix in digits)
        self.step = [-1] * len(pieces)
        self.turn = 0
        self.plans = []
        orders = digit_orders(digits)
        for c, piece in enumerate(pieces):
            at, rows, inbox_at, sem = 0, piece[6], piece[3], base + c * self.copies
            plan, kept = [], []
            for digit in orders[c % len(orders)]:
                value, found = peers(digit)
                radix = digit[2]
                rows //= radix
                keep = at + value * rows
                moves = []
                for m, device in enumerate(found, 1):
                    moves.append((device, at + (value + m) % radix * rows, inbox_at, sem))
                    inbox_at += rows
                    sem += 1
                kept.append((found, keep, rows))
                plan.append((moves, keep, rows))
                at = keep
            for found, keep, rows in reversed(kept):
                moves = [(device, keep, None, sem + m) for m, device in enumerate(found)]
                sem += len(found)
                plan.append((moves, keep, rows))
            self.plans.append(plan)

    def transfers(self, c, k):
        part, start, inbox, _, total, total_at, _, own = self.pieces[c]
        moves, _, rows = self.plans[c][k]
        found = []
        for device, at, inbox_at, sem in moves:
            if k < self.half_steps:
                source = part.at[pl.ds(pl.multiple_of(start + at, 16), rows)]
                target = inbox.at[pl.ds(inbox_at, rows)]
            else:
                target = total.at[pl.ds(pl.multiple_of(total_at + at, 16), rows)]
                source = target if own is None or k > self.half_steps else own
            found.append(
                pltpu.make_async_remote_copy(
                    src_ref=source,
                    dst_ref=target,
                    send_sem=self.send.at[sem],
                    recv_sem=self.recv.at[sem],
                    device_id=device,
                    device_id_type=MESH,
                )
            )
        return found

    def settled(self, c):
        _, _, _, _, total, total_at, _, own = self.pieces[c]
        _, at, rows = self.plans[c][self.half_steps]
        target = total.at[pl.ds(pl.multiple_of(total_at + at, 16), rows)]
        return pltpu.make_async_copy(own, target, self.settle.at[c])

    def finish(self, c):
        k = self.step[c]
        part, start, inbox, _, total, total_at, _, own = self.pieces[c]
        for transfer in self.transfers(c, k):
            transfer.wait()
        if k == self.half_steps and own is not None:
            self.settled(c).wait()
        if k >= self.half_steps:
            return
        moves, keep, rows = self.plans[c][k]
        step = min(rows, 256)
        last = k == self.half_steps - 1

        def add(i, carry):
            here = pl.ds(pl.multiple_of(start + keep + i * step, 16), step)
            value = part[here].astype(F32)
            for _, _, inbox_at, _ in moves:
                value += inbox[pl.ds(pl.multiple_of(inbox_at + i * step, 16), step)].astype(F32)
            value = value.astype(BF16)
            if not last:
                part[here] = value
            elif own is None:
                total[pl.ds(pl.multiple_of(total_at + keep + i * step, 16), step)] = value
            else:
                own[...] = value
            return carry

        if rows == step:
            add(0, 0)
        else:
            lax.fori_loop(0, rows // step, add, 0)
        if last and own is not None:
            self.settled(c).start()

    def tick(self, *which):
        for c in which:
            if self.step[c] >= 0:
                self.finish(c)
            self.step[c] += 1
            if self.step[c] < self.steps:
                for transfer in self.transfers(c, self.step[c]):
                    transfer.start()

    def begun(self):
        return [c for c in range(len(self.pieces)) if 0 <= self.step[c] < self.steps]

    def go_on(self):
        self.tick(*self.begun())

    def go_on_half(self):
        self.turn += 1
        self.tick(*[c for c in self.begun() if (c // 2 + self.turn) % 2])

    def run(self):
        while self.begun():
            self.go_on()


class Exchange:
    def __init__(self, makers):
        self.makers, self.started = makers, 0

    def start(self, count):
        for make in self.makers[self.started : self.started + count]:
            make().start()
        self.started = min(self.started + count, len(self.makers))

    def wait(self):
        self.start(len(self.makers))
        for make in self.makers:
            make().wait()


def fused_kernel(
    sizes,
    cap,
    dest_ref,
    expr_ref,
    gain_one_ref,
    shift_one_ref,
    gain_two_ref,
    shift_two_ref,
    omega_ref,
    enc_hbm,
    in_hbm,
    query_hbm,
    key_hbm,
    value_hbm,
    out_hbm,
    up_hbm,
    down_hbm,
    cot_hbm,
    layer_hbm,
    enc_grad_hbm,
    in_sum_hbm,
    query_sum_hbm,
    key_sum_hbm,
    value_sum_hbm,
    out_sum_hbm,
    up_sum_hbm,
    down_sum_hbm,
    small_sum_hbm,
    feat_hbm,
    enc,
    in_w,
    query_w,
    key_w,
    value_w,
    out_w,
    up_w,
    down_w,
    slots,
    cot,
    hidden,
    normed,
    queries,
    keys,
    values,
    query_feat,
    kv_part,
    kv_inbox,
    kv,
    kv_grad,
    kt_part,
    kt_inbox,
    kt,
    kt_grad,
    attended,
    normed_two,
    grad_att,
    grad_num,
    den_pair,
    den_grad,
    early_part,
    early_inbox,
    early_own,
    feat_w,
    cell_x,
    cell_64,
    keep_col,
    share_col,
    slot_row,
    total_rows,
    spread,
    sums,
    load_sem,
    slot_send,
    slot_recv,
    layer_send,
    layer_recv,
    copy_sem,
    settle_sem,
    sum_send,
    sum_recv,
):
    grp, seq = lax.axis_index("grp"), lax.axis_index("seq")
    cells = sizes["grp"]
    digits = digits_of(sizes)
    tokens = enc.shape[0]
    blocks = dest_ref.shape[2]
    width = cells * DH
    pair_rows = slots.shape[0] // cells
    unit_rows = 16 * sizes["grp"] * sizes["seq"]
    factor = DH ** (-0.25)
    hidden_tiles = FF // D

    own_slots = pl.ds(pl.multiple_of(grp * pair_rows, pair_rows), pair_rows)
    sources = [
        (enc_hbm, enc),
        (in_hbm, in_w),
        (key_hbm, key_w),
        (value_hbm, value_w),
        (query_hbm, query_w),
        (out_hbm, out_w),
        (down_hbm, down_w),
        (cot_hbm.at[own_slots], slots.at[own_slots]),
    ]
    sources += [(up_hbm.at[:, pl.ds(j * D, D)], up_w.at[pl.ds(j * D, D)]) for j in range(hidden_tiles)]

    def load(i):
        return pltpu.make_async_copy(*sources[i], load_sem.at[i])

    for i in range(len(sources)):
        load(i).start()

    barrier = pltpu.get_barrier_semaphore()
    others = [(lax.rem(grp + k, cells), seq) for k in range(1, cells)]
    mates = [device for digit in digits if digit[0] == "seq" for device in peers(digit)[1]]
    for device in others + mates:
        pl.semaphore_signal(barrier, inc=1, device_id=device, device_id_type=MESH)
    pl.semaphore_wait(barrier, len(others) + len(mates))

    part_rows = pair_rows // PARTS

    def slot_copy(k, i):
        theirs = pl.multiple_of(others[k][0] * pair_rows + i * part_rows, part_rows)
        ours = pl.multiple_of(grp * pair_rows + i * part_rows, part_rows)
        return pltpu.make_async_remote_copy(
            src_ref=cot_hbm.at[pl.ds(theirs, part_rows)],
            dst_ref=slots.at[pl.ds(ours, part_rows)],
            send_sem=slot_send.at[k * PARTS + i],
            recv_sem=slot_recv.at[k * PARTS + i],
            device_id=others[k],
            device_id_type=MESH,
        )

    def layer_copy(k, i):
        theirs = pl.multiple_of(others[k][0] * pair_rows + i * part_rows, part_rows)
        ours = pl.multiple_of(grp * pair_rows + i * part_rows, part_rows)
        return pltpu.make_async_remote_copy(
            src_ref=slots.at[pl.ds(theirs, part_rows)],
            dst_ref=layer_hbm.at[pl.ds(ours, part_rows)],
            send_sem=layer_send.at[k * PARTS + i],
            recv_sem=layer_recv.at[k * PARTS + i],
            device_id=others[k],
            device_id_type=MESH,
        )

    order = [(k, i) for i in range(PARTS) for k in range(cells - 1)]
    slot_exchange = Exchange([functools.partial(slot_copy, k, i) for k, i in order])
    layer_exchange = Exchange([functools.partial(layer_copy, k, i) for k, i in order])
    slot_exchange.start(SLOTS_FIRST)

    def kv_pieces(total, small):
        rows = 2 * width
        pieces = [(kv_part, at, kv_inbox, at, total, at, rows, None) for at in range(0, kv.shape[0], rows)]
        return pieces + [(kt_part, 0, kt_inbox, 0, small, 0, kt_part.shape[0], None)]

    forward_sum = Sum(digits, kv_pieces(kv, kt), sum_send, sum_recv, 0)
    backward_sum = Sum(digits, kv_pieces(kv_grad, kt_grad), sum_send, sum_recv, 0)
    late_sum = Sum(
        digits,
        [(kv_part, at, kv_inbox, at, kv, at, unit_rows, None) for at in range(0, kv.shape[0], unit_rows)],
        sum_send,
        sum_recv,
        0,
    )
    early_totals = []
    for j in range(hidden_tiles):
        early_totals.append((down_sum_hbm, j * D))
        early_totals.append((up_sum_hbm.at[:, pl.ds(j * D, D)], 0))
    early_totals += [(out_sum_hbm, 0), (query_sum_hbm, 0)]
    early_sum = Sum(
        digits,
        [
            (early_part, c * D, early_inbox, c * D, total, at, D, early_own.at[pl.ds(c * 16, 16)])
            for c, (total, at) in enumerate(early_totals)
        ],
        sum_send,
        sum_recv,
        late_sum.copies * len(late_sum.pieces),
        settle_sem,
    )
    own = dest_ref[grp, pl.ds(seq, 1), :]
    cell_x[...] = hot(iota((width, blocks), 0) >> 6 == own).astype(BF16)
    cell_64[...] = hot((iota((HEADS * cells, blocks), 0) & (cells - 1)) == own).astype(BF16)
    cell_hot = hot(iota((cells, blocks), 0) == own)
    earlier = hot(iota((blocks, blocks), 0) < iota((blocks, blocks), 1)).astype(BF16)
    rank = jnp.sum(dot(cell_hot.astype(BF16), earlier) * cell_hot, axis=0, keepdims=True)
    slot_block = own.astype(F32) * cap + rank
    block_of = hot(iota((blocks, tokens), 1) >> 3 == iota((blocks, tokens), 0)).astype(BF16)
    slot_row[...] = dot(jnp.broadcast_to(slot_block, (8, blocks)).astype(BF16), block_of) * BLK + (
        iota((8, tokens), 1) & (BLK - 1)
    ).astype(F32)
    expressed = expr_ref[grp, pl.ds(seq, 1), :].astype(F32)
    keep_col[...] = jnp.broadcast_to(expressed, (LANES, tokens)).T
    cell_rows = dot(cell_hot.astype(BF16), block_of)
    keep_rows = cell_rows * expressed
    sums[...] = jnp.zeros_like(sums)
    kt_part[...] = jnp.zeros_like(kt_part)
    omega = omega_ref[...]
    zero = jnp.zeros_like(omega)
    one = jnp.ones_like(omega)
    feat_w[...] = jnp.concatenate(
        [
            jnp.concatenate([omega, zero], axis=1),
            jnp.concatenate([zero, omega], axis=1),
            jnp.concatenate([-one, zero], axis=1),
            jnp.concatenate([zero, -one], axis=1),
        ],
        axis=0,
    )

    def tables():
        counted = [jnp.zeros(dest_ref.shape[1:], F32) for _ in range(cells)]
        whole = jnp.zeros(dest_ref.shape[1:], F32)
        for g in range(dest_ref.shape[0]):
            block_sum = dot_nt(expr_ref[g].astype(F32).astype(BF16), block_of)
            whole += block_sum
            for c in range(cells):
                counted[c] += jnp.where(dest_ref[g] == c, block_sum, 0.0)
        share = jnp.zeros((1, blocks), F32)
        for c in range(cells):
            share += jnp.where(own == c, jnp.sum(counted[c], keepdims=True), 0.0)
        share = share * cells / jnp.sum(whole, keepdims=True)
        share_col[...] = lax.dot_general(
            hot(iota((tokens, blocks), 0) >> 3 == iota((tokens, blocks), 1)),
            jnp.broadcast_to(share, (LANES, blocks)),
            (((1,), (1,)), ((), ())),
            precision=lax.Precision.HIGHEST,
            preferred_element_type=F32,
        )
        head_lanes = iota((HEADS * cells * 2, D), 1) >> 6
        spread[...] = hot(
            (iota((HEADS * cells * 2, D), 0) & (HEADS * cells - 1)) >> cells.bit_length() - 1 == head_lanes
        ).astype(BF16)

    def rows_at(t, tile):
        return pl.ds(pl.multiple_of(t * tile, tile), tile)

    def block_hot(t, tile):
        return hot((iota((tile, blocks), 0) + t * tile) >> 3 == iota((tile, blocks), 1)).astype(BF16)

    def fold(a, b, mask):
        left = iota((a.shape[0], LANES), 1) < DH
        a, b = a * mask, b * mask
        sum_a = sum(a[:, i : i + LANES] for i in range(0, width, LANES))
        sum_b = sum(b[:, i : i + LANES] for i in range(0, width, LANES))
        return jnp.where(left, sum_a, sum_b) + pltpu.roll(jnp.where(left, sum_b, sum_a), DH, 1)

    def unfold(x, mask):
        left = iota((x.shape[0], LANES), 1) < DH
        turned = pltpu.roll(x, DH, 1)
        a, b = jnp.where(left, x, turned), jnp.where(left, turned, x)
        copies = width // LANES
        return (
            (jnp.concatenate([a] * copies, axis=1) * mask).astype(BF16),
            (jnp.concatenate([b] * copies, axis=1) * mask).astype(BF16),
        )

    def features(x):
        xf = x.astype(F32)
        squares = (xf * xf * (0.0625 / factor)).astype(BF16)
        inner = dot(jnp.concatenate([x, squares], axis=1), feat_w[...])
        return jnp.exp2(inner * (factor * LOG2E) - 4.0)

    def feature_back(grad, feat, x):
        scaled = (grad.astype(BF16).astype(F32) * feat.astype(F32)).astype(BF16)
        through = dot_nt(scaled, feat_w[...])
        return through[:, :LANES] * factor + through[:, LANES:] * x.astype(F32) * (factor * factor)

    def total_table(ref):
        flat = ref[: cells * HEADS * FEATS // LANES].astype(F32)
        row = jnp.concatenate(
            [flat[i * cells : (i + 1) * cells] for i in range(HEADS * FEATS // LANES)], axis=1
        )
        full = jnp.concatenate([row] * HEADS, axis=0)
        shape = (HEADS * cells, HEADS * FEATS)
        return (full * hot(iota(shape, 0) >> cells.bit_length() - 1 == iota(shape, 1) >> 8)).astype(BF16)

    def pair_sums(turned, mask_rows, extra, feat_ref, j):
        totals = []
        for i in range(2):
            head = 2 * j + i
            own_rows = turned[i * DH : (i + 1) * DH]
            tall = jnp.concatenate(
                [own_rows * mask_rows[c : c + 1] for c in range(cells)] + [extra(head)], axis=0
            ).astype(BF16)
            both = dot(tall, feat_ref[:, head * FEATS : (head + 1) * FEATS])
            kv_part[j * width : (j + 1) * width, i * FEATS : (i + 1) * FEATS] = both[:width].astype(BF16)
            totals.append(both[width : width + cells])
        return totals

    def store_totals(totals):
        for i in range(0, len(totals), 2):
            tall = jnp.concatenate(
                [x[:, at : at + LANES] for x in totals[i : i + 2] for at in range(0, FEATS, LANES)], axis=0
            )
            kt_part[i * 2 * cells : (i + 2) * 2 * cells] = tall.astype(BF16)

    def spilled(key_feat):
        return pltpu.make_async_copy(key_feat, feat_hbm, copy_sem.at[0])

    def refilled(key_feat):
        return pltpu.make_async_copy(feat_hbm, key_feat, copy_sem.at[1])

    def front(key_feat):
        for i in range(4):
            load(i).wait()

        def project(t, carry):
            rows = rows_at(t, TILE)
            hid = dot(enc[rows], in_w[...]).astype(BF16)
            hidden[rows] = hid
            unit, _ = moments(hid.astype(F32))
            nor = (unit * gain_one_ref[...] + shift_one_ref[...]).astype(BF16)
            normed[rows] = nor
            key = dot(nor, key_w[...]).astype(BF16)
            keys[rows] = key
            values[rows] = dot(nor, value_w[...]).astype(BF16)
            for j in range(HEADS // 2):
                pair = features(key[:, j * LANES : (j + 1) * LANES])
                key_feat[rows, j * 2 * FEATS : (j + 1) * 2 * FEATS] = pair.astype(BF16)
            return carry

        lax.fori_loop(0, tokens // TILE, project, 0)
        spilled(key_feat).start()
        totals = []
        for j in range(HEADS // 2):
            turned = lax.dot_general(
                value_w[:, j * LANES : (j + 1) * LANES],
                normed[...],
                (((0,), (1,)), ((), ())),
                preferred_element_type=F32,
            )
            totals += pair_sums(turned, keep_rows, lambda head: keep_rows, key_feat, j)
            if j % 2:
                forward_sum.tick(j // 2)
        store_totals(totals)
        forward_sum.tick(HEADS // 4)
        spilled(key_feat).wait()

    pl.run_scoped(front, pltpu.VMEM((tokens, HEADS * FEATS), BF16))

    def query_side(t, carry):
        rows = rows_at(t, TILE)
        query = dot(normed[rows], query_w[...]).astype(BF16)
        queries[rows] = query
        for j in range(HEADS // 2):
            pair = features(query[:, j * LANES : (j + 1) * LANES])
            query_feat[rows, j * 2 * FEATS : (j + 1) * 2 * FEATS] = pair.astype(BF16)
        return carry

    load(4).wait()
    forward_sum.go_on()
    slot_exchange.start(SLOTS_STEP)
    lax.fori_loop(0, tokens // TILE, query_side, 0)
    forward_sum.go_on()
    slot_exchange.start(SLOTS_STEP)
    tables()
    while forward_sum.begun():
        forward_sum.go_on()
        slot_exchange.start(SLOTS_STEP)
    slot_exchange.start(len(order))

    total_rows[...] = total_table(kt)
    load(5).wait()

    def middle(stream, grad_sum, unit_two, scale_two, act, grad_up):
        def attention(t, carry):
            rows = rows_at(t, TILE)
            here = block_hot(t, TILE)
            mask = dot_nt(here, cell_x[...])
            den = dot_nt(query_feat[rows], total_rows[...]) * dot_nt(here, cell_64[...])
            den_high = den.astype(BF16)
            den_low = (den - den_high.astype(F32)).astype(BF16)
            den_both = jnp.concatenate([den_high, den_low], axis=1)
            den_pair[rows] = den_both
            over = 1.0 / dot(den_both, spread[...])
            for j in range(HEADS // 2):
                at = pl.ds(j * width, width)
                num = fold(
                    dot_nt(query_feat[rows, j * 2 * FEATS : j * 2 * FEATS + FEATS], kv[at, :FEATS]),
                    dot_nt(query_feat[rows, j * 2 * FEATS + FEATS : (j + 1) * 2 * FEATS], kv[at, FEATS:]),
                    mask,
                )
                lanes = slice(j * LANES, (j + 1) * LANES)
                attended[rows, lanes] = (num * over[:, lanes]).astype(BF16)
            mixed = hidden[rows].astype(F32) + dot(attended[rows], out_w[...])
            stream[rows] = mixed
            unit, scale = moments(mixed)
            unit_two[rows] = unit.astype(BF16)
            scale_two[rows] = jnp.broadcast_to(scale, (TILE, LANES))
            normed_two[rows] = (unit * gain_two_ref[...] + shift_two_ref[...]).astype(BF16)
            return carry

        lax.fori_loop(0, tokens // TILE, attention, 0)

        slot_exchange.wait()
        for i in range(6, len(sources)):
            load(i).wait()

        def gather(t, carry):
            rows = rows_at(t, TILE)
            slot_col = dot_nt(
                block_hot(t, TILE), jnp.broadcast_to(slot_block, (LANES, blocks)).astype(BF16)
            ) * BLK + (iota((TILE, LANES), 0) & (BLK - 1)).astype(F32)
            pick = jnp.concatenate(
                [
                    hot(slot_col == (iota((TILE, LANES), 1) + i).astype(F32)).astype(BF16)
                    for i in range(0, slots.shape[0], LANES)
                ],
                axis=1,
            )
            share = jnp.concatenate([share_col[rows]] * (D // LANES), axis=1)
            cot[rows] = (dot(pick, slots[...]) * share).astype(BF16)
            return carry

        lax.fori_loop(0, tokens // TILE, gather, 0)

        for j in range(hidden_tiles):
            ff = slice(j * D, (j + 1) * D)

            def feed(t, carry):
                rows = rows_at(t, WIDE)
                x = dot(normed_two[rows], up_w[ff])
                square = x * x
                bent = jnp.tanh(x * (GELU_A + (GELU_A * GELU_B) * square))
                ramp = 0.5 + 0.5 * bent
                slope = ramp + (0.5 * x) * (1.0 - bent * bent) * (
                    GELU_A + (3.0 * GELU_A * GELU_B) * square
                )
                act[rows] = (x * ramp).astype(BF16)
                grad_up[rows] = (slope * dot_nt(cot[rows], down_w[ff])).astype(BF16)
                stream[rows] += dot(act[rows], down_w[ff])
                back = dot_nt(grad_up[rows], up_w[ff])
                if j == 0:
                    grad_sum[rows] = back
                else:
                    grad_sum[rows] += back
                return carry

            lax.fori_loop(0, tokens // WIDE, feed, 0)
            early_part[2 * j * D : (2 * j + 1) * D] = dot_tn(act[...], cot[...]).astype(BF16)
            early_part[(2 * j + 1) * D : (2 * j + 2) * D] = dot_tn(normed_two[...], grad_up[...]).astype(BF16)
            early_sum.tick(2 * j, 2 * j + 1)
            if j > 1:
                early_sum.tick(2 * j - 4, 2 * j - 3)

        def back(t, carry):
            rows = rows_at(t, TILE)
            act[rows] = stream[rows].astype(BF16)
            here = block_hot(t, TILE)
            grad_nor = grad_sum[rows]
            unit = unit_two[rows].astype(F32)
            sums[0:8] += jnp.sum((grad_nor * unit).reshape(TILE // 8, 8, D), axis=0)
            sums[8:16] += jnp.sum(grad_nor.reshape(TILE // 8, 8, D), axis=0)
            scale = jnp.concatenate([scale_two[rows]] * (D // LANES), axis=1)
            grad_mix = (
                cot[rows].astype(F32) + norm_back(grad_nor, gain_two_ref[...], unit, scale)
            ).astype(BF16)
            grad_att[rows] = grad_mix
            grad = dot_nt(grad_mix, out_w[...]) / dot(den_pair[rows], spread[...])
            grad_num[rows] = grad.astype(BF16)
            products = (grad * attended[rows].astype(F32)).astype(BF16)
            den_grad[rows] = dot_nt(products, spread[: HEADS * cells]) * dot_nt(here, cell_64[...]) * -1.0
            return carry

        lax.fori_loop(0, tokens // TILE, back, 0)
        early_sum.tick(*range(2 * hidden_tiles - 4, 2 * hidden_tiles))

        den_rows = jnp.concatenate(
            [den_grad[...], jnp.zeros((tokens, LANES - HEADS * cells), F32)], axis=1
        ).T
        totals = []
        for j in range(HEADS // 2):
            turned = grad_num[:, j * LANES : (j + 1) * LANES].astype(F32).T
            totals += pair_sums(
                turned, cell_rows, lambda head: den_rows[head * cells : (head + 1) * cells], query_feat, j
            )
            if j % 2:
                backward_sum.tick(j // 2)
        store_totals(totals)
        backward_sum.tick(HEADS // 4)

        for k in range(cells):
            cell = lax.rem(grp + k, cells)
            pick = hot(
                slot_row[0:1] == (iota((pair_rows, tokens), 0) + cell * pair_rows).astype(F32)
            ).astype(BF16)
            here = pl.ds(pl.multiple_of(cell * pair_rows, pair_rows), pair_rows)
            slots[here] = dot(pick, act[...]).astype(BF16)

    pl.run_scoped(
        middle,
        pltpu.VMEM((tokens, D), F32),
        pltpu.VMEM((tokens, D), F32),
        pltpu.VMEM((tokens, D), BF16),
        pltpu.VMEM((tokens, LANES), F32),
        pltpu.VMEM((tokens, D), BF16),
        pltpu.VMEM((tokens, D), BF16),
    )

    def layer_own():
        return pltpu.make_async_copy(slots.at[own_slots], layer_hbm.at[own_slots], copy_sem.at[2])

    def end(key_feat):
        refilled(key_feat).start()
        layer_own().start()

        def step(count=LAYER_STEP):
            backward_sum.go_on()
            early_sum.go_on_half()
            layer_exchange.start(count)

        def query_back(t, carry):
            rows = rows_at(t, TILE)
            mask = dot_nt(block_hot(t, TILE), cell_x[...])
            den = den_grad[rows].astype(BF16)
            for j in range(HEADS // 2):
                lanes = slice(j * LANES, (j + 1) * LANES)
                feats = slice(j * 2 * FEATS, (j + 1) * 2 * FEATS)
                a, b = unfold(grad_num[rows, lanes].astype(F32), mask)
                at = pl.ds(j * width, width)
                grad = jnp.concatenate([dot(a, kv[at, :FEATS]), dot(b, kv[at, FEATS:])], axis=1)
                grad += dot(den, total_rows[:, feats])
                queries[rows, lanes] = feature_back(
                    grad, query_feat[rows, feats], queries[rows, lanes]
                ).astype(BF16)
            return carry

        step()
        out_row = 2 * hidden_tiles * D
        early_part[out_row : out_row + D] = dot_tn(attended[...], grad_att[...]).astype(BF16)
        early_sum.tick(2 * hidden_tiles)
        step()
        lax.fori_loop(0, tokens // TILE // 2, query_back, 0)
        step()
        lax.fori_loop(tokens // TILE // 2, tokens // TILE, query_back, 0)
        step()
        early_part[out_row + D : out_row + 2 * D] = dot_tn(normed[...], queries[...]).astype(BF16)
        early_sum.tick(2 * hidden_tiles + 1)
        while backward_sum.begun():
            step()

        refilled(key_feat).wait()
        total_rows[...] = total_table(kt_grad)

        def key_back(t, carry):
            rows = rows_at(t, TILE)
            here = block_hot(t, TILE)
            keep = keep_col[rows]
            mask = dot_nt(here, cell_x[...]) * jnp.concatenate([keep] * (width // LANES), axis=1)
            mask_64 = (dot_nt(here, cell_64[...]) * keep[:, : HEADS * cells]).astype(BF16)
            for j in range(HEADS // 2):
                lanes = slice(j * LANES, (j + 1) * LANES)
                feats = slice(j * 2 * FEATS, (j + 1) * 2 * FEATS)
                a, b = unfold(values[rows, lanes].astype(F32), mask)
                at = pl.ds(j * width, width)
                feat = key_feat[rows, feats]
                grad = jnp.concatenate([dot(a, kv_grad[at, :FEATS]), dot(b, kv_grad[at, FEATS:])], axis=1)
                grad += dot(mask_64, total_rows[:, feats])
                keys[rows, lanes] = feature_back(grad, feat, keys[rows, lanes]).astype(BF16)
                values[rows, lanes] = fold(
                    dot_nt(feat[:, :FEATS], kv_grad[at, :FEATS]),
                    dot_nt(feat[:, FEATS:], kv_grad[at, FEATS:]),
                    mask,
                ).astype(BF16)
            return carry

        lax.fori_loop(0, tokens // TILE // 2, key_back, 0)
        early_sum.go_on_half()
        layer_exchange.start(LAYER_LATE)
        lax.fori_loop(tokens // TILE // 2, tokens // TILE, key_back, 0)
        early_sum.go_on_half()
        layer_exchange.start(LAYER_LATE)
        kv_part[0:D] = dot_tn(normed[...], keys[...]).astype(BF16)
        kv_part[D : 2 * D] = dot_tn(normed[...], values[...]).astype(BF16)
        late_sum.tick(0, 1)

        def hidden_back(t, carry):
            rows = rows_at(t, TILE)
            grad_nor = (
                dot_nt(queries[rows], query_w[...])
                + dot_nt(keys[rows], key_w[...])
                + dot_nt(values[rows], value_w[...])
            )
            unit, scale = moments(hidden[rows].astype(F32))
            sums[16:24] += jnp.sum((grad_nor * unit).reshape(TILE // 8, 8, D), axis=0)
            sums[24:32] += jnp.sum(grad_nor.reshape(TILE // 8, 8, D), axis=0)
            cot[rows] = (
                grad_att[rows].astype(F32) + norm_back(grad_nor, gain_one_ref[...], unit, scale)
            ).astype(BF16)
            return carry

        lax.fori_loop(0, tokens // TILE, hidden_back, 0)
        late_sum.tick(0, 1)
        kv_part[2 * D : 2 * D + D_IN] = dot_tn(enc[...], cot[...]).astype(BF16)
        small = jnp.concatenate(
            [jnp.sum(sums[8 * i : 8 * i + 8], axis=0, keepdims=True) for i in range(4)]
            + [jnp.zeros((12, D), F32)],
            axis=0,
        )
        at = 2 * D + D_IN
        kv_part[at : at + 16] = small.astype(BF16)
        kv_part[at + 16 :] = jnp.zeros((kv_part.shape[0] - at - 16, D), BF16)
        late_sum.tick(2, 3)
        early_sum.go_on_half()
        layer_exchange.start(LAYER_LATE)

        def encoder_grad(t, carry):
            rows = rows_at(t, TILE)
            enc[rows] = dot_nt(cot[rows], in_w[...]).astype(BF16)
            return carry

        lax.fori_loop(0, tokens // TILE, encoder_grad, 0)
        enc_copy = pltpu.make_async_copy(enc, enc_grad_hbm, copy_sem.at[3])
        enc_copy.start()
        while late_sum.begun():
            late_sum.go_on()
            early_sum.go_on_half()
            layer_exchange.start(LAYER_LATE)
        early_sum.run()
        ends = []
        for i, (at, rows, target) in enumerate(
            (
                (0, D, key_sum_hbm),
                (D, D, value_sum_hbm),
                (2 * D, D_IN, in_sum_hbm),
                (2 * D + D_IN, 16, small_sum_hbm),
            )
        ):
            ends.append(pltpu.make_async_copy(kv.at[pl.ds(at, rows)], target, copy_sem.at[4 + i]))
            ends[-1].start()
        layer_exchange.wait()
        layer_own().wait()
        enc_copy.wait()
        for copy in ends:
            copy.wait()

    pl.run_scoped(end, pltpu.VMEM((tokens, HEADS * FEATS), BF16))


def fused(
    mesh,
    encoded,
    destination,
    expressed,
    in_proj,
    gain_one,
    shift_one,
    query_w,
    key_w,
    value_w,
    out_w,
    gain_two,
    shift_two,
    up_w,
    down_w,
    random_features,
    out_cotangent,
):
    sizes = {"grp": mesh.shape["grp"], "seq": mesh.shape["seq"]}
    cells, splits, blocks = destination.shape
    tokens = encoded.shape[2]
    slot_total = out_cotangent.shape[2]
    cap = slot_total // (cells * BLK)
    width = cells * DH
    digits = digits_of(sizes)
    unit = 16 * sizes["grp"] * sizes["seq"]
    steps = 2 * sum(radix - 1 for _, _, radix in digits)
    early = 2 * FF + 2 * D
    half = HEADS // 2 * width
    count = half // unit + early // unit

    def vmem(shape, kind=BF16):
        return pltpu.VMEM(shape, kind)

    def shape(*dims):
        return jax.ShapeDtypeStruct(dims, BF16)

    spec, rest = pl.BlockSpec(memory_space=pltpu.VMEM), pl.BlockSpec(memory_space=pl.ANY)
    results = pl.pallas_call(
        functools.partial(fused_kernel, sizes, cap),
        out_shape=(
            shape(slot_total, D),
            shape(tokens, D_IN),
            shape(D_IN, D),
            shape(D, D),
            shape(D, D),
            shape(D, D),
            shape(D, D),
            shape(D, FF),
            shape(FF, D),
            shape(16, D),
            shape(tokens, HEADS * FEATS),
        ),
        in_specs=[spec] * 7 + [rest] * 9,
        out_specs=(rest,) * 11,
        scratch_shapes=[
            vmem((tokens, D_IN)),
            vmem((D_IN, D)),
            vmem((D, D)),
            vmem((D, D)),
            vmem((D, D)),
            vmem((D, D)),
            vmem((FF, D)),
            vmem((FF, D)),
            vmem((slot_total, D)),
            vmem((tokens, D)),
            vmem((tokens, D)),
            vmem((tokens, D)),
            vmem((tokens, D)),
            vmem((tokens, D)),
            vmem((tokens, D)),
            vmem((tokens, HEADS * FEATS)),
            vmem((half, 2 * FEATS)),
            vmem((half, 2 * FEATS)),
            vmem((half, 2 * FEATS)),
            vmem((half, 2 * FEATS)),
            vmem((unit, LANES)),
            vmem((unit, LANES)),
            vmem((unit, LANES)),
            vmem((unit, LANES)),
            vmem((tokens, D)),
            vmem((tokens, D)),
            vmem((tokens, D)),
            vmem((tokens, D)),
            vmem((tokens, 2 * HEADS * cells)),
            vmem((tokens, HEADS * cells), F32),
            vmem((early, D)),
            vmem((early, D)),
            vmem((early // unit * 16, D)),
            vmem((4 * DH, 2 * FEATS)),
            vmem((width, blocks)),
            vmem((HEADS * cells, blocks)),
            vmem((tokens, LANES), F32),
            vmem((tokens, LANES), F32),
            vmem((8, tokens), F32),
            vmem((HEADS * cells, HEADS * FEATS)),
            vmem((2 * HEADS * cells, D)),
            vmem((32, D), F32),
            pltpu.SemaphoreType.DMA((8 + FF // D,)),
            pltpu.SemaphoreType.DMA((PARTS * (cells - 1),)),
            pltpu.SemaphoreType.DMA((PARTS * (cells - 1),)),
            pltpu.SemaphoreType.DMA((PARTS * (cells - 1),)),
            pltpu.SemaphoreType.DMA((PARTS * (cells - 1),)),
            pltpu.SemaphoreType.DMA((8,)),
            pltpu.SemaphoreType.DMA((early // unit,)),
            pltpu.SemaphoreType.DMA((count * steps,)),
            pltpu.SemaphoreType.DMA((count * steps,)),
        ],
        compiler_params=pltpu.CompilerParams(
            collective_id=1, has_side_effects=True, vmem_limit_bytes=VMEM_LIMIT
        ),
        name="layer_and_gradients",
    )(
        destination,
        expressed,
        gain_one.reshape(1, D),
        shift_one.reshape(1, D),
        gain_two.reshape(1, D),
        shift_two.reshape(1, D),
        random_features,
        encoded.reshape(tokens, D_IN),
        in_proj,
        query_w,
        key_w,
        value_w,
        out_w,
        up_w,
        down_w,
        out_cotangent.reshape(slot_total, D),
    )
    layer, enc_grad, in_b, query_b, key_b, value_b, out_b, up_b, down_b, small_b = results[:10]
    small = small_b.astype(F32)
    return (
        layer.astype(F32).reshape(1, 1, slot_total, D),
        enc_grad.reshape(1, 1, tokens, D_IN),
        in_b.astype(F32),
        small[2],
        small[3],
        query_b.astype(F32),
        key_b.astype(F32),
        value_b.astype(F32),
        out_b.astype(F32),
        small[0],
        small[1],
        up_b.astype(F32),
        down_b.astype(F32),
    )


def layer_norm(values, gain, shift):
    center = values - jnp.mean(values, axis=-1, keepdims=True)
    variance = jnp.mean(center * center, axis=-1, keepdims=True)
    return center * lax.rsqrt(variance + 1e-05) * gain + shift


def feature_map(projected, omega_b, key_keep):
    row_count = projected.shape[0]
    pieces = projected.reshape(row_count, HEADS, DH)
    factor = DH ** (-0.25)
    logits = jnp.einsum("nhd,dm->nhm", pieces, omega_b, preferred_element_type=jnp.float32) * factor
    squares = (
        0.5
        * factor
        * factor
        * jnp.sum(jnp.square(pieces.astype(jnp.float32)), axis=-1, keepdims=True)
    )
    return jnp.exp(logits - squares) * FEATS ** (-0.5) * key_keep[:, None, None]


def feature_grad(grad_feat, feat_full, projected, omega_b):
    row_count = projected.shape[0]
    factor = DH ** (-0.25)
    scaled = grad_feat.astype(jnp.float32) * feat_full
    logit_grad = scaled.astype(jnp.bfloat16)
    pieces = projected.reshape(row_count, HEADS, DH).astype(jnp.float32)
    through = (
        jnp.einsum("nhm,dm->nhd", logit_grad, omega_b, preferred_element_type=jnp.float32) * factor
    )
    direct = pieces * (factor * factor) * jnp.sum(scaled, axis=-1, keepdims=True)
    return (through - direct).reshape(row_count, HEADS * DH).astype(jnp.bfloat16)


def weight_term(left, right):
    return jnp.einsum("nk,nd->kd", left, right, preferred_element_type=jnp.float32)


def plain(
    encoded,
    destination,
    expressed,
    in_proj,
    gain_one,
    shift_one,
    query_w,
    key_w,
    value_w,
    out_w,
    gain_two,
    shift_two,
    up_w,
    down_w,
    random_features,
    out_cotangent,
):
    cell_count = destination.shape[0]
    split_count = destination.shape[1]
    blocks = destination.shape[2]
    tokens = encoded.shape[2]
    block_len = tokens // blocks
    row_total = out_cotangent.shape[2]
    slot_count = row_total // (cell_count * block_len)
    pair_rows = slot_count * block_len
    group_index = lax.axis_index("grp")
    split_index = lax.axis_index("seq")
    targets = jnp.arange(cell_count, dtype=jnp.int32)
    slot_ids = jnp.arange(slot_count, dtype=jnp.int32)
    within = jnp.arange(block_len, dtype=jnp.int32)
    block_ids = jnp.arange(blocks, dtype=jnp.int32)
    column = lax.dynamic_index_in_dim(destination, split_index, 1, keepdims=False)
    block_hits = (column[:, :, None] == targets).astype(jnp.int32)
    block_rank = jnp.sum(jnp.cumsum(block_hits, axis=1) * block_hits, axis=2) - 1
    own_dest = lax.dynamic_index_in_dim(column, group_index, 0, keepdims=False)
    own_rank = lax.dynamic_index_in_dim(block_rank, group_index, 0, keepdims=False)
    send_match = (
        (own_dest[:, None, None] == targets[:, None]) & (own_rank[:, None, None] == slot_ids)
    ).astype(jnp.int32)
    send_found = jnp.sum(send_match, axis=0)
    send_block = jnp.sum(send_match * block_ids[:, None, None], axis=0)
    send_index = (send_block[:, :, None] * block_len + within).reshape(-1)
    send_keep = jnp.repeat(send_found.reshape(-1), block_len).astype(jnp.bfloat16)
    back_index = ((own_dest * slot_count + own_rank)[:, None] * block_len + within).reshape(-1)
    recv_match = (
        (column[:, :, None] == group_index) & (block_rank[:, :, None] == slot_ids)
    ).astype(jnp.int32)
    recv_found = jnp.sum(recv_match, axis=1)
    recv_block = jnp.sum(recv_match * block_ids[:, None], axis=1)
    recv_token = (recv_block[:, :, None] * block_len + within).reshape(cell_count, pair_rows)
    expressed_col = lax.dynamic_index_in_dim(expressed, split_index, 1, keepdims=False)
    valid = jnp.repeat(recv_found.reshape(-1), block_len).astype(jnp.float32)
    key_keep = (
        jnp.take_along_axis(expressed_col, recv_token, axis=1).reshape(-1).astype(jnp.float32)
        * valid
    )
    block_sum = jnp.sum(expressed.reshape(cell_count, split_count, blocks, block_len), axis=3)
    dest_hits = destination[..., None] == targets
    counts = jnp.sum(jnp.where(dest_hits, block_sum[..., None], 0), axis=(0, 1, 2)).astype(
        jnp.float32
    )
    own_count = lax.dynamic_index_in_dim(counts, group_index, 0, keepdims=False)
    share = cell_count * own_count / jnp.sum(counts)
    token_rows = encoded.reshape(tokens, D_IN)
    token_hidden = jnp.dot(token_rows, in_proj, preferred_element_type=jnp.float32).astype(
        jnp.bfloat16
    )
    outgoing = jnp.take(token_hidden, send_index, axis=0) * send_keep[:, None]
    hidden_b = lax.all_to_all(
        outgoing.reshape(cell_count, pair_rows, D),
        "grp",
        split_axis=0,
        concat_axis=0,
        tiled=True,
    ).reshape(row_total, D)
    hidden_f = hidden_b.astype(jnp.float32)
    normed_f, norm_one_pull = jax.vjp(layer_norm, hidden_f, gain_one, shift_one)
    normed_b = normed_f.astype(jnp.bfloat16)
    queries_b = jnp.dot(normed_b, query_w, preferred_element_type=jnp.float32).astype(jnp.bfloat16)
    keys_b = jnp.dot(normed_b, key_w, preferred_element_type=jnp.float32).astype(jnp.bfloat16)
    values_b = jnp.dot(normed_b, value_w, preferred_element_type=jnp.float32).astype(jnp.bfloat16)
    query_full = feature_map(queries_b, random_features, jnp.ones((row_total,), jnp.float32))
    key_full = feature_map(keys_b, random_features, key_keep)
    query_feature_rows = query_full.astype(jnp.bfloat16)
    key_feature_rows = key_full.astype(jnp.bfloat16)
    value_per_head = values_b.reshape(row_total, HEADS, DH)
    value_part = jnp.einsum(
        "pgk,pgz->gkz", key_feature_rows, value_per_head, preferred_element_type=jnp.float32
    )
    total_part = jnp.sum(key_feature_rows, axis=0, dtype=jnp.float32)
    key_value_products, key_total = lax.psum((value_part, total_part), "seq")
    key_value_batched = key_value_products.astype(jnp.bfloat16)
    attention_numerator = jnp.einsum(
        "bli,lie->ble", query_feature_rows, key_value_batched, preferred_element_type=jnp.float32
    )
    denominator = jnp.sum(query_feature_rows.astype(jnp.float32) * key_total[None], axis=-1)
    attended_b = (
        (attention_numerator / denominator[:, :, None]).reshape(row_total, D).astype(jnp.bfloat16)
    )
    mixed = hidden_f + jnp.dot(attended_b, out_w, preferred_element_type=jnp.float32)
    normed_two_f, norm_two_pull = jax.vjp(layer_norm, mixed, gain_two, shift_two)
    normed_two_b = normed_two_f.astype(jnp.bfloat16)
    expanded = jnp.dot(normed_two_b, up_w, preferred_element_type=jnp.float32)
    activated_f, gelu_pull = jax.vjp(partial_gelu, expanded)
    activated_b = activated_f.astype(jnp.bfloat16)
    layer_out = (mixed + jnp.dot(activated_b, down_w, preferred_element_type=jnp.float32)) * valid[
        :, None
    ]
    grad_out = out_cotangent.reshape(row_total, D).astype(jnp.float32) * (valid * share)[:, None]
    grad_mlp = grad_out.astype(jnp.bfloat16)
    down_term = weight_term(activated_b, grad_mlp)
    grad_activated = jnp.dot(grad_mlp, down_w.T, preferred_element_type=jnp.float32)
    grad_up = gelu_pull(grad_activated)[0].astype(jnp.bfloat16)
    up_term = weight_term(normed_two_b, grad_up)
    grad_normed_two = jnp.dot(grad_up, up_w.T, preferred_element_type=jnp.float32)
    mixed_back, gain_two_term, shift_two_term = norm_two_pull(grad_normed_two)
    grad_mixed = grad_out + mixed_back
    grad_att = grad_mixed.astype(jnp.bfloat16)
    out_term = weight_term(attended_b, grad_att)
    grad_attended = jnp.dot(grad_att, out_w.T, preferred_element_type=jnp.float32).reshape(
        row_total, HEADS, DH
    )
    numerator_gradient = (grad_attended / denominator[:, :, None]).astype(jnp.bfloat16)
    grad_den = -jnp.sum(grad_attended * attention_numerator, axis=-1) / (denominator * denominator)
    value_grad_part = jnp.einsum(
        "pgk,pgz->gkz", query_feature_rows, numerator_gradient, preferred_element_type=jnp.float32
    )
    total_grad_part = jnp.sum(query_feature_rows.astype(jnp.float32) * grad_den[:, :, None], axis=0)
    grad_query_feat = (
        jnp.einsum(
            "pao,ajo->paj",
            numerator_gradient,
            key_value_batched,
            preferred_element_type=jnp.float32,
        )
        + grad_den[:, :, None] * key_total[None]
    ).astype(jnp.bfloat16)
    grad_kv, grad_total = lax.psum((value_grad_part, total_grad_part), "seq")
    key_value_gradient_batched = grad_kv.astype(jnp.bfloat16)
    grad_key_feat = (
        jnp.einsum(
            "pao,ajo->paj",
            value_per_head,
            key_value_gradient_batched,
            preferred_element_type=jnp.float32,
        )
        + grad_total[None]
    ).astype(jnp.bfloat16)
    grad_values = (
        jnp.einsum(
            "bli,lie->ble",
            key_feature_rows,
            key_value_gradient_batched,
            preferred_element_type=jnp.float32,
        )
        .reshape(row_total, D)
        .astype(jnp.bfloat16)
    )
    grad_queries = feature_grad(grad_query_feat, query_full, queries_b, random_features)
    grad_keys = feature_grad(grad_key_feat, key_full, keys_b, random_features)
    query_term = weight_term(normed_b, grad_queries)
    key_term = weight_term(normed_b, grad_keys)
    value_term = weight_term(normed_b, grad_values)
    grad_normed = jnp.dot(grad_queries, query_w.T, preferred_element_type=jnp.float32)
    grad_normed = grad_normed + jnp.dot(grad_keys, key_w.T, preferred_element_type=jnp.float32)
    grad_normed = grad_normed + jnp.dot(grad_values, value_w.T, preferred_element_type=jnp.float32)
    hidden_back, gain_one_term, shift_one_term = norm_one_pull(grad_normed)
    grad_hidden = (grad_mixed + hidden_back).astype(jnp.bfloat16)
    returned = lax.all_to_all(
        grad_hidden.reshape(cell_count, pair_rows, D),
        "grp",
        split_axis=0,
        concat_axis=0,
        tiled=True,
    )
    token_grad = jnp.take(returned.reshape(row_total, D), back_index, axis=0)
    encoded_grad = jnp.dot(token_grad, in_proj.T, preferred_element_type=jnp.float32).astype(
        jnp.bfloat16
    )
    in_term = weight_term(token_rows, token_grad)
    (
        in_sum,
        query_sum,
        key_sum,
        value_sum,
        out_sum,
        up_sum,
        down_sum,
        gain_one_sum,
        shift_one_sum,
        gain_two_sum,
        shift_two_sum,
    ) = lax.psum(
        (
            in_term,
            query_term,
            key_term,
            value_term,
            out_term,
            up_term,
            down_term,
            gain_one_term,
            shift_one_term,
            gain_two_term,
            shift_two_term,
        ),
        ("grp", "seq"),
    )
    return (
        layer_out.reshape(1, 1, row_total, D),
        encoded_grad.reshape(1, 1, tokens, D_IN),
        in_sum,
        gain_one_sum,
        shift_one_sum,
        query_sum,
        key_sum,
        value_sum,
        out_sum,
        gain_two_sum,
        shift_two_sum,
        up_sum,
        down_sum,
    )


def partial_gelu(values):
    return jax.nn.gelu(values, approximate=True)


def solution(mesh):
    in_specs = (
        P("grp", "seq", None, None),
        P(),
        P(),
        P(),
        P(),
        P(),
        P(),
        P(),
        P(),
        P(),
        P(),
        P(),
        P(),
        P(),
        P(),
        P("grp", "seq", None, None),
    )
    out_specs = (
        P("grp", "seq", None, None),
        P("grp", "seq", None, None),
        P(),
        P(),
        P(),
        P(),
        P(),
        P(),
        P(),
        P(),
        P(),
        P(),
        P(),
    )
    body = functools.partial(fused, mesh) if mesh.shape["grp"] <= FUSED_CELLS else plain
    return jax.shard_map(body, mesh=mesh, in_specs=in_specs, out_specs=out_specs, check_vma=False)
```

```python
import functools

import jax
import jax.numpy as jnp
from jax import lax
from jax.experimental import pallas as pl
from jax.experimental.pallas import tpu as pltpu
from jax.sharding import PartitionSpec as P

D_IN = 768
D = 512
HEADS = 8
DH = 64
FEATS = 256
FF = 2048
BLK = 8
LANES = 128
TILE = 256
WIDE = 512
PARTS = 4
SLOTS_FIRST = 8
SLOTS_PACE = (4, 3, 1, 0, 0, 0, 0, 2, 4, 4)
LAYER_FIRST = 4
LAYER_FEED = 4
LAYER_PACE = (1, 1, 1, 0, 0, 0, 1, 1, 1, 1)
LAYER_LATE = 2
KV_ORDERS = (0, 1, 0)
EARLY_ORDERS = (0, 1)
EARLY_WINDOW = False
LATE_ORDERS = (0, 1)
FUSED_CELLS = 8
VMEM_LIMIT = 62 << 20
LOG2E = 1.4426950408889634
GELU_A = 0.7978845608028654
GELU_B = 0.044715
F32, BF16 = jnp.float32, jnp.bfloat16
MESH = pl.DeviceIdType.MESH


def dot(a, b):
    return jnp.dot(a, b, preferred_element_type=F32)


def dot_nt(a, b):
    return lax.dot_general(a, b, (((1,), (1,)), ((), ())), preferred_element_type=F32)


def dot_tn(a, b):
    return lax.dot_general(a, b, (((0,), (0,)), ((), ())), preferred_element_type=F32)


def iota(shape, axis):
    return lax.broadcasted_iota(jnp.int32, shape, axis)


def hot(condition):
    return jnp.where(condition, 1.0, 0.0)


def moments(x):
    center = x - jnp.mean(x, axis=-1, keepdims=True)
    scale = lax.rsqrt(jnp.mean(center * center, axis=-1, keepdims=True) + 1e-05)
    return center * scale, scale


def norm_back(grad, gain, unit, scale):
    inner = grad * gain
    return scale * (
        inner
        - jnp.mean(inner, axis=-1, keepdims=True)
        - unit * jnp.mean(inner * unit, axis=-1, keepdims=True)
    )


def digits_of(sizes):
    digits = []
    for axis in ("seq", "grp"):
        if sizes[axis] > 1:
            digits.append((axis, 1, 2))
        step = 2
        while step < sizes[axis]:
            digits.append((axis, step, 2))
            step *= 2
    return digits


def peers(digit):
    grp, seq = lax.axis_index("grp"), lax.axis_index("seq")
    axis, step, radix = digit
    index = seq if axis == "seq" else grp
    value = (index // step) % radix
    found = []
    for m in range(1, radix):
        other = index + ((value + m) % radix - value) * step
        found.append((grp, other) if axis == "seq" else (other, seq))
    return value, found


def digit_orders(digits):
    first, second = list(digits), list(digits)
    if len(digits) > 2:
        second[1], second[2] = second[2], second[1]
    return first, second


class Sum:
    def __init__(self, digits, pieces, pattern, send, recv, base, settle=None):
        self.pieces, self.send, self.recv, self.base, self.settle = pieces, send, recv, base, settle
        self.half_steps, self.steps = len(digits), 2 * len(digits)
        self.copies = 2 * sum(radix - 1 for _, _, radix in digits)
        self.step = [-1] * len(pieces)
        self.turn = 0
        self.plans = []
        orders = digit_orders(digits)
        for c, piece in enumerate(pieces):
            at, rows, inbox_at, sem = 0, piece[6], piece[3], base + c * self.copies
            plan, kept = [], []
            for digit in orders[pattern[c % len(pattern)]]:
                value, found = peers(digit)
                radix = digit[2]
                rows //= radix
                keep = at + value * rows
                moves = []
                for m, device in enumerate(found, 1):
                    moves.append((device, at + (value + m) % radix * rows, inbox_at, sem))
                    inbox_at += rows
                    sem += 1
                kept.append((found, keep, rows))
                plan.append((moves, keep, rows))
                at = keep
            for found, keep, rows in reversed(kept):
                moves = [(device, keep, None, sem + m) for m, device in enumerate(found)]
                sem += len(found)
                plan.append((moves, keep, rows))
            self.plans.append(plan)

    def transfers(self, c, k):
        part, start, inbox, _, total, total_at, _, own = self.pieces[c]
        moves, _, rows = self.plans[c][k]
        found = []
        for device, at, inbox_at, sem in moves:
            if k < self.half_steps:
                source = part.at[pl.ds(pl.multiple_of(start + at, 16), rows)]
                target = inbox.at[pl.ds(inbox_at, rows)]
            else:
                target = total.at[pl.ds(pl.multiple_of(total_at + at, 16), rows)]
                source = target if own is None or k > self.half_steps else own
            found.append(
                pltpu.make_async_remote_copy(
                    src_ref=source,
                    dst_ref=target,
                    send_sem=self.send.at[sem],
                    recv_sem=self.recv.at[sem],
                    device_id=device,
                    device_id_type=MESH,
                )
            )
        return found

    def settled(self, c):
        _, _, _, _, total, total_at, _, own = self.pieces[c]
        _, at, rows = self.plans[c][self.half_steps]
        target = total.at[pl.ds(pl.multiple_of(total_at + at, 16), rows)]
        return pltpu.make_async_copy(own, target, self.settle.at[c])

    def finish(self, c):
        k = self.step[c]
        part, start, inbox, _, total, total_at, _, own = self.pieces[c]
        for transfer in self.transfers(c, k):
            transfer.wait()
        if k == self.half_steps and own is not None:
            self.settled(c).wait()
        if k >= self.half_steps:
            return
        moves, keep, rows = self.plans[c][k]
        step = min(rows, 256)
        last = k == self.half_steps - 1

        def add(i, carry):
            here = pl.ds(pl.multiple_of(start + keep + i * step, 16), step)
            value = part[here].astype(F32)
            for _, _, inbox_at, _ in moves:
                value += inbox[pl.ds(pl.multiple_of(inbox_at + i * step, 16), step)].astype(F32)
            value = value.astype(BF16)
            if not last:
                part[here] = value
            elif own is None:
                total[pl.ds(pl.multiple_of(total_at + keep + i * step, 16), step)] = value
            else:
                own[...] = value
            return carry

        if rows == step:
            add(0, 0)
        else:
            lax.fori_loop(0, rows // step, add, 0)
        if last and own is not None:
            self.settled(c).start()

    def tick(self, *which):
        for c in which:
            if self.step[c] >= 0:
                self.finish(c)
            self.step[c] += 1
            if self.step[c] < self.steps:
                for transfer in self.transfers(c, self.step[c]):
                    transfer.start()

    def begun(self):
        return [c for c in range(len(self.pieces)) if 0 <= self.step[c] < self.steps]

    def go_on(self):
        self.tick(*self.begun())

    def go_on_half(self):
        self.turn += 1
        self.tick(*[c for c in self.begun() if (c // 2 + self.turn) % 2])

    def run(self):
        while self.begun():
            self.go_on()


class Exchange:
    def __init__(self, makers):
        self.makers, self.started = makers, 0

    def start(self, count):
        for make in self.makers[self.started : self.started + count]:
            make().start()
        self.started = min(self.started + count, len(self.makers))

    def wait(self):
        self.start(len(self.makers))
        for make in self.makers:
            make().wait()


def fused_kernel(
    sizes,
    cap,
    dest_hbm,
    expr_hbm,
    gain_one_hbm,
    shift_one_hbm,
    gain_two_hbm,
    shift_two_hbm,
    omega_hbm,
    enc_hbm,
    in_hbm,
    query_hbm,
    key_hbm,
    value_hbm,
    out_hbm,
    up_hbm,
    down_hbm,
    cot_hbm,
    layer_hbm,
    enc_grad_hbm,
    in_sum_hbm,
    query_sum_hbm,
    key_sum_hbm,
    value_sum_hbm,
    out_sum_hbm,
    up_sum_hbm,
    down_sum_hbm,
    small_sum_hbm,
    feat_hbm,
    dest_ref,
    expr_ref,
    gain_one_ref,
    shift_one_ref,
    gain_two_ref,
    shift_two_ref,
    omega_ref,
    enc,
    in_w,
    query_w,
    key_w,
    value_w,
    out_w,
    up_w,
    down_w,
    slots,
    cot,
    hidden,
    normed,
    queries,
    keys,
    values,
    query_feat,
    kv_part,
    kv_inbox,
    kv,
    kv_grad,
    kt_part,
    kt_inbox,
    kt,
    kt_grad,
    attended,
    normed_two,
    grad_att,
    grad_num,
    den_pair,
    den_grad,
    early_part,
    early_inbox,
    early_own,
    feat_w,
    cell_x,
    cell_64,
    keep_col,
    share_col,
    slot_row,
    total_rows,
    spread,
    sums,
    load_sem,
    slot_send,
    slot_recv,
    layer_send,
    layer_recv,
    copy_sem,
    settle_sem,
    sum_send,
    sum_recv,
):
    grp, seq = lax.axis_index("grp"), lax.axis_index("seq")
    cells = sizes["grp"]
    digits = digits_of(sizes)
    tokens = enc.shape[0]
    blocks = dest_ref.shape[2]
    width = cells * DH
    pair_rows = slots.shape[0] // cells
    unit_rows = 16 * sizes["grp"] * sizes["seq"]
    factor = DH ** (-0.25)
    hidden_tiles = FF // D

    own_slots = pl.ds(pl.multiple_of(grp * pair_rows, pair_rows), pair_rows)
    sources = [
        (enc_hbm, enc),
        (in_hbm, in_w),
        (key_hbm, key_w),
        (value_hbm, value_w),
        (query_hbm, query_w),
        (out_hbm, out_w),
        (down_hbm, down_w),
        (cot_hbm.at[own_slots], slots.at[own_slots]),
    ]
    sources += [(up_hbm.at[:, pl.ds(j * D, D)], up_w.at[pl.ds(j * D, D)]) for j in range(hidden_tiles)]

    def load(i):
        return pltpu.make_async_copy(*sources[i], load_sem.at[i])

    matrices = len(sources)
    sources += [
        (dest_hbm, dest_ref),
        (expr_hbm, expr_ref),
        (omega_hbm, omega_ref),
        (gain_one_hbm, gain_one_ref),
        (shift_one_hbm, shift_one_ref),
        (gain_two_hbm, gain_two_ref),
        (shift_two_hbm, shift_two_ref),
    ]
    for i in list(range(matrices, len(sources))) + list(range(matrices)):
        load(i).start()

    barrier = pltpu.get_barrier_semaphore()
    others = [(lax.rem(grp + k, cells), seq) for k in range(1, cells)]
    mates = [device for digit in digits if digit[0] == "seq" for device in peers(digit)[1]]
    for device in others + mates:
        pl.semaphore_signal(barrier, inc=1, device_id=device, device_id_type=MESH)

    part_rows = pair_rows // PARTS

    def slot_copy(k, i):
        theirs = pl.multiple_of(others[k][0] * pair_rows + i * part_rows, part_rows)
        ours = pl.multiple_of(grp * pair_rows + i * part_rows, part_rows)
        return pltpu.make_async_remote_copy(
            src_ref=cot_hbm.at[pl.ds(theirs, part_rows)],
            dst_ref=slots.at[pl.ds(ours, part_rows)],
            send_sem=slot_send.at[k * PARTS + i],
            recv_sem=slot_recv.at[k * PARTS + i],
            device_id=others[k],
            device_id_type=MESH,
        )

    def layer_copy(k, i):
        theirs = pl.multiple_of(others[k][0] * pair_rows + i * part_rows, part_rows)
        ours = pl.multiple_of(grp * pair_rows + i * part_rows, part_rows)
        return pltpu.make_async_remote_copy(
            src_ref=slots.at[pl.ds(theirs, part_rows)],
            dst_ref=layer_hbm.at[pl.ds(ours, part_rows)],
            send_sem=layer_send.at[k * PARTS + i],
            recv_sem=layer_recv.at[k * PARTS + i],
            device_id=others[k],
            device_id_type=MESH,
        )

    order = [(k, i) for i in range(PARTS) for k in range(cells - 1)]
    slot_exchange = Exchange([functools.partial(slot_copy, k, i) for k, i in order])
    layer_exchange = Exchange([functools.partial(layer_copy, k, i) for k, i in order])

    def columns(ref, i):
        return ref.at[:, pl.ds(i * FEATS, FEATS)]

    def kv_pieces(total, rows):
        return [
            (columns(kv_part, i), at, columns(kv_inbox, i), at, columns(total, i), at, rows, None)
            for at in range(0, kv.shape[0], rows)
            for i in range(2)
        ]

    def kt_piece(total):
        return [(kt_part, 0, kt_inbox, 0, total, 0, kt_part.shape[0], None)]

    forward_sum = Sum(
        digits, kv_pieces(kv, width) + kt_piece(kt), KV_ORDERS, sum_send, sum_recv, 0
    )
    backward_sum = Sum(
        digits, kv_pieces(kv_grad, width) + kt_piece(kt_grad), KV_ORDERS, sum_send, sum_recv, 0
    )
    late_sum = Sum(digits, kv_pieces(kv, unit_rows), LATE_ORDERS, sum_send, sum_recv, 0)
    early_totals = []
    for j in range(hidden_tiles):
        early_totals.append((down_sum_hbm, j * D))
        early_totals.append((up_sum_hbm.at[:, pl.ds(j * D, D)], 0))
    early_totals += [(out_sum_hbm, 0), (query_sum_hbm, 0)]
    early_sum = Sum(
        digits,
        [
            (early_part, c * D, early_inbox, c * D, total, at, D, early_own.at[pl.ds(c * 16, 16)])
            for c, (total, at) in enumerate(early_totals)
        ],
        EARLY_ORDERS,
        sum_send,
        sum_recv,
        forward_sum.copies * len(forward_sum.pieces),
        settle_sem,
    )
    for i in range(matrices, len(sources)):
        load(i).wait()

    own = dest_ref[grp, pl.ds(seq, 1), :]
    cell_hot = hot(iota((cells, blocks), 0) == own)
    block_of = hot(iota((blocks, tokens), 1) >> 3 == iota((blocks, tokens), 0)).astype(BF16)
    expressed = expr_ref[grp, pl.ds(seq, 1), :].astype(F32)
    cell_rows = dot(cell_hot.astype(BF16), block_of)
    keep_rows = cell_rows * expressed
    kt_part[...] = jnp.zeros_like(kt_part)
    omega = omega_ref[...]
    zero = jnp.zeros_like(omega)
    one = jnp.ones_like(omega)
    feat_w[...] = jnp.concatenate(
        [
            jnp.concatenate([omega, zero], axis=1),
            jnp.concatenate([zero, omega], axis=1),
            jnp.concatenate([-one, zero], axis=1),
            jnp.concatenate([zero, -one], axis=1),
        ],
        axis=0,
    )

    def tables():
        cell_x[...] = hot(iota((width, blocks), 0) >> 6 == own).astype(BF16)
        cell_64[...] = hot((iota((HEADS * cells, blocks), 0) & (cells - 1)) == own).astype(BF16)
        earlier = hot(iota((blocks, blocks), 0) < iota((blocks, blocks), 1)).astype(BF16)
        rank = jnp.sum(dot(cell_hot.astype(BF16), earlier) * cell_hot, axis=0, keepdims=True)
        slot_block = own.astype(F32) * cap + rank
        slot_row[...] = dot(jnp.broadcast_to(slot_block, (8, blocks)).astype(BF16), block_of) * BLK + (
            iota((8, tokens), 1) & (BLK - 1)
        ).astype(F32)
        keep_col[...] = jnp.broadcast_to(expressed, (LANES, tokens)).T
        sums[...] = jnp.zeros_like(sums)
        counted = [jnp.zeros(dest_ref.shape[1:], F32) for _ in range(cells)]
        whole = jnp.zeros(dest_ref.shape[1:], F32)
        for g in range(dest_ref.shape[0]):
            block_sum = dot_nt(expr_ref[g].astype(F32).astype(BF16), block_of)
            whole += block_sum
            for c in range(cells):
                counted[c] += jnp.where(dest_ref[g] == c, block_sum, 0.0)
        share = jnp.zeros((1, blocks), F32)
        for c in range(cells):
            share += jnp.where(own == c, jnp.sum(counted[c], keepdims=True), 0.0)
        share = share * cells / jnp.sum(whole, keepdims=True)
        share_col[...] = lax.dot_general(
            hot(iota((tokens, blocks), 0) >> 3 == iota((tokens, blocks), 1)),
            jnp.broadcast_to(share, (LANES, blocks)),
            (((1,), (1,)), ((), ())),
            precision=lax.Precision.HIGHEST,
            preferred_element_type=F32,
        )
        head_lanes = iota((HEADS * cells * 2, D), 1) >> 6
        spread[...] = hot(
            (iota((HEADS * cells * 2, D), 0) & (HEADS * cells - 1)) >> cells.bit_length() - 1 == head_lanes
        ).astype(BF16)
        return slot_block

    def rows_at(t, tile):
        return pl.ds(pl.multiple_of(t * tile, tile), tile)

    def block_hot(t, tile):
        return hot((iota((tile, blocks), 0) + t * tile) >> 3 == iota((tile, blocks), 1)).astype(BF16)

    def fold(a, b, mask):
        left = iota((a.shape[0], LANES), 1) < DH
        a, b = a * mask, b * mask
        sum_a = sum(a[:, i : i + LANES] for i in range(0, width, LANES))
        sum_b = sum(b[:, i : i + LANES] for i in range(0, width, LANES))
        return jnp.where(left, sum_a, sum_b) + pltpu.roll(jnp.where(left, sum_b, sum_a), DH, 1)

    def unfold(x, mask):
        left = iota((x.shape[0], LANES), 1) < DH
        turned = pltpu.roll(x, DH, 1)
        a, b = jnp.where(left, x, turned), jnp.where(left, turned, x)
        copies = width // LANES
        return (
            (jnp.concatenate([a] * copies, axis=1) * mask).astype(BF16),
            (jnp.concatenate([b] * copies, axis=1) * mask).astype(BF16),
        )

    def features(x):
        xf = x.astype(F32)
        squares = (xf * xf * (0.0625 / factor)).astype(BF16)
        inner = dot(jnp.concatenate([x, squares], axis=1), feat_w[...])
        return jnp.exp2(inner * (factor * LOG2E) - 4.0)

    def feature_back(grad, feat, x):
        scaled = (grad.astype(BF16).astype(F32) * feat.astype(F32)).astype(BF16)
        through = dot_nt(scaled, feat_w[...])
        return through[:, :LANES] * factor + through[:, LANES:] * x.astype(F32) * (factor * factor)

    def total_table(ref):
        flat = ref[: cells * HEADS * FEATS // LANES].astype(F32)
        row = jnp.concatenate(
            [flat[i * cells : (i + 1) * cells] for i in range(HEADS * FEATS // LANES)], axis=1
        )
        full = jnp.concatenate([row] * HEADS, axis=0)
        shape = (HEADS * cells, HEADS * FEATS)
        return (full * hot(iota(shape, 0) >> cells.bit_length() - 1 == iota(shape, 1) >> 8)).astype(BF16)

    def pair_sums(turned, mask_rows, extra, feat_ref, j):
        totals = []
        for i in range(2):
            head = 2 * j + i
            own_rows = turned[i * DH : (i + 1) * DH]
            tall = jnp.concatenate(
                [own_rows * mask_rows[c : c + 1] for c in range(cells)] + [extra(head)], axis=0
            ).astype(BF16)
            both = dot(tall, feat_ref[:, head * FEATS : (head + 1) * FEATS])
            kv_part[j * width : (j + 1) * width, i * FEATS : (i + 1) * FEATS] = both[:width].astype(BF16)
            totals.append(both[width : width + cells])
        return totals

    def store_totals(totals):
        for i in range(0, len(totals), 2):
            tall = jnp.concatenate(
                [x[:, at : at + LANES] for x in totals[i : i + 2] for at in range(0, FEATS, LANES)], axis=0
            )
            kt_part[i * 2 * cells : (i + 2) * 2 * cells] = tall.astype(BF16)

    def spilled(key_feat):
        return pltpu.make_async_copy(key_feat, feat_hbm, copy_sem.at[0])

    def refilled(key_feat):
        return pltpu.make_async_copy(feat_hbm, key_feat, copy_sem.at[1])

    def front(key_feat):
        for i in range(4):
            load(i).wait()

        def project(t, carry):
            rows = rows_at(t, TILE)
            hid = dot(enc[rows], in_w[...]).astype(BF16)
            hidden[rows] = hid
            unit, _ = moments(hid.astype(F32))
            nor = (unit * gain_one_ref[...] + shift_one_ref[...]).astype(BF16)
            normed[rows] = nor
            key = dot(nor, key_w[...]).astype(BF16)
            keys[rows] = key
            values[rows] = dot(nor, value_w[...]).astype(BF16)
            for j in range(HEADS // 2):
                pair = features(key[:, j * LANES : (j + 1) * LANES])
                key_feat[rows, j * 2 * FEATS : (j + 1) * 2 * FEATS] = pair.astype(BF16)
            return carry

        lax.fori_loop(0, 1, project, 0)
        pl.semaphore_wait(barrier, len(others) + len(mates))
        slot_exchange.start(SLOTS_FIRST)
        lax.fori_loop(1, tokens // TILE, project, 0)
        spilled(key_feat).start()
        totals = []
        for j in range(HEADS // 2):
            turned = lax.dot_general(
                value_w[:, j * LANES : (j + 1) * LANES],
                normed[...],
                (((0,), (1,)), ((), ())),
                preferred_element_type=F32,
            )
            totals += pair_sums(turned, keep_rows, lambda head: keep_rows, key_feat, j)
            forward_sum.tick(2 * j, 2 * j + 1)
        store_totals(totals)
        forward_sum.tick(HEADS)
        spilled(key_feat).wait()

    pl.run_scoped(front, pltpu.VMEM((tokens, HEADS * FEATS), BF16))

    def query_side(t, carry):
        rows = rows_at(t, TILE)
        query = dot(normed[rows], query_w[...]).astype(BF16)
        queries[rows] = query
        for j in range(HEADS // 2):
            pair = features(query[:, j * LANES : (j + 1) * LANES])
            query_feat[rows, j * 2 * FEATS : (j + 1) * 2 * FEATS] = pair.astype(BF16)
        return carry

    load(4).wait()
    pace = list(SLOTS_PACE)

    def forward_step():
        forward_sum.go_on()
        slot_exchange.start(pace.pop(0) if pace else 0)

    forward_step()
    lax.fori_loop(0, tokens // TILE, query_side, 0)
    forward_step()
    slot_block = tables()
    while forward_sum.begun():
        forward_step()
    slot_exchange.start(len(order))

    total_rows[...] = total_table(kt)
    load(5).wait()

    def layer_own():
        return pltpu.make_async_copy(slots.at[own_slots], layer_hbm.at[own_slots], copy_sem.at[2])

    def middle(stream, grad_sum, unit_two, scale_two, slopes):
        def attention(t, carry):
            rows = rows_at(t, TILE)
            here = block_hot(t, TILE)
            mask = dot_nt(here, cell_x[...])
            den = dot_nt(query_feat[rows], total_rows[...]) * dot_nt(here, cell_64[...])
            den_high = den.astype(BF16)
            den_low = (den - den_high.astype(F32)).astype(BF16)
            den_both = jnp.concatenate([den_high, den_low], axis=1)
            den_pair[rows] = den_both
            over = 1.0 / dot(den_both, spread[...])
            for j in range(HEADS // 2):
                at = pl.ds(j * width, width)
                num = fold(
                    dot_nt(query_feat[rows, j * 2 * FEATS : j * 2 * FEATS + FEATS], kv[at, :FEATS]),
                    dot_nt(query_feat[rows, j * 2 * FEATS + FEATS : (j + 1) * 2 * FEATS], kv[at, FEATS:]),
                    mask,
                )
                lanes = slice(j * LANES, (j + 1) * LANES)
                attended[rows, lanes] = (num * over[:, lanes]).astype(BF16)
            mixed = hidden[rows].astype(F32) + dot(attended[rows], out_w[...])
            stream[rows] = mixed
            unit, scale = moments(mixed)
            unit_two[rows] = unit.astype(BF16)
            scale_two[rows] = jnp.broadcast_to(scale, (TILE, LANES))
            normed_two[rows] = (unit * gain_two_ref[...] + shift_two_ref[...]).astype(BF16)
            return carry

        lax.fori_loop(0, tokens // TILE, attention, 0)

        for j in range(hidden_tiles):
            ff = slice(j * D, (j + 1) * D)

            def feed(t, carry):
                rows = rows_at(t, WIDE)
                x = dot(normed_two[rows], up_w[ff])
                square = x * x
                bent = jnp.tanh(x * (GELU_A + (GELU_A * GELU_B) * square))
                ramp = 0.5 + 0.5 * bent
                slope = ramp + (0.5 * x) * (1.0 - bent * bent) * (
                    GELU_A + (3.0 * GELU_A * GELU_B) * square
                )
                active = (x * ramp).astype(BF16)
                there = pl.ds(pl.multiple_of(j * tokens + t * WIDE, WIDE), WIDE)
                early_part[there] = active
                slopes[there] = slope.astype(BF16)
                stream[rows] += dot(active, down_w[ff])
                return carry

            for i in range(8 + j, matrices, hidden_tiles):
                load(i).wait()
            if j == 0:
                load(6).wait()
            lax.fori_loop(0, tokens // WIDE, feed, 0)

        slot_exchange.wait()
        load(7).wait()

        def gather(t, carry):
            rows = rows_at(t, TILE)
            slot_col = dot_nt(
                block_hot(t, TILE), jnp.broadcast_to(slot_block, (LANES, blocks)).astype(BF16)
            ) * BLK + (iota((TILE, LANES), 0) & (BLK - 1)).astype(F32)
            pick = jnp.concatenate(
                [
                    hot(slot_col == (iota((TILE, LANES), 1) + i).astype(F32)).astype(BF16)
                    for i in range(0, slots.shape[0], LANES)
                ],
                axis=1,
            )
            share = jnp.concatenate([share_col[rows]] * (D // LANES), axis=1)
            cot[rows] = (dot(pick, slots[...]) * share).astype(BF16)
            grad_att[rows] = stream[rows].astype(BF16)
            return carry

        lax.fori_loop(0, tokens // TILE, gather, 0)
        for k in list(range(1, cells)) + [0]:
            cell = lax.rem(grp + k, cells)
            pick = hot(
                slot_row[0:1] == (iota((pair_rows, tokens), 0) + cell * pair_rows).astype(F32)
            ).astype(BF16)
            here = pl.ds(pl.multiple_of(cell * pair_rows, pair_rows), pair_rows)
            slots[here] = dot(pick, grad_att[...]).astype(BF16)
            if 0 < k <= LAYER_FIRST:
                layer_exchange.start(1)
        layer_own().start()

        for j in range(hidden_tiles):
            ff = slice(j * D, (j + 1) * D)

            def feed_back(t, carry):
                rows = rows_at(t, WIDE)
                there = pl.ds(pl.multiple_of(j * tokens + t * WIDE, WIDE), WIDE)
                grad_up = (slopes[there].astype(F32) * dot_nt(cot[rows], down_w[ff])).astype(BF16)
                slopes[there] = grad_up
                back = dot_nt(grad_up, up_w[ff])
                if j == 0:
                    grad_sum[rows] = back
                else:
                    grad_sum[rows] += back
                return carry

            lax.fori_loop(0, tokens // WIDE, feed_back, 0)
            layer_exchange.start(LAYER_FEED)

        def back(t, carry):
            rows = rows_at(t, TILE)
            here = block_hot(t, TILE)
            grad_nor = grad_sum[rows]
            unit = unit_two[rows].astype(F32)
            sums[0:8] += jnp.sum((grad_nor * unit).reshape(TILE // 8, 8, D), axis=0)
            sums[8:16] += jnp.sum(grad_nor.reshape(TILE // 8, 8, D), axis=0)
            scale = jnp.concatenate([scale_two[rows]] * (D // LANES), axis=1)
            grad_mix = (
                cot[rows].astype(F32) + norm_back(grad_nor, gain_two_ref[...], unit, scale)
            ).astype(BF16)
            grad_att[rows] = grad_mix
            grad = dot_nt(grad_mix, out_w[...]) / dot(den_pair[rows], spread[...])
            grad_num[rows] = grad.astype(BF16)
            products = (grad * attended[rows].astype(F32)).astype(BF16)
            den_grad[rows] = dot_nt(products, spread[: HEADS * cells]) * dot_nt(here, cell_64[...]) * -1.0
            return carry

        lax.fori_loop(0, tokens // TILE, back, 0)

        den_rows = jnp.concatenate(
            [den_grad[...], jnp.zeros((tokens, LANES - HEADS * cells), F32)], axis=1
        ).T
        totals = []
        for j in range(HEADS // 2):
            turned = grad_num[:, j * LANES : (j + 1) * LANES].astype(F32).T
            totals += pair_sums(
                turned, cell_rows, lambda head: den_rows[head * cells : (head + 1) * cells], query_feat, j
            )
            backward_sum.tick(2 * j, 2 * j + 1)
        store_totals(totals)
        backward_sum.tick(HEADS)

        for j in range(hidden_tiles):
            down_term = dot_tn(early_part[j * tokens : (j + 1) * tokens], cot[...]).astype(BF16)
            up_term = dot_tn(normed_two[...], slopes[j * tokens : (j + 1) * tokens]).astype(BF16)
            early_part[2 * j * D : (2 * j + 1) * D] = down_term
            early_part[(2 * j + 1) * D : (2 * j + 2) * D] = up_term
            back_step()
            early_sum.tick(2 * j, 2 * j + 1)

    back_pace = list(LAYER_PACE)

    def back_step():
        backward_sum.go_on()
        early_sum.go_on_half()
        layer_exchange.start(back_pace.pop(0) if back_pace else 0)

    pl.run_scoped(
        middle,
        pltpu.VMEM((tokens, D), F32),
        pltpu.VMEM((tokens, D), F32),
        pltpu.VMEM((tokens, D), BF16),
        pltpu.VMEM((tokens, LANES), F32),
        pltpu.VMEM((hidden_tiles * tokens, D), BF16),
    )

    early_window = early_sum.go_on if EARLY_WINDOW else early_sum.go_on_half

    def end(key_feat):
        refilled(key_feat).start()
        def query_back(t, carry):
            rows = rows_at(t, TILE)
            mask = dot_nt(block_hot(t, TILE), cell_x[...])
            den = den_grad[rows].astype(BF16)
            for j in range(HEADS // 2):
                lanes = slice(j * LANES, (j + 1) * LANES)
                feats = slice(j * 2 * FEATS, (j + 1) * 2 * FEATS)
                a, b = unfold(grad_num[rows, lanes].astype(F32), mask)
                at = pl.ds(j * width, width)
                grad = jnp.concatenate([dot(a, kv[at, :FEATS]), dot(b, kv[at, FEATS:])], axis=1)
                grad += dot(den, total_rows[:, feats])
                queries[rows, lanes] = feature_back(
                    grad, query_feat[rows, feats], queries[rows, lanes]
                ).astype(BF16)
            return carry

        out_row = 2 * hidden_tiles * D
        early_part[out_row : out_row + D] = dot_tn(attended[...], grad_att[...]).astype(BF16)
        back_step()
        early_sum.tick(2 * hidden_tiles)
        lax.fori_loop(0, tokens // TILE // 2, query_back, 0)
        back_step()
        lax.fori_loop(tokens // TILE // 2, tokens // TILE, query_back, 0)
        early_part[out_row + D : out_row + 2 * D] = dot_tn(normed[...], queries[...]).astype(BF16)
        back_step()
        early_sum.tick(2 * hidden_tiles + 1)
        while backward_sum.begun():
            back_step()

        refilled(key_feat).wait()
        total_rows[...] = total_table(kt_grad)

        def key_back(t, carry):
            rows = rows_at(t, TILE)
            here = block_hot(t, TILE)
            keep = keep_col[rows]
            mask = dot_nt(here, cell_x[...]) * jnp.concatenate([keep] * (width // LANES), axis=1)
            mask_64 = (dot_nt(here, cell_64[...]) * keep[:, : HEADS * cells]).astype(BF16)
            for j in range(HEADS // 2):
                lanes = slice(j * LANES, (j + 1) * LANES)
                feats = slice(j * 2 * FEATS, (j + 1) * 2 * FEATS)
                a, b = unfold(values[rows, lanes].astype(F32), mask)
                at = pl.ds(j * width, width)
                feat = key_feat[rows, feats]
                grad = jnp.concatenate([dot(a, kv_grad[at, :FEATS]), dot(b, kv_grad[at, FEATS:])], axis=1)
                grad += dot(mask_64, total_rows[:, feats])
                keys[rows, lanes] = feature_back(grad, feat, keys[rows, lanes]).astype(BF16)
                values[rows, lanes] = fold(
                    dot_nt(feat[:, :FEATS], kv_grad[at, :FEATS]),
                    dot_nt(feat[:, FEATS:], kv_grad[at, FEATS:]),
                    mask,
                ).astype(BF16)
            return carry

        lax.fori_loop(0, tokens // TILE // 2, key_back, 0)
        early_window()
        layer_exchange.start(LAYER_LATE)
        lax.fori_loop(tokens // TILE // 2, tokens // TILE, key_back, 0)
        early_window()
        layer_exchange.start(LAYER_LATE)
        kv_part[0:D] = dot_tn(normed[...], keys[...]).astype(BF16)
        kv_part[D : 2 * D] = dot_tn(normed[...], values[...]).astype(BF16)
        late_sum.tick(0, 1, 2, 3)

        def hidden_back(t, carry):
            rows = rows_at(t, TILE)
            grad_nor = (
                dot_nt(queries[rows], query_w[...])
                + dot_nt(keys[rows], key_w[...])
                + dot_nt(values[rows], value_w[...])
            )
            unit, scale = moments(hidden[rows].astype(F32))
            sums[16:24] += jnp.sum((grad_nor * unit).reshape(TILE // 8, 8, D), axis=0)
            sums[24:32] += jnp.sum(grad_nor.reshape(TILE // 8, 8, D), axis=0)
            cot[rows] = (
                grad_att[rows].astype(F32) + norm_back(grad_nor, gain_one_ref[...], unit, scale)
            ).astype(BF16)
            return carry

        lax.fori_loop(0, tokens // TILE, hidden_back, 0)
        early_window()
        late_sum.tick(0, 1, 2, 3)
        kv_part[2 * D : 2 * D + D_IN] = dot_tn(enc[...], cot[...]).astype(BF16)
        small = jnp.concatenate(
            [jnp.sum(sums[8 * i : 8 * i + 8], axis=0, keepdims=True) for i in range(4)]
            + [jnp.zeros((12, D), F32)],
            axis=0,
        )
        at = 2 * D + D_IN
        kv_part[at : at + 16] = small.astype(BF16)
        kv_part[at + 16 :] = jnp.zeros((kv_part.shape[0] - at - 16, D), BF16)
        late_sum.tick(4, 5, 6, 7)
        early_window()
        layer_exchange.start(LAYER_LATE)

        def encoder_grad(t, carry):
            rows = rows_at(t, TILE)
            enc[rows] = dot_nt(cot[rows], in_w[...]).astype(BF16)
            return carry

        lax.fori_loop(0, tokens // TILE, encoder_grad, 0)
        enc_copy = pltpu.make_async_copy(enc, enc_grad_hbm, copy_sem.at[3])
        enc_copy.start()
        while late_sum.begun():
            late_sum.go_on()
            early_sum.go_on_half()
            layer_exchange.start(LAYER_LATE)
        early_sum.run()
        ends = []
        for i, (at, rows, target) in enumerate(
            (
                (0, D, key_sum_hbm),
                (D, D, value_sum_hbm),
                (2 * D, D_IN, in_sum_hbm),
                (2 * D + D_IN, 16, small_sum_hbm),
            )
        ):
            ends.append(pltpu.make_async_copy(kv.at[pl.ds(at, rows)], target, copy_sem.at[4 + i]))
            ends[-1].start()
        layer_exchange.wait()
        layer_own().wait()
        enc_copy.wait()
        for copy in ends:
            copy.wait()

    pl.run_scoped(end, pltpu.VMEM((tokens, HEADS * FEATS), BF16))


def fused(
    mesh,
    encoded,
    destination,
    expressed,
    in_proj,
    gain_one,
    shift_one,
    query_w,
    key_w,
    value_w,
    out_w,
    gain_two,
    shift_two,
    up_w,
    down_w,
    random_features,
    out_cotangent,
):
    sizes = {"grp": mesh.shape["grp"], "seq": mesh.shape["seq"]}
    cells, splits, blocks = destination.shape
    tokens = encoded.shape[2]
    slot_total = out_cotangent.shape[2]
    cap = slot_total // (cells * BLK)
    width = cells * DH
    digits = digits_of(sizes)
    unit = 16 * sizes["grp"] * sizes["seq"]
    steps = 2 * sum(radix - 1 for _, _, radix in digits)
    early = 2 * FF + 2 * D
    half = HEADS // 2 * width
    count = HEADS + 1 + early // unit

    def vmem(shape, kind=BF16):
        return pltpu.VMEM(shape, kind)

    def shape(*dims):
        return jax.ShapeDtypeStruct(dims, BF16)

    rest = pl.BlockSpec(memory_space=pl.ANY)
    results = pl.pallas_call(
        functools.partial(fused_kernel, sizes, cap),
        out_shape=(
            shape(slot_total, D),
            shape(tokens, D_IN),
            shape(D_IN, D),
            shape(D, D),
            shape(D, D),
            shape(D, D),
            shape(D, D),
            shape(D, FF),
            shape(FF, D),
            shape(16, D),
            shape(tokens, HEADS * FEATS),
        ),
        in_specs=[rest] * 16,
        out_specs=(rest,) * 11,
        scratch_shapes=[
            vmem(destination.shape, jnp.int32),
            vmem(expressed.shape, jnp.int32),
            vmem((1, D), F32),
            vmem((1, D), F32),
            vmem((1, D), F32),
            vmem((1, D), F32),
            vmem((DH, FEATS)),
            vmem((tokens, D_IN)),
            vmem((D_IN, D)),
            vmem((D, D)),
            vmem((D, D)),
            vmem((D, D)),
            vmem((D, D)),
            vmem((FF, D)),
            vmem((FF, D)),
            vmem((slot_total, D)),
            vmem((tokens, D)),
            vmem((tokens, D)),
            vmem((tokens, D)),
            vmem((tokens, D)),
            vmem((tokens, D)),
            vmem((tokens, D)),
            vmem((tokens, HEADS * FEATS)),
            vmem((half, 2 * FEATS)),
            vmem((half, 2 * FEATS)),
            vmem((half, 2 * FEATS)),
            vmem((half, 2 * FEATS)),
            vmem((unit, LANES)),
            vmem((unit, LANES)),
            vmem((unit, LANES)),
            vmem((unit, LANES)),
            vmem((tokens, D)),
            vmem((tokens, D)),
            vmem((tokens, D)),
            vmem((tokens, D)),
            vmem((tokens, 2 * HEADS * cells)),
            vmem((tokens, HEADS * cells), F32),
            vmem((early, D)),
            vmem((early, D)),
            vmem((early // unit * 16, D)),
            vmem((4 * DH, 2 * FEATS)),
            vmem((width, blocks)),
            vmem((HEADS * cells, blocks)),
            vmem((tokens, LANES), F32),
            vmem((tokens, LANES), F32),
            vmem((8, tokens), F32),
            vmem((HEADS * cells, HEADS * FEATS)),
            vmem((2 * HEADS * cells, D)),
            vmem((32, D), F32),
            pltpu.SemaphoreType.DMA((15 + FF // D,)),
            pltpu.SemaphoreType.DMA((PARTS * (cells - 1),)),
            pltpu.SemaphoreType.DMA((PARTS * (cells - 1),)),
            pltpu.SemaphoreType.DMA((PARTS * (cells - 1),)),
            pltpu.SemaphoreType.DMA((PARTS * (cells - 1),)),
            pltpu.SemaphoreType.DMA((8,)),
            pltpu.SemaphoreType.DMA((early // unit,)),
            pltpu.SemaphoreType.DMA((count * steps,)),
            pltpu.SemaphoreType.DMA((count * steps,)),
        ],
        compiler_params=pltpu.CompilerParams(
            collective_id=1, has_side_effects=True, vmem_limit_bytes=VMEM_LIMIT
        ),
        name="layer_and_gradients",
    )(
        destination,
        expressed,
        gain_one.reshape(1, D),
        shift_one.reshape(1, D),
        gain_two.reshape(1, D),
        shift_two.reshape(1, D),
        random_features,
        encoded.reshape(tokens, D_IN),
        in_proj,
        query_w,
        key_w,
        value_w,
        out_w,
        up_w,
        down_w,
        out_cotangent.reshape(slot_total, D),
    )
    layer, enc_grad, in_b, query_b, key_b, value_b, out_b, up_b, down_b, small_b = results[:10]
    small = small_b.astype(F32)
    return (
        layer.astype(F32).reshape(1, 1, slot_total, D),
        enc_grad.reshape(1, 1, tokens, D_IN),
        in_b.astype(F32),
        small[2],
        small[3],
        query_b.astype(F32),
        key_b.astype(F32),
        value_b.astype(F32),
        out_b.astype(F32),
        small[0],
        small[1],
        up_b.astype(F32),
        down_b.astype(F32),
    )


def layer_norm(values, gain, shift):
    center = values - jnp.mean(values, axis=-1, keepdims=True)
    variance = jnp.mean(center * center, axis=-1, keepdims=True)
    return center * lax.rsqrt(variance + 1e-05) * gain + shift


def feature_map(projected, omega_b, key_keep):
    row_count = projected.shape[0]
    pieces = projected.reshape(row_count, HEADS, DH)
    factor = DH ** (-0.25)
    logits = jnp.einsum("nhd,dm->nhm", pieces, omega_b, preferred_element_type=jnp.float32) * factor
    squares = (
        0.5
        * factor
        * factor
        * jnp.sum(jnp.square(pieces.astype(jnp.float32)), axis=-1, keepdims=True)
    )
    return jnp.exp(logits - squares) * FEATS ** (-0.5) * key_keep[:, None, None]


def feature_grad(grad_feat, feat_full, projected, omega_b):
    row_count = projected.shape[0]
    factor = DH ** (-0.25)
    scaled = grad_feat.astype(jnp.float32) * feat_full
    logit_grad = scaled.astype(jnp.bfloat16)
    pieces = projected.reshape(row_count, HEADS, DH).astype(jnp.float32)
    through = (
        jnp.einsum("nhm,dm->nhd", logit_grad, omega_b, preferred_element_type=jnp.float32) * factor
    )
    direct = pieces * (factor * factor) * jnp.sum(scaled, axis=-1, keepdims=True)
    return (through - direct).reshape(row_count, HEADS * DH).astype(jnp.bfloat16)


def weight_term(left, right):
    return jnp.einsum("nk,nd->kd", left, right, preferred_element_type=jnp.float32)


def plain(
    encoded,
    destination,
    expressed,
    in_proj,
    gain_one,
    shift_one,
    query_w,
    key_w,
    value_w,
    out_w,
    gain_two,
    shift_two,
    up_w,
    down_w,
    random_features,
    out_cotangent,
):
    cell_count = destination.shape[0]
    split_count = destination.shape[1]
    blocks = destination.shape[2]
    tokens = encoded.shape[2]
    block_len = tokens // blocks
    row_total = out_cotangent.shape[2]
    slot_count = row_total // (cell_count * block_len)
    pair_rows = slot_count * block_len
    group_index = lax.axis_index("grp")
    split_index = lax.axis_index("seq")
    targets = jnp.arange(cell_count, dtype=jnp.int32)
    slot_ids = jnp.arange(slot_count, dtype=jnp.int32)
    within = jnp.arange(block_len, dtype=jnp.int32)
    block_ids = jnp.arange(blocks, dtype=jnp.int32)
    column = lax.dynamic_index_in_dim(destination, split_index, 1, keepdims=False)
    block_hits = (column[:, :, None] == targets).astype(jnp.int32)
    block_rank = jnp.sum(jnp.cumsum(block_hits, axis=1) * block_hits, axis=2) - 1
    own_dest = lax.dynamic_index_in_dim(column, group_index, 0, keepdims=False)
    own_rank = lax.dynamic_index_in_dim(block_rank, group_index, 0, keepdims=False)
    send_match = (
        (own_dest[:, None, None] == targets[:, None]) & (own_rank[:, None, None] == slot_ids)
    ).astype(jnp.int32)
    send_found = jnp.sum(send_match, axis=0)
    send_block = jnp.sum(send_match * block_ids[:, None, None], axis=0)
    send_index = (send_block[:, :, None] * block_len + within).reshape(-1)
    send_keep = jnp.repeat(send_found.reshape(-1), block_len).astype(jnp.bfloat16)
    back_index = ((own_dest * slot_count + own_rank)[:, None] * block_len + within).reshape(-1)
    recv_match = (
        (column[:, :, None] == group_index) & (block_rank[:, :, None] == slot_ids)
    ).astype(jnp.int32)
    recv_found = jnp.sum(recv_match, axis=1)
    recv_block = jnp.sum(recv_match * block_ids[:, None], axis=1)
    recv_token = (recv_block[:, :, None] * block_len + within).reshape(cell_count, pair_rows)
    expressed_col = lax.dynamic_index_in_dim(expressed, split_index, 1, keepdims=False)
    valid = jnp.repeat(recv_found.reshape(-1), block_len).astype(jnp.float32)
    key_keep = (
        jnp.take_along_axis(expressed_col, recv_token, axis=1).reshape(-1).astype(jnp.float32)
        * valid
    )
    block_sum = jnp.sum(expressed.reshape(cell_count, split_count, blocks, block_len), axis=3)
    dest_hits = destination[..., None] == targets
    counts = jnp.sum(jnp.where(dest_hits, block_sum[..., None], 0), axis=(0, 1, 2)).astype(
        jnp.float32
    )
    own_count = lax.dynamic_index_in_dim(counts, group_index, 0, keepdims=False)
    share = cell_count * own_count / jnp.sum(counts)
    token_rows = encoded.reshape(tokens, D_IN)
    token_hidden = jnp.dot(token_rows, in_proj, preferred_element_type=jnp.float32).astype(
        jnp.bfloat16
    )
    outgoing = jnp.take(token_hidden, send_index, axis=0) * send_keep[:, None]
    hidden_b = lax.all_to_all(
        outgoing.reshape(cell_count, pair_rows, D),
        "grp",
        split_axis=0,
        concat_axis=0,
        tiled=True,
    ).reshape(row_total, D)
    hidden_f = hidden_b.astype(jnp.float32)
    normed_f, norm_one_pull = jax.vjp(layer_norm, hidden_f, gain_one, shift_one)
    normed_b = normed_f.astype(jnp.bfloat16)
    queries_b = jnp.dot(normed_b, query_w, preferred_element_type=jnp.float32).astype(jnp.bfloat16)
    keys_b = jnp.dot(normed_b, key_w, preferred_element_type=jnp.float32).astype(jnp.bfloat16)
    values_b = jnp.dot(normed_b, value_w, preferred_element_type=jnp.float32).astype(jnp.bfloat16)
    query_full = feature_map(queries_b, random_features, jnp.ones((row_total,), jnp.float32))
    key_full = feature_map(keys_b, random_features, key_keep)
    query_feature_rows = query_full.astype(jnp.bfloat16)
    key_feature_rows = key_full.astype(jnp.bfloat16)
    value_per_head = values_b.reshape(row_total, HEADS, DH)
    value_part = jnp.einsum(
        "pgk,pgz->gkz", key_feature_rows, value_per_head, preferred_element_type=jnp.float32
    )
    total_part = jnp.sum(key_feature_rows, axis=0, dtype=jnp.float32)
    key_value_products, key_total = lax.psum((value_part, total_part), "seq")
    key_value_batched = key_value_products.astype(jnp.bfloat16)
    attention_numerator = jnp.einsum(
        "bli,lie->ble", query_feature_rows, key_value_batched, preferred_element_type=jnp.float32
    )
    denominator = jnp.sum(query_feature_rows.astype(jnp.float32) * key_total[None], axis=-1)
    attended_b = (
        (attention_numerator / denominator[:, :, None]).reshape(row_total, D).astype(jnp.bfloat16)
    )
    mixed = hidden_f + jnp.dot(attended_b, out_w, preferred_element_type=jnp.float32)
    normed_two_f, norm_two_pull = jax.vjp(layer_norm, mixed, gain_two, shift_two)
    normed_two_b = normed_two_f.astype(jnp.bfloat16)
    expanded = jnp.dot(normed_two_b, up_w, preferred_element_type=jnp.float32)
    activated_f, gelu_pull = jax.vjp(partial_gelu, expanded)
    activated_b = activated_f.astype(jnp.bfloat16)
    layer_out = (mixed + jnp.dot(activated_b, down_w, preferred_element_type=jnp.float32)) * valid[
        :, None
    ]
    grad_out = out_cotangent.reshape(row_total, D).astype(jnp.float32) * (valid * share)[:, None]
    grad_mlp = grad_out.astype(jnp.bfloat16)
    down_term = weight_term(activated_b, grad_mlp)
    grad_activated = jnp.dot(grad_mlp, down_w.T, preferred_element_type=jnp.float32)
    grad_up = gelu_pull(grad_activated)[0].astype(jnp.bfloat16)
    up_term = weight_term(normed_two_b, grad_up)
    grad_normed_two = jnp.dot(grad_up, up_w.T, preferred_element_type=jnp.float32)
    mixed_back, gain_two_term, shift_two_term = norm_two_pull(grad_normed_two)
    grad_mixed = grad_out + mixed_back
    grad_att = grad_mixed.astype(jnp.bfloat16)
    out_term = weight_term(attended_b, grad_att)
    grad_attended = jnp.dot(grad_att, out_w.T, preferred_element_type=jnp.float32).reshape(
        row_total, HEADS, DH
    )
    numerator_gradient = (grad_attended / denominator[:, :, None]).astype(jnp.bfloat16)
    grad_den = -jnp.sum(grad_attended * attention_numerator, axis=-1) / (denominator * denominator)
    value_grad_part = jnp.einsum(
        "pgk,pgz->gkz", query_feature_rows, numerator_gradient, preferred_element_type=jnp.float32
    )
    total_grad_part = jnp.sum(query_feature_rows.astype(jnp.float32) * grad_den[:, :, None], axis=0)
    grad_query_feat = (
        jnp.einsum(
            "pao,ajo->paj",
            numerator_gradient,
            key_value_batched,
            preferred_element_type=jnp.float32,
        )
        + grad_den[:, :, None] * key_total[None]
    ).astype(jnp.bfloat16)
    grad_kv, grad_total = lax.psum((value_grad_part, total_grad_part), "seq")
    key_value_gradient_batched = grad_kv.astype(jnp.bfloat16)
    grad_key_feat = (
        jnp.einsum(
            "pao,ajo->paj",
            value_per_head,
            key_value_gradient_batched,
            preferred_element_type=jnp.float32,
        )
        + grad_total[None]
    ).astype(jnp.bfloat16)
    grad_values = (
        jnp.einsum(
            "bli,lie->ble",
            key_feature_rows,
            key_value_gradient_batched,
            preferred_element_type=jnp.float32,
        )
        .reshape(row_total, D)
        .astype(jnp.bfloat16)
    )
    grad_queries = feature_grad(grad_query_feat, query_full, queries_b, random_features)
    grad_keys = feature_grad(grad_key_feat, key_full, keys_b, random_features)
    query_term = weight_term(normed_b, grad_queries)
    key_term = weight_term(normed_b, grad_keys)
    value_term = weight_term(normed_b, grad_values)
    grad_normed = jnp.dot(grad_queries, query_w.T, preferred_element_type=jnp.float32)
    grad_normed = grad_normed + jnp.dot(grad_keys, key_w.T, preferred_element_type=jnp.float32)
    grad_normed = grad_normed + jnp.dot(grad_values, value_w.T, preferred_element_type=jnp.float32)
    hidden_back, gain_one_term, shift_one_term = norm_one_pull(grad_normed)
    grad_hidden = (grad_mixed + hidden_back).astype(jnp.bfloat16)
    returned = lax.all_to_all(
        grad_hidden.reshape(cell_count, pair_rows, D),
        "grp",
        split_axis=0,
        concat_axis=0,
        tiled=True,
    )
    token_grad = jnp.take(returned.reshape(row_total, D), back_index, axis=0)
    encoded_grad = jnp.dot(token_grad, in_proj.T, preferred_element_type=jnp.float32).astype(
        jnp.bfloat16
    )
    in_term = weight_term(token_rows, token_grad)
    (
        in_sum,
        query_sum,
        key_sum,
        value_sum,
        out_sum,
        up_sum,
        down_sum,
        gain_one_sum,
        shift_one_sum,
        gain_two_sum,
        shift_two_sum,
    ) = lax.psum(
        (
            in_term,
            query_term,
            key_term,
            value_term,
            out_term,
            up_term,
            down_term,
            gain_one_term,
            shift_one_term,
            gain_two_term,
            shift_two_term,
        ),
        ("grp", "seq"),
    )
    return (
        layer_out.reshape(1, 1, row_total, D),
        encoded_grad.reshape(1, 1, tokens, D_IN),
        in_sum,
        gain_one_sum,
        shift_one_sum,
        query_sum,
        key_sum,
        value_sum,
        out_sum,
        gain_two_sum,
        shift_two_sum,
        up_sum,
        down_sum,
    )


def partial_gelu(values):
    return jax.nn.gelu(values, approximate=True)


def solution(mesh):
    in_specs = (
        P("grp", "seq", None, None),
        P(),
        P(),
        P(),
        P(),
        P(),
        P(),
        P(),
        P(),
        P(),
        P(),
        P(),
        P(),
        P(),
        P(),
        P("grp", "seq", None, None),
    )
    out_specs = (
        P("grp", "seq", None, None),
        P("grp", "seq", None, None),
        P(),
        P(),
        P(),
        P(),
        P(),
        P(),
        P(),
        P(),
        P(),
        P(),
        P(),
    )
    body = functools.partial(fused, mesh) if mesh.shape["grp"] <= FUSED_CELLS else plain
    return jax.shard_map(body, mesh=mesh, in_specs=in_specs, out_specs=out_specs, check_vma=False)
```

```python
import functools

import jax
import jax.numpy as jnp
from jax import lax
from jax.experimental import pallas as pl
from jax.experimental.pallas import tpu as pltpu
from jax.sharding import PartitionSpec as P

D_IN = 768
D = 512
HEADS = 8
DH = 64
FEATS = 256
FF = 2048
BLK = 8
LANES = 128
TILE = 256
WIDE = 512
PARTS = 4
WIDEN_DEPTH = 8
SLOTS_FIRST = 8
SLOTS_PACE = (4, 3, 1, 0, 0, 0, 0, 2, 4, 4)
LAYER_FIRST = 4
LAYER_FEED = 4
LAYER_PACE = (1, 1, 1, 0, 0, 0, 1, 1, 1, 1)
LAYER_LATE = 2
KV_ORDERS = (0, 1, 0)
EARLY_ORDERS = (0, 1)
EARLY_WINDOW = False
LATE_ORDERS = (0, 1)
FUSED_CELLS = 8
VMEM_LIMIT = 62 << 20
LOG2E = 1.4426950408889634
GELU_A = 0.7978845608028654
GELU_B = 0.044715
F32, BF16 = jnp.float32, jnp.bfloat16
MESH = pl.DeviceIdType.MESH


def dot(a, b):
    return jnp.dot(a, b, preferred_element_type=F32)


def dot_nt(a, b):
    return lax.dot_general(a, b, (((1,), (1,)), ((), ())), preferred_element_type=F32)


def dot_tn(a, b):
    return lax.dot_general(a, b, (((0,), (0,)), ((), ())), preferred_element_type=F32)


def iota(shape, axis):
    return lax.broadcasted_iota(jnp.int32, shape, axis)


def hot(condition):
    return jnp.where(condition, 1.0, 0.0)


def moments(x):
    center = x - jnp.mean(x, axis=-1, keepdims=True)
    scale = lax.rsqrt(jnp.mean(center * center, axis=-1, keepdims=True) + 1e-05)
    return center * scale, scale


def norm_back(grad, gain, unit, scale):
    inner = grad * gain
    return scale * (
        inner
        - jnp.mean(inner, axis=-1, keepdims=True)
        - unit * jnp.mean(inner * unit, axis=-1, keepdims=True)
    )


def digits_of(sizes):
    digits = []
    for axis in ("seq", "grp"):
        if sizes[axis] > 1:
            digits.append((axis, 1, 2))
        step = 2
        while step < sizes[axis]:
            digits.append((axis, step, 2))
            step *= 2
    return digits


def peers(digit):
    grp, seq = lax.axis_index("grp"), lax.axis_index("seq")
    axis, step, radix = digit
    index = seq if axis == "seq" else grp
    value = (index // step) % radix
    found = []
    for m in range(1, radix):
        other = index + ((value + m) % radix - value) * step
        found.append((grp, other) if axis == "seq" else (other, seq))
    return value, found


def digit_orders(digits):
    first, second = list(digits), list(digits)
    if len(digits) > 2:
        second[1], second[2] = second[2], second[1]
    return first, second


class Sum:
    def __init__(self, digits, pieces, pattern, send, recv, base, settle=None):
        self.pieces, self.send, self.recv, self.base, self.settle = pieces, send, recv, base, settle
        self.half_steps, self.steps = len(digits), 2 * len(digits)
        self.copies = 2 * sum(radix - 1 for _, _, radix in digits)
        self.step = [-1] * len(pieces)
        self.turn = 0
        self.plans = []
        orders = digit_orders(digits)
        for c, piece in enumerate(pieces):
            at, rows, inbox_at, sem = 0, piece[6], piece[3], base + c * self.copies
            plan, kept = [], []
            for digit in orders[pattern[c % len(pattern)]]:
                value, found = peers(digit)
                radix = digit[2]
                rows //= radix
                keep = at + value * rows
                moves = []
                for m, device in enumerate(found, 1):
                    moves.append((device, at + (value + m) % radix * rows, inbox_at, sem))
                    inbox_at += rows
                    sem += 1
                kept.append((found, keep, rows))
                plan.append((moves, keep, rows))
                at = keep
            for found, keep, rows in reversed(kept):
                moves = [(device, keep, None, sem + m) for m, device in enumerate(found)]
                sem += len(found)
                plan.append((moves, keep, rows))
            self.plans.append(plan)

    def transfers(self, c, k):
        part, start, inbox, _, total, total_at, _, own = self.pieces[c]
        moves, _, rows = self.plans[c][k]
        found = []
        for device, at, inbox_at, sem in moves:
            if k < self.half_steps:
                source = part.at[pl.ds(pl.multiple_of(start + at, 16), rows)]
                target = inbox.at[pl.ds(inbox_at, rows)]
            else:
                target = total.at[pl.ds(pl.multiple_of(total_at + at, 16), rows)]
                source = target if own is None or k > self.half_steps else own
            found.append(
                pltpu.make_async_remote_copy(
                    src_ref=source,
                    dst_ref=target,
                    send_sem=self.send.at[sem],
                    recv_sem=self.recv.at[sem],
                    device_id=device,
                    device_id_type=MESH,
                )
            )
        return found

    def settled(self, c):
        _, _, _, _, total, total_at, _, own = self.pieces[c]
        _, at, rows = self.plans[c][self.half_steps]
        target = total.at[pl.ds(pl.multiple_of(total_at + at, 16), rows)]
        return pltpu.make_async_copy(own, target, self.settle.at[c])

    def finish(self, c):
        k = self.step[c]
        part, start, inbox, _, total, total_at, _, own = self.pieces[c]
        for transfer in self.transfers(c, k):
            transfer.wait()
        if k == self.half_steps and own is not None:
            self.settled(c).wait()
        if k >= self.half_steps:
            return
        moves, keep, rows = self.plans[c][k]
        step = min(rows, 256)
        last = k == self.half_steps - 1

        def add(i, carry):
            here = pl.ds(pl.multiple_of(start + keep + i * step, 16), step)
            value = part[here].astype(F32)
            for _, _, inbox_at, _ in moves:
                value += inbox[pl.ds(pl.multiple_of(inbox_at + i * step, 16), step)].astype(F32)
            value = value.astype(BF16)
            if not last:
                part[here] = value
            elif own is None:
                total[pl.ds(pl.multiple_of(total_at + keep + i * step, 16), step)] = value
            else:
                own[...] = value
            return carry

        if rows == step:
            add(0, 0)
        else:
            lax.fori_loop(0, rows // step, add, 0)
        if last and own is not None:
            self.settled(c).start()

    def tick(self, *which):
        for c in which:
            if self.step[c] >= 0:
                self.finish(c)
            self.step[c] += 1
            if self.step[c] < self.steps:
                for transfer in self.transfers(c, self.step[c]):
                    transfer.start()

    def begun(self):
        return [c for c in range(len(self.pieces)) if 0 <= self.step[c] < self.steps]

    def go_on(self):
        self.tick(*self.begun())

    def go_on_half(self):
        self.turn += 1
        self.tick(*[c for c in self.begun() if (c // 2 + self.turn) % 2])

    def run(self):
        while self.begun():
            self.go_on()


class Exchange:
    def __init__(self, makers):
        self.makers, self.started = makers, 0

    def start(self, count):
        for make in self.makers[self.started : self.started + count]:
            make().start()
        self.started = min(self.started + count, len(self.makers))

    def wait(self):
        self.start(len(self.makers))
        for make in self.makers:
            make().wait()


def fused_kernel(
    sizes,
    cap,
    dest_hbm,
    expr_hbm,
    gain_one_hbm,
    shift_one_hbm,
    gain_two_hbm,
    shift_two_hbm,
    omega_hbm,
    enc_hbm,
    in_hbm,
    query_hbm,
    key_hbm,
    value_hbm,
    out_hbm,
    up_hbm,
    down_hbm,
    cot_hbm,
    layer_hbm,
    enc_grad_hbm,
    in_sum_hbm,
    query_sum_hbm,
    key_sum_hbm,
    value_sum_hbm,
    out_sum_hbm,
    up_sum_hbm,
    down_sum_hbm,
    small_sum_hbm,
    dest_ref,
    expr_ref,
    gain_one_ref,
    shift_one_ref,
    gain_two_ref,
    shift_two_ref,
    omega_ref,
    enc,
    in_w,
    query_w,
    key_w,
    value_w,
    out_w,
    up_w,
    down_w,
    slots,
    cot,
    hidden,
    normed,
    queries,
    keys,
    values,
    query_feat,
    kv_part,
    kv_inbox,
    kv,
    kv_grad,
    kt_part,
    kt_inbox,
    kt,
    kt_grad,
    attended,
    normed_two,
    grad_att,
    grad_num,
    den_pair,
    den_grad,
    early_part,
    early_inbox,
    early_own,
    feat_w,
    cell_x,
    cell_64,
    keep_col,
    share_col,
    slot_row,
    total_rows,
    spread,
    sums,
    load_sem,
    slot_send,
    slot_recv,
    layer_send,
    layer_recv,
    copy_sem,
    settle_sem,
    sum_send,
    sum_recv,
):
    grp, seq = lax.axis_index("grp"), lax.axis_index("seq")
    cells = sizes["grp"]
    digits = digits_of(sizes)
    tokens = enc.shape[0]
    blocks = dest_ref.shape[2]
    width = cells * DH
    pair_rows = slots.shape[0] // cells
    unit_rows = 16 * sizes["grp"] * sizes["seq"]
    factor = DH ** (-0.25)
    hidden_tiles = FF // D

    own_slots = pl.ds(pl.multiple_of(grp * pair_rows, pair_rows), pair_rows)
    sources = [
        (enc_hbm, enc),
        (in_hbm, in_w),
        (key_hbm, key_w),
        (value_hbm, value_w),
        (query_hbm, query_w),
        (out_hbm, out_w),
        (down_hbm, down_w),
        (cot_hbm.at[own_slots], slots.at[own_slots]),
    ]
    sources += [(up_hbm.at[:, pl.ds(j * D, D)], up_w.at[pl.ds(j * D, D)]) for j in range(hidden_tiles)]

    def load(i):
        return pltpu.make_async_copy(*sources[i], load_sem.at[i])

    matrices = len(sources)
    sources += [
        (dest_hbm, dest_ref),
        (expr_hbm, expr_ref),
        (omega_hbm, omega_ref),
        (gain_one_hbm, gain_one_ref),
        (shift_one_hbm, shift_one_ref),
        (gain_two_hbm, gain_two_ref),
        (shift_two_hbm, shift_two_ref),
    ]
    for i in list(range(matrices, len(sources))) + list(range(matrices)):
        load(i).start()

    barrier = pltpu.get_barrier_semaphore()
    others = [(lax.rem(grp + k, cells), seq) for k in range(1, cells)]
    mates = [device for digit in digits if digit[0] == "seq" for device in peers(digit)[1]]
    for device in others + mates:
        pl.semaphore_signal(barrier, inc=1, device_id=device, device_id_type=MESH)

    part_rows = pair_rows // PARTS

    def slot_copy(k, i):
        theirs = pl.multiple_of(others[k][0] * pair_rows + i * part_rows, part_rows)
        ours = pl.multiple_of(grp * pair_rows + i * part_rows, part_rows)
        return pltpu.make_async_remote_copy(
            src_ref=cot_hbm.at[pl.ds(theirs, part_rows)],
            dst_ref=slots.at[pl.ds(ours, part_rows)],
            send_sem=slot_send.at[k * PARTS + i],
            recv_sem=slot_recv.at[k * PARTS + i],
            device_id=others[k],
            device_id_type=MESH,
        )

    def layer_copy(k, i):
        theirs = pl.multiple_of(others[k][0] * pair_rows + i * part_rows, part_rows)
        ours = pl.multiple_of(grp * pair_rows + i * part_rows, part_rows)
        return pltpu.make_async_remote_copy(
            src_ref=slots.at[pl.ds(theirs, part_rows)],
            dst_ref=layer_hbm.at[pl.ds(ours, part_rows)],
            send_sem=layer_send.at[k * PARTS + i],
            recv_sem=layer_recv.at[k * PARTS + i],
            device_id=others[k],
            device_id_type=MESH,
        )

    order = [(k, i) for i in range(PARTS) for k in range(cells - 1)]
    slot_exchange = Exchange([functools.partial(slot_copy, k, i) for k, i in order])
    layer_exchange = Exchange([functools.partial(layer_copy, k, i) for k, i in order])

    def columns(ref, i):
        return ref.at[:, pl.ds(i * FEATS, FEATS)]

    def kv_pieces(total, rows):
        return [
            (columns(kv_part, i), at, columns(kv_inbox, i), at, columns(total, i), at, rows, None)
            for at in range(0, kv.shape[0], rows)
            for i in range(2)
        ]

    def kt_piece(total):
        return [(kt_part, 0, kt_inbox, 0, total, 0, kt_part.shape[0], None)]

    forward_sum = Sum(
        digits, kv_pieces(kv, width) + kt_piece(kt), KV_ORDERS, sum_send, sum_recv, 0
    )
    backward_sum = Sum(
        digits, kv_pieces(kv_grad, width) + kt_piece(kt_grad), KV_ORDERS, sum_send, sum_recv, 0
    )
    late_sum = Sum(digits, kv_pieces(kv, unit_rows), LATE_ORDERS, sum_send, sum_recv, 0)
    early_totals = []
    for j in range(hidden_tiles):
        early_totals.append((down_sum_hbm, j * D))
        early_totals.append((up_sum_hbm.at[:, pl.ds(j * D, D)], 0))
    early_totals += [(out_sum_hbm, 0), (query_sum_hbm, 0)]
    early_sum = Sum(
        digits,
        [
            (early_part, c * D, early_inbox, c * D, total, at, D, early_own.at[pl.ds(c * 16, 16)])
            for c, (total, at) in enumerate(early_totals)
        ],
        EARLY_ORDERS,
        sum_send,
        sum_recv,
        forward_sum.copies * len(forward_sum.pieces),
        settle_sem,
    )
    for i in range(matrices, len(sources)):
        load(i).wait()

    own = dest_ref[grp, pl.ds(seq, 1), :]
    cell_hot = hot(iota((cells, blocks), 0) == own)
    block_of = hot(iota((blocks, tokens), 1) >> 3 == iota((blocks, tokens), 0)).astype(BF16)
    expressed = expr_ref[grp, pl.ds(seq, 1), :].astype(F32)
    cell_rows = dot(cell_hot.astype(BF16), block_of)
    keep_rows = cell_rows * expressed
    kt_part[...] = jnp.zeros_like(kt_part)
    omega = omega_ref[...]
    zero = jnp.zeros_like(omega)
    one = jnp.ones_like(omega)
    feat_w[...] = jnp.concatenate(
        [
            jnp.concatenate([omega, zero], axis=1),
            jnp.concatenate([zero, omega], axis=1),
            jnp.concatenate([-one, zero], axis=1),
            jnp.concatenate([zero, -one], axis=1),
        ],
        axis=0,
    )

    def tables():
        cell_x[...] = hot(iota((width, blocks), 0) >> 6 == own).astype(BF16)
        cell_64[...] = hot((iota((HEADS * cells, blocks), 0) & (cells - 1)) == own).astype(BF16)
        earlier = hot(iota((blocks, blocks), 0) < iota((blocks, blocks), 1)).astype(BF16)
        rank = jnp.sum(dot(cell_hot.astype(BF16), earlier) * cell_hot, axis=0, keepdims=True)
        slot_block = own.astype(F32) * cap + rank
        slot_row[...] = dot(jnp.broadcast_to(slot_block, (8, blocks)).astype(BF16), block_of) * BLK + (
            iota((8, tokens), 1) & (BLK - 1)
        ).astype(F32)
        keep_col[...] = jnp.broadcast_to(expressed, (LANES, tokens)).T
        sums[...] = jnp.zeros_like(sums)
        counted = [jnp.zeros(dest_ref.shape[1:], F32) for _ in range(cells)]
        whole = jnp.zeros(dest_ref.shape[1:], F32)
        for g in range(dest_ref.shape[0]):
            block_sum = dot_nt(expr_ref[g].astype(F32).astype(BF16), block_of)
            whole += block_sum
            for c in range(cells):
                counted[c] += jnp.where(dest_ref[g] == c, block_sum, 0.0)
        share = jnp.zeros((1, blocks), F32)
        for c in range(cells):
            share += jnp.where(own == c, jnp.sum(counted[c], keepdims=True), 0.0)
        share = share * cells / jnp.sum(whole, keepdims=True)
        share_col[...] = lax.dot_general(
            hot(iota((tokens, blocks), 0) >> 3 == iota((tokens, blocks), 1)),
            jnp.broadcast_to(share, (LANES, blocks)),
            (((1,), (1,)), ((), ())),
            precision=lax.Precision.HIGHEST,
            preferred_element_type=F32,
        )
        head_lanes = iota((HEADS * cells * 2, D), 1) >> 6
        spread[...] = hot(
            (iota((HEADS * cells * 2, D), 0) & (HEADS * cells - 1)) >> cells.bit_length() - 1 == head_lanes
        ).astype(BF16)
        return slot_block

    def rows_at(t, tile):
        return pl.ds(pl.multiple_of(t * tile, tile), tile)

    def block_hot(t, tile):
        return hot((iota((tile, blocks), 0) + t * tile) >> 3 == iota((tile, blocks), 1)).astype(BF16)

    def fold(a, b, mask):
        left = iota((a.shape[0], LANES), 1) < DH
        a, b = a * mask, b * mask
        sum_a = sum(a[:, i : i + LANES] for i in range(0, width, LANES))
        sum_b = sum(b[:, i : i + LANES] for i in range(0, width, LANES))
        return jnp.where(left, sum_a, sum_b) + pltpu.roll(jnp.where(left, sum_b, sum_a), DH, 1)

    def unfold(x, mask):
        left = iota((x.shape[0], LANES), 1) < DH
        turned = pltpu.roll(x, DH, 1)
        a, b = jnp.where(left, x, turned), jnp.where(left, turned, x)
        copies = width // LANES
        return (
            (jnp.concatenate([a] * copies, axis=1) * mask).astype(BF16),
            (jnp.concatenate([b] * copies, axis=1) * mask).astype(BF16),
        )

    def features(x):
        xf = x.astype(F32)
        squares = (xf * xf * (0.0625 / factor)).astype(BF16)
        inner = dot(jnp.concatenate([x, squares], axis=1), feat_w[...])
        return jnp.exp2(inner * (factor * LOG2E) - 4.0)

    def feature_back(grad, feat, x):
        scaled = (grad.astype(BF16).astype(F32) * feat.astype(F32)).astype(BF16)
        through = dot_nt(scaled, feat_w[...])
        return through[:, :LANES] * factor + through[:, LANES:] * x.astype(F32) * (factor * factor)

    def total_table(ref):
        flat = ref[: cells * HEADS * FEATS // LANES].astype(F32)
        row = jnp.concatenate(
            [flat[i * cells : (i + 1) * cells] for i in range(HEADS * FEATS // LANES)], axis=1
        )
        full = jnp.concatenate([row] * HEADS, axis=0)
        shape = (HEADS * cells, HEADS * FEATS)
        return (full * hot(iota(shape, 0) >> cells.bit_length() - 1 == iota(shape, 1) >> 8)).astype(BF16)

    def pair_sums(turned, mask_rows, extra, feat_ref, j):
        totals = []
        for i in range(2):
            head = 2 * j + i
            own_rows = turned[i * DH : (i + 1) * DH]
            tall = jnp.concatenate(
                [own_rows * mask_rows[c : c + 1] for c in range(cells)] + [extra(head)], axis=0
            ).astype(BF16)
            both = dot(tall, feat_ref[:, head * FEATS : (head + 1) * FEATS])
            kv_part[j * width : (j + 1) * width, i * FEATS : (i + 1) * FEATS] = both[:width].astype(BF16)
            totals.append(both[width : width + cells])
        return totals

    def store_totals(totals):
        for i in range(0, len(totals), 2):
            tall = jnp.concatenate(
                [x[:, at : at + LANES] for x in totals[i : i + 2] for at in range(0, FEATS, LANES)], axis=0
            )
            kt_part[i * 2 * cells : (i + 2) * 2 * cells] = tall.astype(BF16)

    def front(key_feat):
        for i in range(4):
            load(i).wait()

        def project(t, carry):
            rows = rows_at(t, TILE)
            hid = dot(enc[rows], in_w[...]).astype(BF16)
            hidden[rows] = hid
            unit, _ = moments(hid.astype(F32))
            nor = (unit * gain_one_ref[...] + shift_one_ref[...]).astype(BF16)
            normed[rows] = nor
            key = dot(nor, key_w[...]).astype(BF16)
            keys[rows] = key
            values[rows] = dot(nor, value_w[...]).astype(BF16)
            for j in range(HEADS // 2):
                pair = features(key[:, j * LANES : (j + 1) * LANES])
                key_feat[rows, j * 2 * FEATS : (j + 1) * 2 * FEATS] = pair.astype(BF16)
            return carry

        lax.fori_loop(0, 1, project, 0)
        pl.semaphore_wait(barrier, len(others) + len(mates))
        slot_exchange.start(SLOTS_FIRST)
        lax.fori_loop(1, tokens // TILE, project, 0)
        totals = []
        for j in range(HEADS // 2):
            turned = lax.dot_general(
                value_w[:, j * LANES : (j + 1) * LANES],
                normed[...],
                (((0,), (1,)), ((), ())),
                preferred_element_type=F32,
            )
            totals += pair_sums(turned, keep_rows, lambda head: keep_rows, key_feat, j)
            forward_sum.tick(2 * j, 2 * j + 1)
        store_totals(totals)
        forward_sum.tick(HEADS)

    pl.run_scoped(front, pltpu.VMEM((tokens, HEADS * FEATS), BF16))

    def query_side(t, carry):
        rows = rows_at(t, TILE)
        query = dot(normed[rows], query_w[...]).astype(BF16)
        queries[rows] = query
        for j in range(HEADS // 2):
            pair = features(query[:, j * LANES : (j + 1) * LANES])
            query_feat[rows, j * 2 * FEATS : (j + 1) * 2 * FEATS] = pair.astype(BF16)
        return carry

    load(4).wait()
    pace = list(SLOTS_PACE)

    def forward_step():
        forward_sum.go_on()
        slot_exchange.start(pace.pop(0) if pace else 0)

    forward_step()
    lax.fori_loop(0, tokens // TILE, query_side, 0)
    forward_step()
    slot_block = tables()
    while forward_sum.begun():
        forward_step()
    slot_exchange.start(len(order))

    total_rows[...] = total_table(kt)
    load(5).wait()

    def layer_own():
        return pltpu.make_async_copy(slots.at[own_slots], layer_hbm.at[own_slots], copy_sem.at[2])

    def middle(stream, grad_sum, unit_two, scale_two, slopes):
        def attention(t, carry):
            rows = rows_at(t, TILE)
            here = block_hot(t, TILE)
            mask = dot_nt(here, cell_x[...])
            den = dot_nt(query_feat[rows], total_rows[...]) * dot_nt(here, cell_64[...])
            den_high = den.astype(BF16)
            den_low = (den - den_high.astype(F32)).astype(BF16)
            den_both = jnp.concatenate([den_high, den_low], axis=1)
            den_pair[rows] = den_both
            over = 1.0 / dot(den_both, spread[...])
            for j in range(HEADS // 2):
                at = pl.ds(j * width, width)
                num = fold(
                    dot_nt(query_feat[rows, j * 2 * FEATS : j * 2 * FEATS + FEATS], kv[at, :FEATS]),
                    dot_nt(query_feat[rows, j * 2 * FEATS + FEATS : (j + 1) * 2 * FEATS], kv[at, FEATS:]),
                    mask,
                )
                lanes = slice(j * LANES, (j + 1) * LANES)
                attended[rows, lanes] = (num * over[:, lanes]).astype(BF16)
            mixed = hidden[rows].astype(F32) + dot(attended[rows], out_w[...])
            stream[rows] = mixed
            unit, scale = moments(mixed)
            unit_two[rows] = unit.astype(BF16)
            scale_two[rows] = jnp.broadcast_to(scale, (TILE, LANES))
            normed_two[rows] = (unit * gain_two_ref[...] + shift_two_ref[...]).astype(BF16)
            return carry

        lax.fori_loop(0, tokens // TILE, attention, 0)

        for j in range(hidden_tiles):
            ff = slice(j * D, (j + 1) * D)

            def feed(t, carry):
                rows = rows_at(t, WIDE)
                x = dot(normed_two[rows], up_w[ff])
                square = x * x
                bent = jnp.tanh(x * (GELU_A + (GELU_A * GELU_B) * square))
                ramp = 0.5 + 0.5 * bent
                slope = ramp + (0.5 * x) * (1.0 - bent * bent) * (
                    GELU_A + (3.0 * GELU_A * GELU_B) * square
                )
                active = (x * ramp).astype(BF16)
                there = pl.ds(pl.multiple_of(j * tokens + t * WIDE, WIDE), WIDE)
                early_part[there] = active
                slopes[there] = slope.astype(BF16)
                stream[rows] += dot(active, down_w[ff])
                return carry

            for i in range(8 + j, matrices, hidden_tiles):
                load(i).wait()
            if j == 0:
                load(6).wait()
            lax.fori_loop(0, tokens // WIDE, feed, 0)

        slot_exchange.wait()
        load(7).wait()

        def gather(t, carry):
            rows = rows_at(t, TILE)
            slot_col = dot_nt(
                block_hot(t, TILE), jnp.broadcast_to(slot_block, (LANES, blocks)).astype(BF16)
            ) * BLK + (iota((TILE, LANES), 0) & (BLK - 1)).astype(F32)
            pick = jnp.concatenate(
                [
                    hot(slot_col == (iota((TILE, LANES), 1) + i).astype(F32)).astype(BF16)
                    for i in range(0, slots.shape[0], LANES)
                ],
                axis=1,
            )
            share = jnp.concatenate([share_col[rows]] * (D // LANES), axis=1)
            cot[rows] = (dot(pick, slots[...]) * share).astype(BF16)
            grad_att[rows] = stream[rows].astype(BF16)
            return carry

        lax.fori_loop(0, tokens // TILE, gather, 0)
        for k in list(range(1, cells)) + [0]:
            cell = lax.rem(grp + k, cells)
            pick = hot(
                slot_row[0:1] == (iota((pair_rows, tokens), 0) + cell * pair_rows).astype(F32)
            ).astype(BF16)
            here = pl.ds(pl.multiple_of(cell * pair_rows, pair_rows), pair_rows)
            slots[here] = dot(pick, grad_att[...]).astype(BF16)
            if 0 < k <= LAYER_FIRST:
                layer_exchange.start(1)
        layer_own().start()

        for j in range(hidden_tiles):
            ff = slice(j * D, (j + 1) * D)

            def feed_back(t, carry):
                rows = rows_at(t, WIDE)
                there = pl.ds(pl.multiple_of(j * tokens + t * WIDE, WIDE), WIDE)
                grad_up = (slopes[there].astype(F32) * dot_nt(cot[rows], down_w[ff])).astype(BF16)
                slopes[there] = grad_up
                back = dot_nt(grad_up, up_w[ff])
                if j == 0:
                    grad_sum[rows] = back
                else:
                    grad_sum[rows] += back
                return carry

            lax.fori_loop(0, tokens // WIDE, feed_back, 0)
            layer_exchange.start(LAYER_FEED)

        def back(t, carry):
            rows = rows_at(t, TILE)
            here = block_hot(t, TILE)
            grad_nor = grad_sum[rows]
            unit = unit_two[rows].astype(F32)
            sums[0:8] += jnp.sum((grad_nor * unit).reshape(TILE // 8, 8, D), axis=0)
            sums[8:16] += jnp.sum(grad_nor.reshape(TILE // 8, 8, D), axis=0)
            scale = jnp.concatenate([scale_two[rows]] * (D // LANES), axis=1)
            grad_mix = (
                cot[rows].astype(F32) + norm_back(grad_nor, gain_two_ref[...], unit, scale)
            ).astype(BF16)
            grad_att[rows] = grad_mix
            grad = dot_nt(grad_mix, out_w[...]) / dot(den_pair[rows], spread[...])
            grad_num[rows] = grad.astype(BF16)
            products = (grad * attended[rows].astype(F32)).astype(BF16)
            den_grad[rows] = dot_nt(products, spread[: HEADS * cells]) * dot_nt(here, cell_64[...]) * -1.0
            return carry

        lax.fori_loop(0, tokens // TILE, back, 0)

        den_rows = jnp.concatenate(
            [den_grad[...], jnp.zeros((tokens, LANES - HEADS * cells), F32)], axis=1
        ).T
        totals = []
        for j in range(HEADS // 2):
            turned = grad_num[:, j * LANES : (j + 1) * LANES].astype(F32).T
            totals += pair_sums(
                turned, cell_rows, lambda head: den_rows[head * cells : (head + 1) * cells], query_feat, j
            )
            backward_sum.tick(2 * j, 2 * j + 1)
        store_totals(totals)
        backward_sum.tick(HEADS)

        for j in range(hidden_tiles):
            down_term = dot_tn(early_part[j * tokens : (j + 1) * tokens], cot[...]).astype(BF16)
            up_term = dot_tn(normed_two[...], slopes[j * tokens : (j + 1) * tokens]).astype(BF16)
            early_part[2 * j * D : (2 * j + 1) * D] = down_term
            early_part[(2 * j + 1) * D : (2 * j + 2) * D] = up_term
            back_step()
            early_sum.tick(2 * j, 2 * j + 1)

    back_pace = list(LAYER_PACE)

    def back_step():
        backward_sum.go_on()
        early_sum.go_on_half()
        layer_exchange.start(back_pace.pop(0) if back_pace else 0)

    pl.run_scoped(
        middle,
        pltpu.VMEM((tokens, D), F32),
        pltpu.VMEM((tokens, D), F32),
        pltpu.VMEM((tokens, D), BF16),
        pltpu.VMEM((tokens, LANES), F32),
        pltpu.VMEM((hidden_tiles * tokens, D), BF16),
    )

    early_window = early_sum.go_on if EARLY_WINDOW else early_sum.go_on_half

    def end(key_feat):
        def query_back(t, carry):
            rows = rows_at(t, TILE)
            mask = dot_nt(block_hot(t, TILE), cell_x[...])
            den = den_grad[rows].astype(BF16)
            for j in range(HEADS // 2):
                lanes = slice(j * LANES, (j + 1) * LANES)
                feats = slice(j * 2 * FEATS, (j + 1) * 2 * FEATS)
                a, b = unfold(grad_num[rows, lanes].astype(F32), mask)
                at = pl.ds(j * width, width)
                grad = jnp.concatenate([dot(a, kv[at, :FEATS]), dot(b, kv[at, FEATS:])], axis=1)
                grad += dot(den, total_rows[:, feats])
                queries[rows, lanes] = feature_back(
                    grad, query_feat[rows, feats], queries[rows, lanes]
                ).astype(BF16)
            return carry

        out_row = 2 * hidden_tiles * D
        early_part[out_row : out_row + D] = dot_tn(attended[...], grad_att[...]).astype(BF16)
        back_step()
        early_sum.tick(2 * hidden_tiles)
        lax.fori_loop(0, tokens // TILE // 2, query_back, 0)
        back_step()
        lax.fori_loop(tokens // TILE // 2, tokens // TILE, query_back, 0)
        early_part[out_row + D : out_row + 2 * D] = dot_tn(normed[...], queries[...]).astype(BF16)
        back_step()
        early_sum.tick(2 * hidden_tiles + 1)

        def key_side(t, carry):
            rows = rows_at(t, TILE)
            for j in range(HEADS // 2):
                pair = features(keys[rows, j * LANES : (j + 1) * LANES])
                key_feat[rows, j * 2 * FEATS : (j + 1) * 2 * FEATS] = pair.astype(BF16)
            return carry

        lax.fori_loop(0, tokens // TILE, key_side, 0)
        while backward_sum.begun():
            back_step()

        total_rows[...] = total_table(kt_grad)

        def key_back(t, carry):
            rows = rows_at(t, TILE)
            here = block_hot(t, TILE)
            keep = keep_col[rows]
            mask = dot_nt(here, cell_x[...]) * jnp.concatenate([keep] * (width // LANES), axis=1)
            mask_64 = (dot_nt(here, cell_64[...]) * keep[:, : HEADS * cells]).astype(BF16)
            for j in range(HEADS // 2):
                lanes = slice(j * LANES, (j + 1) * LANES)
                feats = slice(j * 2 * FEATS, (j + 1) * 2 * FEATS)
                a, b = unfold(values[rows, lanes].astype(F32), mask)
                at = pl.ds(j * width, width)
                feat = key_feat[rows, feats]
                grad = jnp.concatenate([dot(a, kv_grad[at, :FEATS]), dot(b, kv_grad[at, FEATS:])], axis=1)
                grad += dot(mask_64, total_rows[:, feats])
                keys[rows, lanes] = feature_back(grad, feat, keys[rows, lanes]).astype(BF16)
                values[rows, lanes] = fold(
                    dot_nt(feat[:, :FEATS], kv_grad[at, :FEATS]),
                    dot_nt(feat[:, FEATS:], kv_grad[at, FEATS:]),
                    mask,
                ).astype(BF16)
            return carry

        lax.fori_loop(0, tokens // TILE // 2, key_back, 0)
        early_window()
        layer_exchange.start(LAYER_LATE)
        lax.fori_loop(tokens // TILE // 2, tokens // TILE, key_back, 0)
        early_window()
        layer_exchange.start(LAYER_LATE)
        kv_part[0:D] = dot_tn(normed[...], keys[...]).astype(BF16)
        kv_part[D : 2 * D] = dot_tn(normed[...], values[...]).astype(BF16)
        late_sum.tick(0, 1, 2, 3)

        def hidden_back(t, carry):
            rows = rows_at(t, TILE)
            grad_nor = (
                dot_nt(queries[rows], query_w[...])
                + dot_nt(keys[rows], key_w[...])
                + dot_nt(values[rows], value_w[...])
            )
            unit, scale = moments(hidden[rows].astype(F32))
            sums[16:24] += jnp.sum((grad_nor * unit).reshape(TILE // 8, 8, D), axis=0)
            sums[24:32] += jnp.sum(grad_nor.reshape(TILE // 8, 8, D), axis=0)
            cot[rows] = (
                grad_att[rows].astype(F32) + norm_back(grad_nor, gain_one_ref[...], unit, scale)
            ).astype(BF16)
            return carry

        lax.fori_loop(0, tokens // TILE, hidden_back, 0)
        early_window()
        late_sum.tick(0, 1, 2, 3)
        kv_part[2 * D : 2 * D + D_IN] = dot_tn(enc[...], cot[...]).astype(BF16)
        small = jnp.concatenate(
            [jnp.sum(sums[8 * i : 8 * i + 8], axis=0, keepdims=True) for i in range(4)]
            + [jnp.zeros((12, D), F32)],
            axis=0,
        )
        at = 2 * D + D_IN
        kv_part[at : at + 16] = small.astype(BF16)
        kv_part[at + 16 :] = jnp.zeros((kv_part.shape[0] - at - 16, D), BF16)
        late_sum.tick(4, 5, 6, 7)
        early_window()
        layer_exchange.start(LAYER_LATE)

        def encoder_grad(t, carry):
            rows = rows_at(t, TILE)
            enc[rows] = dot_nt(cot[rows], in_w[...]).astype(BF16)
            return carry

        lax.fori_loop(0, tokens // TILE, encoder_grad, 0)
        enc_copy = pltpu.make_async_copy(enc, enc_grad_hbm, copy_sem.at[3])
        enc_copy.start()
        while late_sum.begun():
            late_sum.go_on()
            early_sum.go_on_half()
            layer_exchange.start(LAYER_LATE)
        early_sum.run()
        ends = []
        for i, (at, rows, target) in enumerate(
            (
                (0, D, key_sum_hbm),
                (D, D, value_sum_hbm),
                (2 * D, D_IN, in_sum_hbm),
                (2 * D + D_IN, 16, small_sum_hbm),
            )
        ):
            ends.append(pltpu.make_async_copy(kv.at[pl.ds(at, rows)], target, copy_sem.at[4 + i]))
            ends[-1].start()
        layer_exchange.wait()
        layer_own().wait()
        enc_copy.wait()
        for copy in ends:
            copy.wait()

    pl.run_scoped(end, pltpu.VMEM((tokens, HEADS * FEATS), BF16))


def widen_kernel(places, *refs):
    count = len(places)
    sources, targets = refs[:count], refs[count : 2 * count]
    narrow, wide, in_sem, out_sem = refs[2 * count :]
    depth = narrow.shape[0]
    chunks = []
    for n, (rows, columns) in enumerate(places):
        for at in range(0, rows, D):
            for left in range(0, columns, D):
                chunks.append((n, at, min(D, rows - at), left))

    def come(i):
        n, at, rows, left = chunks[i]
        source = sources[n].at[pl.ds(at, rows), pl.ds(left, D)]
        return pltpu.make_async_copy(source, narrow.at[i % depth, pl.ds(0, rows)], in_sem.at[i % depth])

    def go(i):
        n, at, rows, left = chunks[i]
        target = targets[n].at[pl.ds(at, rows), pl.ds(left, D)]
        return pltpu.make_async_copy(wide.at[i % depth, pl.ds(0, rows)], target, out_sem.at[i % depth])

    for i in range(min(depth, len(chunks))):
        come(i).start()
    for i in range(len(chunks)):
        rows = chunks[i][2]
        come(i).wait()
        if i >= depth:
            go(i - depth).wait()
        wide[i % depth, :rows] = narrow[i % depth, :rows].astype(F32)
        go(i).start()
        if i + depth < len(chunks):
            come(i + depth).start()
    for i in range(max(0, len(chunks) - depth), len(chunks)):
        go(i).wait()


def widen(*arrays):
    rest = pl.BlockSpec(memory_space=pl.ANY)
    results = pl.pallas_call(
        functools.partial(widen_kernel, tuple(a.shape for a in arrays)),
        out_shape=[jax.ShapeDtypeStruct(a.shape, F32) for a in arrays],
        in_specs=[rest] * len(arrays),
        out_specs=[rest] * len(arrays),
        scratch_shapes=[
            pltpu.VMEM((WIDEN_DEPTH, D, D), BF16),
            pltpu.VMEM((WIDEN_DEPTH, D, D), F32),
            pltpu.SemaphoreType.DMA((WIDEN_DEPTH,)),
            pltpu.SemaphoreType.DMA((WIDEN_DEPTH,)),
        ],
        compiler_params=pltpu.CompilerParams(vmem_limit_bytes=VMEM_LIMIT),
        name="widen",
    )(*arrays)
    return results


def fused(
    mesh,
    encoded,
    destination,
    expressed,
    in_proj,
    gain_one,
    shift_one,
    query_w,
    key_w,
    value_w,
    out_w,
    gain_two,
    shift_two,
    up_w,
    down_w,
    random_features,
    out_cotangent,
):
    sizes = {"grp": mesh.shape["grp"], "seq": mesh.shape["seq"]}
    cells, splits, blocks = destination.shape
    tokens = encoded.shape[2]
    slot_total = out_cotangent.shape[2]
    cap = slot_total // (cells * BLK)
    width = cells * DH
    digits = digits_of(sizes)
    unit = 16 * sizes["grp"] * sizes["seq"]
    steps = 2 * sum(radix - 1 for _, _, radix in digits)
    early = 2 * FF + 2 * D
    half = HEADS // 2 * width
    count = HEADS + 1 + early // unit

    def vmem(shape, kind=BF16):
        return pltpu.VMEM(shape, kind)

    def shape(*dims):
        return jax.ShapeDtypeStruct(dims, BF16)

    rest = pl.BlockSpec(memory_space=pl.ANY)
    results = pl.pallas_call(
        functools.partial(fused_kernel, sizes, cap),
        out_shape=(
            shape(slot_total, D),
            shape(tokens, D_IN),
            shape(D_IN, D),
            shape(D, D),
            shape(D, D),
            shape(D, D),
            shape(D, D),
            shape(D, FF),
            shape(FF, D),
            shape(16, D),
        ),
        in_specs=[rest] * 16,
        out_specs=(rest,) * 10,
        scratch_shapes=[
            vmem(destination.shape, jnp.int32),
            vmem(expressed.shape, jnp.int32),
            vmem((1, D), F32),
            vmem((1, D), F32),
            vmem((1, D), F32),
            vmem((1, D), F32),
            vmem((DH, FEATS)),
            vmem((tokens, D_IN)),
            vmem((D_IN, D)),
            vmem((D, D)),
            vmem((D, D)),
            vmem((D, D)),
            vmem((D, D)),
            vmem((FF, D)),
            vmem((FF, D)),
            vmem((slot_total, D)),
            vmem((tokens, D)),
            vmem((tokens, D)),
            vmem((tokens, D)),
            vmem((tokens, D)),
            vmem((tokens, D)),
            vmem((tokens, D)),
            vmem((tokens, HEADS * FEATS)),
            vmem((half, 2 * FEATS)),
            vmem((half, 2 * FEATS)),
            vmem((half, 2 * FEATS)),
            vmem((half, 2 * FEATS)),
            vmem((unit, LANES)),
            vmem((unit, LANES)),
            vmem((unit, LANES)),
            vmem((unit, LANES)),
            vmem((tokens, D)),
            vmem((tokens, D)),
            vmem((tokens, D)),
            vmem((tokens, D)),
            vmem((tokens, 2 * HEADS * cells)),
            vmem((tokens, HEADS * cells), F32),
            vmem((early, D)),
            vmem((early, D)),
            vmem((early // unit * 16, D)),
            vmem((4 * DH, 2 * FEATS)),
            vmem((width, blocks)),
            vmem((HEADS * cells, blocks)),
            vmem((tokens, LANES), F32),
            vmem((tokens, LANES), F32),
            vmem((8, tokens), F32),
            vmem((HEADS * cells, HEADS * FEATS)),
            vmem((2 * HEADS * cells, D)),
            vmem((32, D), F32),
            pltpu.SemaphoreType.DMA((15 + FF // D,)),
            pltpu.SemaphoreType.DMA((PARTS * (cells - 1),)),
            pltpu.SemaphoreType.DMA((PARTS * (cells - 1),)),
            pltpu.SemaphoreType.DMA((PARTS * (cells - 1),)),
            pltpu.SemaphoreType.DMA((PARTS * (cells - 1),)),
            pltpu.SemaphoreType.DMA((8,)),
            pltpu.SemaphoreType.DMA((early // unit,)),
            pltpu.SemaphoreType.DMA((count * steps,)),
            pltpu.SemaphoreType.DMA((count * steps,)),
        ],
        compiler_params=pltpu.CompilerParams(
            collective_id=1, has_side_effects=True, vmem_limit_bytes=VMEM_LIMIT
        ),
        name="layer_and_gradients",
    )(
        destination,
        expressed,
        gain_one.reshape(1, D),
        shift_one.reshape(1, D),
        gain_two.reshape(1, D),
        shift_two.reshape(1, D),
        random_features,
        encoded.reshape(tokens, D_IN),
        in_proj,
        query_w,
        key_w,
        value_w,
        out_w,
        up_w,
        down_w,
        out_cotangent.reshape(slot_total, D),
    )
    layer, enc_grad, in_b, query_b, key_b, value_b, out_b, up_b, down_b, small_b = results
    layer, down, up, in_sum, query, key, value, out = widen(
        layer, down_b, up_b, in_b, query_b, key_b, value_b, out_b
    )
    small = small_b.astype(F32)
    return (
        layer.reshape(1, 1, slot_total, D),
        enc_grad.reshape(1, 1, tokens, D_IN),
        in_sum,
        small[2],
        small[3],
        query,
        key,
        value,
        out,
        small[0],
        small[1],
        up,
        down,
    )


def layer_norm(values, gain, shift):
    center = values - jnp.mean(values, axis=-1, keepdims=True)
    variance = jnp.mean(center * center, axis=-1, keepdims=True)
    return center * lax.rsqrt(variance + 1e-05) * gain + shift


def feature_map(projected, omega_b, key_keep):
    row_count = projected.shape[0]
    pieces = projected.reshape(row_count, HEADS, DH)
    factor = DH ** (-0.25)
    logits = jnp.einsum("nhd,dm->nhm", pieces, omega_b, preferred_element_type=jnp.float32) * factor
    squares = (
        0.5
        * factor
        * factor
        * jnp.sum(jnp.square(pieces.astype(jnp.float32)), axis=-1, keepdims=True)
    )
    return jnp.exp(logits - squares) * FEATS ** (-0.5) * key_keep[:, None, None]


def feature_grad(grad_feat, feat_full, projected, omega_b):
    row_count = projected.shape[0]
    factor = DH ** (-0.25)
    scaled = grad_feat.astype(jnp.float32) * feat_full
    logit_grad = scaled.astype(jnp.bfloat16)
    pieces = projected.reshape(row_count, HEADS, DH).astype(jnp.float32)
    through = (
        jnp.einsum("nhm,dm->nhd", logit_grad, omega_b, preferred_element_type=jnp.float32) * factor
    )
    direct = pieces * (factor * factor) * jnp.sum(scaled, axis=-1, keepdims=True)
    return (through - direct).reshape(row_count, HEADS * DH).astype(jnp.bfloat16)


def weight_term(left, right):
    return jnp.einsum("nk,nd->kd", left, right, preferred_element_type=jnp.float32)


def plain(
    encoded,
    destination,
    expressed,
    in_proj,
    gain_one,
    shift_one,
    query_w,
    key_w,
    value_w,
    out_w,
    gain_two,
    shift_two,
    up_w,
    down_w,
    random_features,
    out_cotangent,
):
    cell_count = destination.shape[0]
    split_count = destination.shape[1]
    blocks = destination.shape[2]
    tokens = encoded.shape[2]
    block_len = tokens // blocks
    row_total = out_cotangent.shape[2]
    slot_count = row_total // (cell_count * block_len)
    pair_rows = slot_count * block_len
    group_index = lax.axis_index("grp")
    split_index = lax.axis_index("seq")
    targets = jnp.arange(cell_count, dtype=jnp.int32)
    slot_ids = jnp.arange(slot_count, dtype=jnp.int32)
    within = jnp.arange(block_len, dtype=jnp.int32)
    block_ids = jnp.arange(blocks, dtype=jnp.int32)
    column = lax.dynamic_index_in_dim(destination, split_index, 1, keepdims=False)
    block_hits = (column[:, :, None] == targets).astype(jnp.int32)
    block_rank = jnp.sum(jnp.cumsum(block_hits, axis=1) * block_hits, axis=2) - 1
    own_dest = lax.dynamic_index_in_dim(column, group_index, 0, keepdims=False)
    own_rank = lax.dynamic_index_in_dim(block_rank, group_index, 0, keepdims=False)
    send_match = (
        (own_dest[:, None, None] == targets[:, None]) & (own_rank[:, None, None] == slot_ids)
    ).astype(jnp.int32)
    send_found = jnp.sum(send_match, axis=0)
    send_block = jnp.sum(send_match * block_ids[:, None, None], axis=0)
    send_index = (send_block[:, :, None] * block_len + within).reshape(-1)
    send_keep = jnp.repeat(send_found.reshape(-1), block_len).astype(jnp.bfloat16)
    back_index = ((own_dest * slot_count + own_rank)[:, None] * block_len + within).reshape(-1)
    recv_match = (
        (column[:, :, None] == group_index) & (block_rank[:, :, None] == slot_ids)
    ).astype(jnp.int32)
    recv_found = jnp.sum(recv_match, axis=1)
    recv_block = jnp.sum(recv_match * block_ids[:, None], axis=1)
    recv_token = (recv_block[:, :, None] * block_len + within).reshape(cell_count, pair_rows)
    expressed_col = lax.dynamic_index_in_dim(expressed, split_index, 1, keepdims=False)
    valid = jnp.repeat(recv_found.reshape(-1), block_len).astype(jnp.float32)
    key_keep = (
        jnp.take_along_axis(expressed_col, recv_token, axis=1).reshape(-1).astype(jnp.float32)
        * valid
    )
    block_sum = jnp.sum(expressed.reshape(cell_count, split_count, blocks, block_len), axis=3)
    dest_hits = destination[..., None] == targets
    counts = jnp.sum(jnp.where(dest_hits, block_sum[..., None], 0), axis=(0, 1, 2)).astype(
        jnp.float32
    )
    own_count = lax.dynamic_index_in_dim(counts, group_index, 0, keepdims=False)
    share = cell_count * own_count / jnp.sum(counts)
    token_rows = encoded.reshape(tokens, D_IN)
    token_hidden = jnp.dot(token_rows, in_proj, preferred_element_type=jnp.float32).astype(
        jnp.bfloat16
    )
    outgoing = jnp.take(token_hidden, send_index, axis=0) * send_keep[:, None]
    hidden_b = lax.all_to_all(
        outgoing.reshape(cell_count, pair_rows, D),
        "grp",
        split_axis=0,
        concat_axis=0,
        tiled=True,
    ).reshape(row_total, D)
    hidden_f = hidden_b.astype(jnp.float32)
    normed_f, norm_one_pull = jax.vjp(layer_norm, hidden_f, gain_one, shift_one)
    normed_b = normed_f.astype(jnp.bfloat16)
    queries_b = jnp.dot(normed_b, query_w, preferred_element_type=jnp.float32).astype(jnp.bfloat16)
    keys_b = jnp.dot(normed_b, key_w, preferred_element_type=jnp.float32).astype(jnp.bfloat16)
    values_b = jnp.dot(normed_b, value_w, preferred_element_type=jnp.float32).astype(jnp.bfloat16)
    query_full = feature_map(queries_b, random_features, jnp.ones((row_total,), jnp.float32))
    key_full = feature_map(keys_b, random_features, key_keep)
    query_feature_rows = query_full.astype(jnp.bfloat16)
    key_feature_rows = key_full.astype(jnp.bfloat16)
    value_per_head = values_b.reshape(row_total, HEADS, DH)
    value_part = jnp.einsum(
        "pgk,pgz->gkz", key_feature_rows, value_per_head, preferred_element_type=jnp.float32
    )
    total_part = jnp.sum(key_feature_rows, axis=0, dtype=jnp.float32)
    key_value_products, key_total = lax.psum((value_part, total_part), "seq")
    key_value_batched = key_value_products.astype(jnp.bfloat16)
    attention_numerator = jnp.einsum(
        "bli,lie->ble", query_feature_rows, key_value_batched, preferred_element_type=jnp.float32
    )
    denominator = jnp.sum(query_feature_rows.astype(jnp.float32) * key_total[None], axis=-1)
    attended_b = (
        (attention_numerator / denominator[:, :, None]).reshape(row_total, D).astype(jnp.bfloat16)
    )
    mixed = hidden_f + jnp.dot(attended_b, out_w, preferred_element_type=jnp.float32)
    normed_two_f, norm_two_pull = jax.vjp(layer_norm, mixed, gain_two, shift_two)
    normed_two_b = normed_two_f.astype(jnp.bfloat16)
    expanded = jnp.dot(normed_two_b, up_w, preferred_element_type=jnp.float32)
    activated_f, gelu_pull = jax.vjp(partial_gelu, expanded)
    activated_b = activated_f.astype(jnp.bfloat16)
    layer_out = (mixed + jnp.dot(activated_b, down_w, preferred_element_type=jnp.float32)) * valid[
        :, None
    ]
    grad_out = out_cotangent.reshape(row_total, D).astype(jnp.float32) * (valid * share)[:, None]
    grad_mlp = grad_out.astype(jnp.bfloat16)
    down_term = weight_term(activated_b, grad_mlp)
    grad_activated = jnp.dot(grad_mlp, down_w.T, preferred_element_type=jnp.float32)
    grad_up = gelu_pull(grad_activated)[0].astype(jnp.bfloat16)
    up_term = weight_term(normed_two_b, grad_up)
    grad_normed_two = jnp.dot(grad_up, up_w.T, preferred_element_type=jnp.float32)
    mixed_back, gain_two_term, shift_two_term = norm_two_pull(grad_normed_two)
    grad_mixed = grad_out + mixed_back
    grad_att = grad_mixed.astype(jnp.bfloat16)
    out_term = weight_term(attended_b, grad_att)
    grad_attended = jnp.dot(grad_att, out_w.T, preferred_element_type=jnp.float32).reshape(
        row_total, HEADS, DH
    )
    numerator_gradient = (grad_attended / denominator[:, :, None]).astype(jnp.bfloat16)
    grad_den = -jnp.sum(grad_attended * attention_numerator, axis=-1) / (denominator * denominator)
    value_grad_part = jnp.einsum(
        "pgk,pgz->gkz", query_feature_rows, numerator_gradient, preferred_element_type=jnp.float32
    )
    total_grad_part = jnp.sum(query_feature_rows.astype(jnp.float32) * grad_den[:, :, None], axis=0)
    grad_query_feat = (
        jnp.einsum(
            "pao,ajo->paj",
            numerator_gradient,
            key_value_batched,
            preferred_element_type=jnp.float32,
        )
        + grad_den[:, :, None] * key_total[None]
    ).astype(jnp.bfloat16)
    grad_kv, grad_total = lax.psum((value_grad_part, total_grad_part), "seq")
    key_value_gradient_batched = grad_kv.astype(jnp.bfloat16)
    grad_key_feat = (
        jnp.einsum(
            "pao,ajo->paj",
            value_per_head,
            key_value_gradient_batched,
            preferred_element_type=jnp.float32,
        )
        + grad_total[None]
    ).astype(jnp.bfloat16)
    grad_values = (
        jnp.einsum(
            "bli,lie->ble",
            key_feature_rows,
            key_value_gradient_batched,
            preferred_element_type=jnp.float32,
        )
        .reshape(row_total, D)
        .astype(jnp.bfloat16)
    )
    grad_queries = feature_grad(grad_query_feat, query_full, queries_b, random_features)
    grad_keys = feature_grad(grad_key_feat, key_full, keys_b, random_features)
    query_term = weight_term(normed_b, grad_queries)
    key_term = weight_term(normed_b, grad_keys)
    value_term = weight_term(normed_b, grad_values)
    grad_normed = jnp.dot(grad_queries, query_w.T, preferred_element_type=jnp.float32)
    grad_normed = grad_normed + jnp.dot(grad_keys, key_w.T, preferred_element_type=jnp.float32)
    grad_normed = grad_normed + jnp.dot(grad_values, value_w.T, preferred_element_type=jnp.float32)
    hidden_back, gain_one_term, shift_one_term = norm_one_pull(grad_normed)
    grad_hidden = (grad_mixed + hidden_back).astype(jnp.bfloat16)
    returned = lax.all_to_all(
        grad_hidden.reshape(cell_count, pair_rows, D),
        "grp",
        split_axis=0,
        concat_axis=0,
        tiled=True,
    )
    token_grad = jnp.take(returned.reshape(row_total, D), back_index, axis=0)
    encoded_grad = jnp.dot(token_grad, in_proj.T, preferred_element_type=jnp.float32).astype(
        jnp.bfloat16
    )
    in_term = weight_term(token_rows, token_grad)
    (
        in_sum,
        query_sum,
        key_sum,
        value_sum,
        out_sum,
        up_sum,
        down_sum,
        gain_one_sum,
        shift_one_sum,
        gain_two_sum,
        shift_two_sum,
    ) = lax.psum(
        (
            in_term,
            query_term,
            key_term,
            value_term,
            out_term,
            up_term,
            down_term,
            gain_one_term,
            shift_one_term,
            gain_two_term,
            shift_two_term,
        ),
        ("grp", "seq"),
    )
    return (
        layer_out.reshape(1, 1, row_total, D),
        encoded_grad.reshape(1, 1, tokens, D_IN),
        in_sum,
        gain_one_sum,
        shift_one_sum,
        query_sum,
        key_sum,
        value_sum,
        out_sum,
        gain_two_sum,
        shift_two_sum,
        up_sum,
        down_sum,
    )


def partial_gelu(values):
    return jax.nn.gelu(values, approximate=True)


def solution(mesh):
    in_specs = (
        P("grp", "seq", None, None),
        P(),
        P(),
        P(),
        P(),
        P(),
        P(),
        P(),
        P(),
        P(),
        P(),
        P(),
        P(),
        P(),
        P(),
        P("grp", "seq", None, None),
    )
    out_specs = (
        P("grp", "seq", None, None),
        P("grp", "seq", None, None),
        P(),
        P(),
        P(),
        P(),
        P(),
        P(),
        P(),
        P(),
        P(),
        P(),
        P(),
    )
    body = functools.partial(fused, mesh) if mesh.shape["grp"] <= FUSED_CELLS else plain
    return jax.shard_map(body, mesh=mesh, in_specs=in_specs, out_specs=out_specs, check_vma=False)
```

```python
import functools

import jax
import jax.numpy as jnp
from jax import lax
from jax.experimental import pallas as pl
from jax.experimental.pallas import tpu as pltpu
from jax.sharding import PartitionSpec as P

D_IN = 768
D = 512
HEADS = 8
DH = 64
FEATS = 256
FF = 2048
BLK = 8
LANES = 128
TILE = 256
WIDE = 512
PARTS = 4
WIDEN_DEPTH = 12
SLOTS_FIRST = 10
SLOTS_PACE = (3, 2, 1, 0, 0, 0, 0, 2, 4, 4)
LAYER_FIRST = 4
LAYER_FEED = 4
LAYER_PACE = (1, 1, 1, 0, 0, 0, 1, 1, 1, 1)
LAYER_LATE = 2
KV_ORDERS = (0, 1, 0)
EARLY_ORDERS = (0, 1)
EARLY_WINDOW = False
LATE_ORDERS = (0, 1)
FUSED_CELLS = 8
VMEM_LIMIT = 62 << 20
LOG2E = 1.4426950408889634
GELU_A = 0.7978845608028654
GELU_B = 0.044715
F32, BF16 = jnp.float32, jnp.bfloat16
MESH = pl.DeviceIdType.MESH


def dot(a, b):
    return jnp.dot(a, b, preferred_element_type=F32)


def dot_nt(a, b):
    return lax.dot_general(a, b, (((1,), (1,)), ((), ())), preferred_element_type=F32)


def dot_tn(a, b):
    return lax.dot_general(a, b, (((0,), (0,)), ((), ())), preferred_element_type=F32)


def iota(shape, axis):
    return lax.broadcasted_iota(jnp.int32, shape, axis)


def hot(condition):
    return jnp.where(condition, 1.0, 0.0)


def moments(x):
    center = x - jnp.mean(x, axis=-1, keepdims=True)
    scale = lax.rsqrt(jnp.mean(center * center, axis=-1, keepdims=True) + 1e-05)
    return center * scale, scale


def norm_back(grad, gain, unit, scale):
    inner = grad * gain
    return scale * (
        inner
        - jnp.mean(inner, axis=-1, keepdims=True)
        - unit * jnp.mean(inner * unit, axis=-1, keepdims=True)
    )


def digits_of(sizes):
    digits = []
    for axis in ("seq", "grp"):
        if sizes[axis] > 1:
            digits.append((axis, 1, 2))
        step = 2
        while step < sizes[axis]:
            digits.append((axis, step, 2))
            step *= 2
    return digits


def peers(digit):
    grp, seq = lax.axis_index("grp"), lax.axis_index("seq")
    axis, step, radix = digit
    index = seq if axis == "seq" else grp
    value = (index // step) % radix
    found = []
    for m in range(1, radix):
        other = index + ((value + m) % radix - value) * step
        found.append((grp, other) if axis == "seq" else (other, seq))
    return value, found


def digit_orders(digits):
    first, second = list(digits), list(digits)
    if len(digits) > 2:
        second[1], second[2] = second[2], second[1]
    return first, second


class Sum:
    def __init__(self, digits, pieces, pattern, send, recv, base, settle=None):
        self.pieces, self.send, self.recv, self.base, self.settle = pieces, send, recv, base, settle
        self.half_steps, self.steps = len(digits), 2 * len(digits)
        self.copies = 2 * sum(radix - 1 for _, _, radix in digits)
        self.step = [-1] * len(pieces)
        self.turn = 0
        self.plans = []
        orders = digit_orders(digits)
        for c, piece in enumerate(pieces):
            at, rows, inbox_at, sem = 0, piece[6], piece[3], base + c * self.copies
            plan, kept = [], []
            for digit in orders[pattern[c % len(pattern)]]:
                value, found = peers(digit)
                radix = digit[2]
                rows //= radix
                keep = at + value * rows
                moves = []
                for m, device in enumerate(found, 1):
                    moves.append((device, at + (value + m) % radix * rows, inbox_at, sem))
                    inbox_at += rows
                    sem += 1
                kept.append((found, keep, rows))
                plan.append((moves, keep, rows))
                at = keep
            for found, keep, rows in reversed(kept):
                moves = [(device, keep, None, sem + m) for m, device in enumerate(found)]
                sem += len(found)
                plan.append((moves, keep, rows))
            self.plans.append(plan)

    def transfers(self, c, k):
        part, start, inbox, _, total, total_at, _, own = self.pieces[c]
        moves, _, rows = self.plans[c][k]
        found = []
        for device, at, inbox_at, sem in moves:
            if k < self.half_steps:
                source = part.at[pl.ds(pl.multiple_of(start + at, 16), rows)]
                target = inbox.at[pl.ds(inbox_at, rows)]
            else:
                target = total.at[pl.ds(pl.multiple_of(total_at + at, 16), rows)]
                source = target if own is None or k > self.half_steps else own
            found.append(
                pltpu.make_async_remote_copy(
                    src_ref=source,
                    dst_ref=target,
                    send_sem=self.send.at[sem],
                    recv_sem=self.recv.at[sem],
                    device_id=device,
                    device_id_type=MESH,
                )
            )
        return found

    def settled(self, c):
        _, _, _, _, total, total_at, _, own = self.pieces[c]
        _, at, rows = self.plans[c][self.half_steps]
        target = total.at[pl.ds(pl.multiple_of(total_at + at, 16), rows)]
        return pltpu.make_async_copy(own, target, self.settle.at[c])

    def finish(self, c):
        k = self.step[c]
        part, start, inbox, _, total, total_at, _, own = self.pieces[c]
        for transfer in self.transfers(c, k):
            transfer.wait()
        if k == self.half_steps and own is not None:
            self.settled(c).wait()
        if k >= self.half_steps:
            return
        moves, keep, rows = self.plans[c][k]
        step = min(rows, 256)
        last = k == self.half_steps - 1

        def add(i, carry):
            here = pl.ds(pl.multiple_of(start + keep + i * step, 16), step)
            value = part[here].astype(F32)
            for _, _, inbox_at, _ in moves:
                value += inbox[pl.ds(pl.multiple_of(inbox_at + i * step, 16), step)].astype(F32)
            value = value.astype(BF16)
            if not last:
                part[here] = value
            elif own is None:
                total[pl.ds(pl.multiple_of(total_at + keep + i * step, 16), step)] = value
            else:
                own[...] = value
            return carry

        if rows == step:
            add(0, 0)
        else:
            lax.fori_loop(0, rows // step, add, 0)
        if last and own is not None:
            self.settled(c).start()

    def tick(self, *which):
        for c in which:
            if self.step[c] >= 0:
                self.finish(c)
            self.step[c] += 1
            if self.step[c] < self.steps:
                for transfer in self.transfers(c, self.step[c]):
                    transfer.start()

    def begun(self):
        return [c for c in range(len(self.pieces)) if 0 <= self.step[c] < self.steps]

    def go_on(self):
        self.tick(*self.begun())

    def go_on_half(self):
        self.turn += 1
        self.tick(*[c for c in self.begun() if (c // 2 + self.turn) % 2])

    def run(self):
        while self.begun():
            self.go_on()


class Exchange:
    def __init__(self, makers):
        self.makers, self.started = makers, 0

    def start(self, count):
        for make in self.makers[self.started : self.started + count]:
            make().start()
        self.started = min(self.started + count, len(self.makers))

    def wait(self):
        self.start(len(self.makers))
        for make in self.makers:
            make().wait()


def fused_kernel(
    sizes,
    cap,
    dest_hbm,
    expr_hbm,
    gain_one_hbm,
    shift_one_hbm,
    gain_two_hbm,
    shift_two_hbm,
    omega_hbm,
    enc_hbm,
    in_hbm,
    query_hbm,
    key_hbm,
    value_hbm,
    out_hbm,
    up_hbm,
    down_hbm,
    cot_hbm,
    layer_hbm,
    enc_grad_hbm,
    in_sum_hbm,
    query_sum_hbm,
    key_sum_hbm,
    value_sum_hbm,
    out_sum_hbm,
    up_sum_hbm,
    down_sum_hbm,
    small_sum_hbm,
    dest_ref,
    expr_ref,
    gain_one_ref,
    shift_one_ref,
    gain_two_ref,
    shift_two_ref,
    omega_ref,
    enc,
    in_w,
    query_w,
    key_w,
    value_w,
    out_w,
    up_w,
    down_w,
    slots,
    cot,
    hidden,
    normed,
    queries,
    keys,
    values,
    query_feat,
    kv_part,
    kv_inbox,
    kv,
    kv_grad,
    kt_part,
    kt_inbox,
    kt,
    kt_grad,
    attended,
    normed_two,
    grad_att,
    grad_num,
    den_pair,
    den_grad,
    early_part,
    early_inbox,
    early_own,
    feat_w,
    cell_x,
    cell_64,
    keep_col,
    share_col,
    slot_row,
    total_rows,
    spread,
    sums,
    load_sem,
    slot_send,
    slot_recv,
    layer_send,
    layer_recv,
    copy_sem,
    settle_sem,
    sum_send,
    sum_recv,
):
    grp, seq = lax.axis_index("grp"), lax.axis_index("seq")
    cells = sizes["grp"]
    digits = digits_of(sizes)
    tokens = enc.shape[0]
    blocks = dest_ref.shape[2]
    width = cells * DH
    pair_rows = slots.shape[0] // cells
    unit_rows = 16 * sizes["grp"] * sizes["seq"]
    factor = DH ** (-0.25)
    hidden_tiles = FF // D

    own_slots = pl.ds(pl.multiple_of(grp * pair_rows, pair_rows), pair_rows)
    sources = [
        (enc_hbm, enc),
        (in_hbm, in_w),
        (key_hbm, key_w),
        (value_hbm, value_w),
        (query_hbm, query_w),
        (out_hbm, out_w),
        (down_hbm, down_w),
        (cot_hbm.at[own_slots], slots.at[own_slots]),
    ]
    sources += [(up_hbm.at[:, pl.ds(j * D, D)], up_w.at[pl.ds(j * D, D)]) for j in range(hidden_tiles)]

    def load(i):
        return pltpu.make_async_copy(*sources[i], load_sem.at[i])

    matrices = len(sources)
    sources += [
        (dest_hbm, dest_ref),
        (expr_hbm, expr_ref),
        (omega_hbm, omega_ref),
        (gain_one_hbm, gain_one_ref),
        (shift_one_hbm, shift_one_ref),
        (gain_two_hbm, gain_two_ref),
        (shift_two_hbm, shift_two_ref),
    ]
    for i in list(range(matrices, len(sources))) + list(range(matrices)):
        load(i).start()

    barrier = pltpu.get_barrier_semaphore()
    others = [(lax.rem(grp + k, cells), seq) for k in range(1, cells)]
    mates = [device for digit in digits if digit[0] == "seq" for device in peers(digit)[1]]
    for device in others + mates:
        pl.semaphore_signal(barrier, inc=1, device_id=device, device_id_type=MESH)

    part_rows = pair_rows // PARTS

    def slot_copy(k, i):
        theirs = pl.multiple_of(others[k][0] * pair_rows + i * part_rows, part_rows)
        ours = pl.multiple_of(grp * pair_rows + i * part_rows, part_rows)
        return pltpu.make_async_remote_copy(
            src_ref=cot_hbm.at[pl.ds(theirs, part_rows)],
            dst_ref=slots.at[pl.ds(ours, part_rows)],
            send_sem=slot_send.at[k * PARTS + i],
            recv_sem=slot_recv.at[k * PARTS + i],
            device_id=others[k],
            device_id_type=MESH,
        )

    def layer_copy(k, i):
        theirs = pl.multiple_of(others[k][0] * pair_rows + i * part_rows, part_rows)
        ours = pl.multiple_of(grp * pair_rows + i * part_rows, part_rows)
        return pltpu.make_async_remote_copy(
            src_ref=slots.at[pl.ds(theirs, part_rows)],
            dst_ref=layer_hbm.at[pl.ds(ours, part_rows)],
            send_sem=layer_send.at[k * PARTS + i],
            recv_sem=layer_recv.at[k * PARTS + i],
            device_id=others[k],
            device_id_type=MESH,
        )

    order = [(k, i) for i in range(PARTS) for k in range(cells - 1)]
    slot_exchange = Exchange([functools.partial(slot_copy, k, i) for k, i in order])
    layer_exchange = Exchange([functools.partial(layer_copy, k, i) for k, i in order])

    def columns(ref, i):
        return ref.at[:, pl.ds(i * FEATS, FEATS)]

    def kv_pieces(total, rows):
        return [
            (columns(kv_part, i), at, columns(kv_inbox, i), at, columns(total, i), at, rows, None)
            for at in range(0, kv.shape[0], rows)
            for i in range(2)
        ]

    def kt_piece(total):
        return [(kt_part, 0, kt_inbox, 0, total, 0, kt_part.shape[0], None)]

    forward_sum = Sum(
        digits, kv_pieces(kv, width) + kt_piece(kt), KV_ORDERS, sum_send, sum_recv, 0
    )
    backward_sum = Sum(
        digits, kv_pieces(kv_grad, width) + kt_piece(kt_grad), KV_ORDERS, sum_send, sum_recv, 0
    )
    late_sum = Sum(digits, kv_pieces(kv, unit_rows), LATE_ORDERS, sum_send, sum_recv, 0)
    early_totals = []
    for j in range(hidden_tiles):
        early_totals.append((down_sum_hbm, j * D))
        early_totals.append((up_sum_hbm.at[:, pl.ds(j * D, D)], 0))
    early_totals += [(out_sum_hbm, 0), (query_sum_hbm, 0)]
    early_sum = Sum(
        digits,
        [
            (early_part, c * D, early_inbox, c * D, total, at, D, early_own.at[pl.ds(c * 16, 16)])
            for c, (total, at) in enumerate(early_totals)
        ],
        EARLY_ORDERS,
        sum_send,
        sum_recv,
        forward_sum.copies * len(forward_sum.pieces),
        settle_sem,
    )
    for i in range(matrices, len(sources)):
        load(i).wait()

    own = dest_ref[grp, pl.ds(seq, 1), :]
    cell_hot = hot(iota((cells, blocks), 0) == own)
    block_of = hot(iota((blocks, tokens), 1) >> 3 == iota((blocks, tokens), 0)).astype(BF16)
    expressed = expr_ref[grp, pl.ds(seq, 1), :].astype(F32)
    cell_rows = dot(cell_hot.astype(BF16), block_of)
    keep_rows = cell_rows * expressed
    kt_part[...] = jnp.zeros_like(kt_part)
    omega = omega_ref[...]
    zero = jnp.zeros_like(omega)
    one = jnp.ones_like(omega)
    feat_w[...] = jnp.concatenate(
        [
            jnp.concatenate([omega, zero], axis=1),
            jnp.concatenate([zero, omega], axis=1),
            jnp.concatenate([-one, zero], axis=1),
            jnp.concatenate([zero, -one], axis=1),
        ],
        axis=0,
    )

    def tables():
        cell_x[...] = hot(iota((width, blocks), 0) >> 6 == own).astype(BF16)
        cell_64[...] = hot((iota((HEADS * cells, blocks), 0) & (cells - 1)) == own).astype(BF16)
        earlier = hot(iota((blocks, blocks), 0) < iota((blocks, blocks), 1)).astype(BF16)
        rank = jnp.sum(dot(cell_hot.astype(BF16), earlier) * cell_hot, axis=0, keepdims=True)
        slot_block = own.astype(F32) * cap + rank
        slot_row[...] = dot(jnp.broadcast_to(slot_block, (8, blocks)).astype(BF16), block_of) * BLK + (
            iota((8, tokens), 1) & (BLK - 1)
        ).astype(F32)
        keep_col[...] = jnp.broadcast_to(expressed, (LANES, tokens)).T
        sums[...] = jnp.zeros_like(sums)
        counted = [jnp.zeros(dest_ref.shape[1:], F32) for _ in range(cells)]
        whole = jnp.zeros(dest_ref.shape[1:], F32)
        for g in range(dest_ref.shape[0]):
            block_sum = dot_nt(expr_ref[g].astype(F32).astype(BF16), block_of)
            whole += block_sum
            for c in range(cells):
                counted[c] += jnp.where(dest_ref[g] == c, block_sum, 0.0)
        share = jnp.zeros((1, blocks), F32)
        for c in range(cells):
            share += jnp.where(own == c, jnp.sum(counted[c], keepdims=True), 0.0)
        share = share * cells / jnp.sum(whole, keepdims=True)
        share_col[...] = lax.dot_general(
            hot(iota((tokens, blocks), 0) >> 3 == iota((tokens, blocks), 1)),
            jnp.broadcast_to(share, (LANES, blocks)),
            (((1,), (1,)), ((), ())),
            precision=lax.Precision.HIGHEST,
            preferred_element_type=F32,
        )
        head_lanes = iota((HEADS * cells * 2, D), 1) >> 6
        spread[...] = hot(
            (iota((HEADS * cells * 2, D), 0) & (HEADS * cells - 1)) >> cells.bit_length() - 1 == head_lanes
        ).astype(BF16)
        return slot_block

    def rows_at(t, tile):
        return pl.ds(pl.multiple_of(t * tile, tile), tile)

    def block_hot(t, tile):
        return hot((iota((tile, blocks), 0) + t * tile) >> 3 == iota((tile, blocks), 1)).astype(BF16)

    def fold(a, b, mask):
        left = iota((a.shape[0], LANES), 1) < DH
        a, b = a * mask, b * mask
        sum_a = sum(a[:, i : i + LANES] for i in range(0, width, LANES))
        sum_b = sum(b[:, i : i + LANES] for i in range(0, width, LANES))
        return jnp.where(left, sum_a, sum_b) + pltpu.roll(jnp.where(left, sum_b, sum_a), DH, 1)

    def unfold(x, mask):
        left = iota((x.shape[0], LANES), 1) < DH
        turned = pltpu.roll(x, DH, 1)
        a, b = jnp.where(left, x, turned), jnp.where(left, turned, x)
        copies = width // LANES
        return (
            (jnp.concatenate([a] * copies, axis=1) * mask).astype(BF16),
            (jnp.concatenate([b] * copies, axis=1) * mask).astype(BF16),
        )

    def features(x):
        xf = x.astype(F32)
        squares = (xf * xf * (0.0625 / factor)).astype(BF16)
        inner = dot(jnp.concatenate([x, squares], axis=1), feat_w[...])
        return jnp.exp2(inner * (factor * LOG2E) - 4.0)

    def feature_back(grad, feat, x):
        scaled = (grad.astype(BF16).astype(F32) * feat.astype(F32)).astype(BF16)
        through = dot_nt(scaled, feat_w[...])
        return through[:, :LANES] * factor + through[:, LANES:] * x.astype(F32) * (factor * factor)

    def total_table(ref):
        flat = ref[: cells * HEADS * FEATS // LANES].astype(F32)
        row = jnp.concatenate(
            [flat[i * cells : (i + 1) * cells] for i in range(HEADS * FEATS // LANES)], axis=1
        )
        full = jnp.concatenate([row] * HEADS, axis=0)
        shape = (HEADS * cells, HEADS * FEATS)
        return (full * hot(iota(shape, 0) >> cells.bit_length() - 1 == iota(shape, 1) >> 8)).astype(BF16)

    def pair_sums(turned, mask_rows, extra, feat_ref, j):
        totals = []
        for i in range(2):
            head = 2 * j + i
            own_rows = turned[i * DH : (i + 1) * DH]
            tall = jnp.concatenate(
                [own_rows * mask_rows[c : c + 1] for c in range(cells)] + [extra(head)], axis=0
            ).astype(BF16)
            both = dot(tall, feat_ref[:, head * FEATS : (head + 1) * FEATS])
            kv_part[j * width : (j + 1) * width, i * FEATS : (i + 1) * FEATS] = both[:width].astype(BF16)
            totals.append(both[width : width + cells])
        return totals

    def store_totals(totals):
        for i in range(0, len(totals), 2):
            tall = jnp.concatenate(
                [x[:, at : at + LANES] for x in totals[i : i + 2] for at in range(0, FEATS, LANES)], axis=0
            )
            kt_part[i * 2 * cells : (i + 2) * 2 * cells] = tall.astype(BF16)

    def front(key_feat):
        for i in range(4):
            load(i).wait()

        def project(t, carry):
            rows = rows_at(t, TILE)
            hid = dot(enc[rows], in_w[...]).astype(BF16)
            hidden[rows] = hid
            unit, _ = moments(hid.astype(F32))
            nor = (unit * gain_one_ref[...] + shift_one_ref[...]).astype(BF16)
            normed[rows] = nor
            key = dot(nor, key_w[...]).astype(BF16)
            keys[rows] = key
            values[rows] = dot(nor, value_w[...]).astype(BF16)
            for j in range(HEADS // 2):
                pair = features(key[:, j * LANES : (j + 1) * LANES])
                key_feat[rows, j * 2 * FEATS : (j + 1) * 2 * FEATS] = pair.astype(BF16)
            return carry

        lax.fori_loop(0, 1, project, 0)
        pl.semaphore_wait(barrier, len(others) + len(mates))
        slot_exchange.start(SLOTS_FIRST)
        lax.fori_loop(1, tokens // TILE, project, 0)
        totals = []
        for j in range(HEADS // 2):
            turned = lax.dot_general(
                value_w[:, j * LANES : (j + 1) * LANES],
                normed[...],
                (((0,), (1,)), ((), ())),
                preferred_element_type=F32,
            )
            totals += pair_sums(turned, keep_rows, lambda head: keep_rows, key_feat, j)
            forward_sum.tick(2 * j, 2 * j + 1)
        store_totals(totals)
        forward_sum.tick(HEADS)

    pl.run_scoped(front, pltpu.VMEM((tokens, HEADS * FEATS), BF16))

    def query_side(t, carry):
        rows = rows_at(t, TILE)
        query = dot(normed[rows], query_w[...]).astype(BF16)
        queries[rows] = query
        for j in range(HEADS // 2):
            pair = features(query[:, j * LANES : (j + 1) * LANES])
            query_feat[rows, j * 2 * FEATS : (j + 1) * 2 * FEATS] = pair.astype(BF16)
        return carry

    load(4).wait()
    pace = list(SLOTS_PACE)

    def forward_step():
        forward_sum.go_on()
        slot_exchange.start(pace.pop(0) if pace else 0)

    forward_step()
    lax.fori_loop(0, tokens // TILE, query_side, 0)
    forward_step()
    slot_block = tables()
    while forward_sum.begun():
        forward_step()
    slot_exchange.start(len(order))

    total_rows[...] = total_table(kt)
    load(5).wait()

    def layer_own():
        return pltpu.make_async_copy(slots.at[own_slots], layer_hbm.at[own_slots], copy_sem.at[2])

    def middle(stream, grad_sum, unit_two, scale_two, slopes):
        def attention(t, carry):
            rows = rows_at(t, TILE)
            here = block_hot(t, TILE)
            mask = dot_nt(here, cell_x[...])
            den = dot_nt(query_feat[rows], total_rows[...]) * dot_nt(here, cell_64[...])
            den_high = den.astype(BF16)
            den_low = (den - den_high.astype(F32)).astype(BF16)
            den_both = jnp.concatenate([den_high, den_low], axis=1)
            den_pair[rows] = den_both
            over = 1.0 / dot(den_both, spread[...])
            for j in range(HEADS // 2):
                at = pl.ds(j * width, width)
                num = fold(
                    dot_nt(query_feat[rows, j * 2 * FEATS : j * 2 * FEATS + FEATS], kv[at, :FEATS]),
                    dot_nt(query_feat[rows, j * 2 * FEATS + FEATS : (j + 1) * 2 * FEATS], kv[at, FEATS:]),
                    mask,
                )
                lanes = slice(j * LANES, (j + 1) * LANES)
                attended[rows, lanes] = (num * over[:, lanes]).astype(BF16)
            mixed = hidden[rows].astype(F32) + dot(attended[rows], out_w[...])
            stream[rows] = mixed
            unit, scale = moments(mixed)
            unit_two[rows] = unit.astype(BF16)
            scale_two[rows] = jnp.broadcast_to(scale, (TILE, LANES))
            normed_two[rows] = (unit * gain_two_ref[...] + shift_two_ref[...]).astype(BF16)
            return carry

        lax.fori_loop(0, tokens // TILE, attention, 0)

        for j in range(hidden_tiles):
            ff = slice(j * D, (j + 1) * D)

            def feed(t, carry):
                rows = rows_at(t, WIDE)
                x = dot(normed_two[rows], up_w[ff])
                square = x * x
                bent = jnp.tanh(x * (GELU_A + (GELU_A * GELU_B) * square))
                ramp = 0.5 + 0.5 * bent
                slope = ramp + (0.5 * x) * (1.0 - bent * bent) * (
                    GELU_A + (3.0 * GELU_A * GELU_B) * square
                )
                active = (x * ramp).astype(BF16)
                there = pl.ds(pl.multiple_of(j * tokens + t * WIDE, WIDE), WIDE)
                early_part[there] = active
                slopes[there] = slope.astype(BF16)
                stream[rows] += dot(active, down_w[ff])
                return carry

            for i in range(8 + j, matrices, hidden_tiles):
                load(i).wait()
            if j == 0:
                load(6).wait()
            lax.fori_loop(0, tokens // WIDE, feed, 0)

        slot_exchange.wait()
        load(7).wait()

        def gather(t, carry):
            rows = rows_at(t, TILE)
            slot_col = dot_nt(
                block_hot(t, TILE), jnp.broadcast_to(slot_block, (LANES, blocks)).astype(BF16)
            ) * BLK + (iota((TILE, LANES), 0) & (BLK - 1)).astype(F32)
            pick = jnp.concatenate(
                [
                    hot(slot_col == (iota((TILE, LANES), 1) + i).astype(F32)).astype(BF16)
                    for i in range(0, slots.shape[0], LANES)
                ],
                axis=1,
            )
            share = jnp.concatenate([share_col[rows]] * (D // LANES), axis=1)
            cot[rows] = (dot(pick, slots[...]) * share).astype(BF16)
            grad_att[rows] = stream[rows].astype(BF16)
            return carry

        lax.fori_loop(0, tokens // TILE, gather, 0)
        for k in list(range(1, cells)) + [0]:
            cell = lax.rem(grp + k, cells)
            pick = hot(
                slot_row[0:1] == (iota((pair_rows, tokens), 0) + cell * pair_rows).astype(F32)
            ).astype(BF16)
            here = pl.ds(pl.multiple_of(cell * pair_rows, pair_rows), pair_rows)
            slots[here] = dot(pick, grad_att[...]).astype(BF16)
            if 0 < k <= LAYER_FIRST:
                layer_exchange.start(1)
        layer_own().start()

        for j in range(hidden_tiles):
            ff = slice(j * D, (j + 1) * D)

            def feed_back(t, carry):
                rows = rows_at(t, WIDE)
                there = pl.ds(pl.multiple_of(j * tokens + t * WIDE, WIDE), WIDE)
                grad_up = (slopes[there].astype(F32) * dot_nt(cot[rows], down_w[ff])).astype(BF16)
                slopes[there] = grad_up
                back = dot_nt(grad_up, up_w[ff])
                if j == 0:
                    grad_sum[rows] = back
                else:
                    grad_sum[rows] += back
                return carry

            lax.fori_loop(0, tokens // WIDE, feed_back, 0)
            layer_exchange.start(LAYER_FEED)

        def back(t, carry):
            rows = rows_at(t, TILE)
            here = block_hot(t, TILE)
            grad_nor = grad_sum[rows]
            unit = unit_two[rows].astype(F32)
            sums[0:8] += jnp.sum((grad_nor * unit).reshape(TILE // 8, 8, D), axis=0)
            sums[8:16] += jnp.sum(grad_nor.reshape(TILE // 8, 8, D), axis=0)
            scale = jnp.concatenate([scale_two[rows]] * (D // LANES), axis=1)
            grad_mix = (
                cot[rows].astype(F32) + norm_back(grad_nor, gain_two_ref[...], unit, scale)
            ).astype(BF16)
            grad_att[rows] = grad_mix
            grad = dot_nt(grad_mix, out_w[...]) / dot(den_pair[rows], spread[...])
            grad_num[rows] = grad.astype(BF16)
            products = (grad * attended[rows].astype(F32)).astype(BF16)
            den_grad[rows] = dot_nt(products, spread[: HEADS * cells]) * dot_nt(here, cell_64[...]) * -1.0
            return carry

        lax.fori_loop(0, tokens // TILE, back, 0)

        den_rows = jnp.concatenate(
            [den_grad[...], jnp.zeros((tokens, LANES - HEADS * cells), F32)], axis=1
        ).T
        totals = []
        for j in range(HEADS // 2):
            turned = grad_num[:, j * LANES : (j + 1) * LANES].astype(F32).T
            totals += pair_sums(
                turned, cell_rows, lambda head: den_rows[head * cells : (head + 1) * cells], query_feat, j
            )
            backward_sum.tick(2 * j, 2 * j + 1)
        store_totals(totals)
        backward_sum.tick(HEADS)

        for j in range(hidden_tiles):
            down_term = dot_tn(early_part[j * tokens : (j + 1) * tokens], cot[...]).astype(BF16)
            up_term = dot_tn(normed_two[...], slopes[j * tokens : (j + 1) * tokens]).astype(BF16)
            early_part[2 * j * D : (2 * j + 1) * D] = down_term
            early_part[(2 * j + 1) * D : (2 * j + 2) * D] = up_term
            back_step()
            early_sum.tick(2 * j, 2 * j + 1)

    back_pace = list(LAYER_PACE)

    def back_step():
        backward_sum.go_on()
        early_sum.go_on_half()
        layer_exchange.start(back_pace.pop(0) if back_pace else 0)

    pl.run_scoped(
        middle,
        pltpu.VMEM((tokens, D), F32),
        pltpu.VMEM((tokens, D), F32),
        pltpu.VMEM((tokens, D), BF16),
        pltpu.VMEM((tokens, LANES), F32),
        pltpu.VMEM((hidden_tiles * tokens, D), BF16),
    )

    early_window = early_sum.go_on if EARLY_WINDOW else early_sum.go_on_half

    def end(key_feat):
        def query_back(t, carry):
            rows = rows_at(t, TILE)
            mask = dot_nt(block_hot(t, TILE), cell_x[...])
            den = den_grad[rows].astype(BF16)
            for j in range(HEADS // 2):
                lanes = slice(j * LANES, (j + 1) * LANES)
                feats = slice(j * 2 * FEATS, (j + 1) * 2 * FEATS)
                a, b = unfold(grad_num[rows, lanes].astype(F32), mask)
                at = pl.ds(j * width, width)
                grad = jnp.concatenate([dot(a, kv[at, :FEATS]), dot(b, kv[at, FEATS:])], axis=1)
                grad += dot(den, total_rows[:, feats])
                queries[rows, lanes] = feature_back(
                    grad, query_feat[rows, feats], queries[rows, lanes]
                ).astype(BF16)
            return carry

        out_row = 2 * hidden_tiles * D
        early_part[out_row : out_row + D] = dot_tn(attended[...], grad_att[...]).astype(BF16)
        back_step()
        early_sum.tick(2 * hidden_tiles)
        lax.fori_loop(0, tokens // TILE // 2, query_back, 0)
        back_step()
        lax.fori_loop(tokens // TILE // 2, tokens // TILE, query_back, 0)
        early_part[out_row + D : out_row + 2 * D] = dot_tn(normed[...], queries[...]).astype(BF16)
        back_step()
        early_sum.tick(2 * hidden_tiles + 1)

        def key_side(t, carry):
            rows = rows_at(t, TILE)
            for j in range(HEADS // 2):
                pair = features(keys[rows, j * LANES : (j + 1) * LANES])
                key_feat[rows, j * 2 * FEATS : (j + 1) * 2 * FEATS] = pair.astype(BF16)
            return carry

        lax.fori_loop(0, tokens // TILE, key_side, 0)
        while backward_sum.begun():
            back_step()

        total_rows[...] = total_table(kt_grad)

        def key_back(t, carry):
            rows = rows_at(t, TILE)
            here = block_hot(t, TILE)
            keep = keep_col[rows]
            mask = dot_nt(here, cell_x[...]) * jnp.concatenate([keep] * (width // LANES), axis=1)
            mask_64 = (dot_nt(here, cell_64[...]) * keep[:, : HEADS * cells]).astype(BF16)
            for j in range(HEADS // 2):
                lanes = slice(j * LANES, (j + 1) * LANES)
                feats = slice(j * 2 * FEATS, (j + 1) * 2 * FEATS)
                a, b = unfold(values[rows, lanes].astype(F32), mask)
                at = pl.ds(j * width, width)
                feat = key_feat[rows, feats]
                grad = jnp.concatenate([dot(a, kv_grad[at, :FEATS]), dot(b, kv_grad[at, FEATS:])], axis=1)
                grad += dot(mask_64, total_rows[:, feats])
                keys[rows, lanes] = feature_back(grad, feat, keys[rows, lanes]).astype(BF16)
                values[rows, lanes] = fold(
                    dot_nt(feat[:, :FEATS], kv_grad[at, :FEATS]),
                    dot_nt(feat[:, FEATS:], kv_grad[at, FEATS:]),
                    mask,
                ).astype(BF16)
            return carry

        lax.fori_loop(0, tokens // TILE // 2, key_back, 0)
        early_window()
        layer_exchange.start(LAYER_LATE)
        lax.fori_loop(tokens // TILE // 2, tokens // TILE, key_back, 0)
        early_window()
        layer_exchange.start(LAYER_LATE)
        kv_part[0:D] = dot_tn(normed[...], keys[...]).astype(BF16)
        kv_part[D : 2 * D] = dot_tn(normed[...], values[...]).astype(BF16)
        late_sum.tick(0, 1, 2, 3)

        def hidden_back(t, carry):
            rows = rows_at(t, TILE)
            grad_nor = (
                dot_nt(queries[rows], query_w[...])
                + dot_nt(keys[rows], key_w[...])
                + dot_nt(values[rows], value_w[...])
            )
            unit, scale = moments(hidden[rows].astype(F32))
            sums[16:24] += jnp.sum((grad_nor * unit).reshape(TILE // 8, 8, D), axis=0)
            sums[24:32] += jnp.sum(grad_nor.reshape(TILE // 8, 8, D), axis=0)
            cot[rows] = (
                grad_att[rows].astype(F32) + norm_back(grad_nor, gain_one_ref[...], unit, scale)
            ).astype(BF16)
            return carry

        lax.fori_loop(0, tokens // TILE, hidden_back, 0)
        early_window()
        late_sum.tick(0, 1, 2, 3)
        kv_part[2 * D : 2 * D + D_IN] = dot_tn(enc[...], cot[...]).astype(BF16)
        small = jnp.concatenate(
            [jnp.sum(sums[8 * i : 8 * i + 8], axis=0, keepdims=True) for i in range(4)]
            + [jnp.zeros((12, D), F32)],
            axis=0,
        )
        at = 2 * D + D_IN
        kv_part[at : at + 16] = small.astype(BF16)
        kv_part[at + 16 :] = jnp.zeros((kv_part.shape[0] - at - 16, D), BF16)
        late_sum.tick(4, 5, 6, 7)
        early_window()
        layer_exchange.start(LAYER_LATE)

        def encoder_grad(t, carry):
            rows = rows_at(t, TILE)
            enc[rows] = dot_nt(cot[rows], in_w[...]).astype(BF16)
            return carry

        lax.fori_loop(0, tokens // TILE, encoder_grad, 0)
        enc_copy = pltpu.make_async_copy(enc, enc_grad_hbm, copy_sem.at[3])
        enc_copy.start()
        while late_sum.begun():
            late_sum.go_on()
            early_sum.go_on_half()
            layer_exchange.start(LAYER_LATE)
        early_sum.run()
        ends = []
        for i, (at, rows, target) in enumerate(
            (
                (0, D, key_sum_hbm),
                (D, D, value_sum_hbm),
                (2 * D, D_IN, in_sum_hbm),
                (2 * D + D_IN, 16, small_sum_hbm),
            )
        ):
            ends.append(pltpu.make_async_copy(kv.at[pl.ds(at, rows)], target, copy_sem.at[4 + i]))
            ends[-1].start()
        layer_exchange.wait()
        layer_own().wait()
        enc_copy.wait()
        for copy in ends:
            copy.wait()

    pl.run_scoped(end, pltpu.VMEM((tokens, HEADS * FEATS), BF16))


def widen_kernel(places, *refs):
    count = len(places)
    sources, targets = refs[:count], refs[count : 2 * count]
    narrow, wide, in_sem, out_sem = refs[2 * count :]
    depth = narrow.shape[0]
    chunks = []
    for n, (rows, columns) in enumerate(places):
        for at in range(0, rows, D):
            for left in range(0, columns, D):
                chunks.append((n, at, min(D, rows - at), left))

    def come(i):
        n, at, rows, left = chunks[i]
        source = sources[n].at[pl.ds(at, rows), pl.ds(left, D)]
        return pltpu.make_async_copy(source, narrow.at[i % depth, pl.ds(0, rows)], in_sem.at[i % depth])

    def go(i):
        n, at, rows, left = chunks[i]
        target = targets[n].at[pl.ds(at, rows), pl.ds(left, D)]
        return pltpu.make_async_copy(wide.at[i % depth, pl.ds(0, rows)], target, out_sem.at[i % depth])

    for i in range(min(depth, len(chunks))):
        come(i).start()
    for i in range(len(chunks)):
        rows = chunks[i][2]
        come(i).wait()
        if i >= depth:
            go(i - depth).wait()
        wide[i % depth, :rows] = narrow[i % depth, :rows].astype(F32)
        go(i).start()
        if i + depth < len(chunks):
            come(i + depth).start()
    for i in range(max(0, len(chunks) - depth), len(chunks)):
        go(i).wait()


def widen(*arrays):
    rest = pl.BlockSpec(memory_space=pl.ANY)
    results = pl.pallas_call(
        functools.partial(widen_kernel, tuple(a.shape for a in arrays)),
        out_shape=[jax.ShapeDtypeStruct(a.shape, F32) for a in arrays],
        in_specs=[rest] * len(arrays),
        out_specs=[rest] * len(arrays),
        scratch_shapes=[
            pltpu.VMEM((WIDEN_DEPTH, D, D), BF16),
            pltpu.VMEM((WIDEN_DEPTH, D, D), F32),
            pltpu.SemaphoreType.DMA((WIDEN_DEPTH,)),
            pltpu.SemaphoreType.DMA((WIDEN_DEPTH,)),
        ],
        compiler_params=pltpu.CompilerParams(vmem_limit_bytes=VMEM_LIMIT),
        name="widen",
    )(*arrays)
    return results


def fused(
    mesh,
    encoded,
    destination,
    expressed,
    in_proj,
    gain_one,
    shift_one,
    query_w,
    key_w,
    value_w,
    out_w,
    gain_two,
    shift_two,
    up_w,
    down_w,
    random_features,
    out_cotangent,
):
    sizes = {"grp": mesh.shape["grp"], "seq": mesh.shape["seq"]}
    cells, splits, blocks = destination.shape
    tokens = encoded.shape[2]
    slot_total = out_cotangent.shape[2]
    cap = slot_total // (cells * BLK)
    width = cells * DH
    digits = digits_of(sizes)
    unit = 16 * sizes["grp"] * sizes["seq"]
    steps = 2 * sum(radix - 1 for _, _, radix in digits)
    early = 2 * FF + 2 * D
    half = HEADS // 2 * width
    count = HEADS + 1 + early // unit

    def vmem(shape, kind=BF16):
        return pltpu.VMEM(shape, kind)

    def shape(*dims):
        return jax.ShapeDtypeStruct(dims, BF16)

    rest = pl.BlockSpec(memory_space=pl.ANY)
    results = pl.pallas_call(
        functools.partial(fused_kernel, sizes, cap),
        out_shape=(
            shape(slot_total, D),
            shape(tokens, D_IN),
            shape(D_IN, D),
            shape(D, D),
            shape(D, D),
            shape(D, D),
            shape(D, D),
            shape(D, FF),
            shape(FF, D),
            shape(16, D),
        ),
        in_specs=[rest] * 16,
        out_specs=(rest,) * 10,
        scratch_shapes=[
            vmem(destination.shape, jnp.int32),
            vmem(expressed.shape, jnp.int32),
            vmem((1, D), F32),
            vmem((1, D), F32),
            vmem((1, D), F32),
            vmem((1, D), F32),
            vmem((DH, FEATS)),
            vmem((tokens, D_IN)),
            vmem((D_IN, D)),
            vmem((D, D)),
            vmem((D, D)),
            vmem((D, D)),
            vmem((D, D)),
            vmem((FF, D)),
            vmem((FF, D)),
            vmem((slot_total, D)),
            vmem((tokens, D)),
            vmem((tokens, D)),
            vmem((tokens, D)),
            vmem((tokens, D)),
            vmem((tokens, D)),
            vmem((tokens, D)),
            vmem((tokens, HEADS * FEATS)),
            vmem((half, 2 * FEATS)),
            vmem((half, 2 * FEATS)),
            vmem((half, 2 * FEATS)),
            vmem((half, 2 * FEATS)),
            vmem((unit, LANES)),
            vmem((unit, LANES)),
            vmem((unit, LANES)),
            vmem((unit, LANES)),
            vmem((tokens, D)),
            vmem((tokens, D)),
            vmem((tokens, D)),
            vmem((tokens, D)),
            vmem((tokens, 2 * HEADS * cells)),
            vmem((tokens, HEADS * cells), F32),
            vmem((early, D)),
            vmem((early, D)),
            vmem((early // unit * 16, D)),
            vmem((4 * DH, 2 * FEATS)),
            vmem((width, blocks)),
            vmem((HEADS * cells, blocks)),
            vmem((tokens, LANES), F32),
            vmem((tokens, LANES), F32),
            vmem((8, tokens), F32),
            vmem((HEADS * cells, HEADS * FEATS)),
            vmem((2 * HEADS * cells, D)),
            vmem((32, D), F32),
            pltpu.SemaphoreType.DMA((15 + FF // D,)),
            pltpu.SemaphoreType.DMA((PARTS * (cells - 1),)),
            pltpu.SemaphoreType.DMA((PARTS * (cells - 1),)),
            pltpu.SemaphoreType.DMA((PARTS * (cells - 1),)),
            pltpu.SemaphoreType.DMA((PARTS * (cells - 1),)),
            pltpu.SemaphoreType.DMA((8,)),
            pltpu.SemaphoreType.DMA((early // unit,)),
            pltpu.SemaphoreType.DMA((count * steps,)),
            pltpu.SemaphoreType.DMA((count * steps,)),
        ],
        compiler_params=pltpu.CompilerParams(
            collective_id=1, has_side_effects=True, vmem_limit_bytes=VMEM_LIMIT
        ),
        name="layer_and_gradients",
    )(
        destination,
        expressed,
        gain_one.reshape(1, D),
        shift_one.reshape(1, D),
        gain_two.reshape(1, D),
        shift_two.reshape(1, D),
        random_features,
        encoded.reshape(tokens, D_IN),
        in_proj,
        query_w,
        key_w,
        value_w,
        out_w,
        up_w,
        down_w,
        out_cotangent.reshape(slot_total, D),
    )
    layer, enc_grad, in_b, query_b, key_b, value_b, out_b, up_b, down_b, small_b = results
    layer, down, up, in_sum, query, key, value, out = widen(
        layer, down_b, up_b, in_b, query_b, key_b, value_b, out_b
    )
    small = small_b.astype(F32)
    return (
        layer.reshape(1, 1, slot_total, D),
        enc_grad.reshape(1, 1, tokens, D_IN),
        in_sum,
        small[2],
        small[3],
        query,
        key,
        value,
        out,
        small[0],
        small[1],
        up,
        down,
    )


def layer_norm(values, gain, shift):
    center = values - jnp.mean(values, axis=-1, keepdims=True)
    variance = jnp.mean(center * center, axis=-1, keepdims=True)
    return center * lax.rsqrt(variance + 1e-05) * gain + shift


def feature_map(projected, omega_b, key_keep):
    row_count = projected.shape[0]
    pieces = projected.reshape(row_count, HEADS, DH)
    factor = DH ** (-0.25)
    logits = jnp.einsum("nhd,dm->nhm", pieces, omega_b, preferred_element_type=jnp.float32) * factor
    squares = (
        0.5
        * factor
        * factor
        * jnp.sum(jnp.square(pieces.astype(jnp.float32)), axis=-1, keepdims=True)
    )
    return jnp.exp(logits - squares) * FEATS ** (-0.5) * key_keep[:, None, None]


def feature_grad(grad_feat, feat_full, projected, omega_b):
    row_count = projected.shape[0]
    factor = DH ** (-0.25)
    scaled = grad_feat.astype(jnp.float32) * feat_full
    logit_grad = scaled.astype(jnp.bfloat16)
    pieces = projected.reshape(row_count, HEADS, DH).astype(jnp.float32)
    through = (
        jnp.einsum("nhm,dm->nhd", logit_grad, omega_b, preferred_element_type=jnp.float32) * factor
    )
    direct = pieces * (factor * factor) * jnp.sum(scaled, axis=-1, keepdims=True)
    return (through - direct).reshape(row_count, HEADS * DH).astype(jnp.bfloat16)


def weight_term(left, right):
    return jnp.einsum("nk,nd->kd", left, right, preferred_element_type=jnp.float32)


def plain(
    encoded,
    destination,
    expressed,
    in_proj,
    gain_one,
    shift_one,
    query_w,
    key_w,
    value_w,
    out_w,
    gain_two,
    shift_two,
    up_w,
    down_w,
    random_features,
    out_cotangent,
):
    cell_count = destination.shape[0]
    split_count = destination.shape[1]
    blocks = destination.shape[2]
    tokens = encoded.shape[2]
    block_len = tokens // blocks
    row_total = out_cotangent.shape[2]
    slot_count = row_total // (cell_count * block_len)
    pair_rows = slot_count * block_len
    group_index = lax.axis_index("grp")
    split_index = lax.axis_index("seq")
    targets = jnp.arange(cell_count, dtype=jnp.int32)
    slot_ids = jnp.arange(slot_count, dtype=jnp.int32)
    within = jnp.arange(block_len, dtype=jnp.int32)
    block_ids = jnp.arange(blocks, dtype=jnp.int32)
    column = lax.dynamic_index_in_dim(destination, split_index, 1, keepdims=False)
    block_hits = (column[:, :, None] == targets).astype(jnp.int32)
    block_rank = jnp.sum(jnp.cumsum(block_hits, axis=1) * block_hits, axis=2) - 1
    own_dest = lax.dynamic_index_in_dim(column, group_index, 0, keepdims=False)
    own_rank = lax.dynamic_index_in_dim(block_rank, group_index, 0, keepdims=False)
    send_match = (
        (own_dest[:, None, None] == targets[:, None]) & (own_rank[:, None, None] == slot_ids)
    ).astype(jnp.int32)
    send_found = jnp.sum(send_match, axis=0)
    send_block = jnp.sum(send_match * block_ids[:, None, None], axis=0)
    send_index = (send_block[:, :, None] * block_len + within).reshape(-1)
    send_keep = jnp.repeat(send_found.reshape(-1), block_len).astype(jnp.bfloat16)
    back_index = ((own_dest * slot_count + own_rank)[:, None] * block_len + within).reshape(-1)
    recv_match = (
        (column[:, :, None] == group_index) & (block_rank[:, :, None] == slot_ids)
    ).astype(jnp.int32)
    recv_found = jnp.sum(recv_match, axis=1)
    recv_block = jnp.sum(recv_match * block_ids[:, None], axis=1)
    recv_token = (recv_block[:, :, None] * block_len + within).reshape(cell_count, pair_rows)
    expressed_col = lax.dynamic_index_in_dim(expressed, split_index, 1, keepdims=False)
    valid = jnp.repeat(recv_found.reshape(-1), block_len).astype(jnp.float32)
    key_keep = (
        jnp.take_along_axis(expressed_col, recv_token, axis=1).reshape(-1).astype(jnp.float32)
        * valid
    )
    block_sum = jnp.sum(expressed.reshape(cell_count, split_count, blocks, block_len), axis=3)
    dest_hits = destination[..., None] == targets
    counts = jnp.sum(jnp.where(dest_hits, block_sum[..., None], 0), axis=(0, 1, 2)).astype(
        jnp.float32
    )
    own_count = lax.dynamic_index_in_dim(counts, group_index, 0, keepdims=False)
    share = cell_count * own_count / jnp.sum(counts)
    token_rows = encoded.reshape(tokens, D_IN)
    token_hidden = jnp.dot(token_rows, in_proj, preferred_element_type=jnp.float32).astype(
        jnp.bfloat16
    )
    outgoing = jnp.take(token_hidden, send_index, axis=0) * send_keep[:, None]
    hidden_b = lax.all_to_all(
        outgoing.reshape(cell_count, pair_rows, D),
        "grp",
        split_axis=0,
        concat_axis=0,
        tiled=True,
    ).reshape(row_total, D)
    hidden_f = hidden_b.astype(jnp.float32)
    normed_f, norm_one_pull = jax.vjp(layer_norm, hidden_f, gain_one, shift_one)
    normed_b = normed_f.astype(jnp.bfloat16)
    queries_b = jnp.dot(normed_b, query_w, preferred_element_type=jnp.float32).astype(jnp.bfloat16)
    keys_b = jnp.dot(normed_b, key_w, preferred_element_type=jnp.float32).astype(jnp.bfloat16)
    values_b = jnp.dot(normed_b, value_w, preferred_element_type=jnp.float32).astype(jnp.bfloat16)
    query_full = feature_map(queries_b, random_features, jnp.ones((row_total,), jnp.float32))
    key_full = feature_map(keys_b, random_features, key_keep)
    query_feature_rows = query_full.astype(jnp.bfloat16)
    key_feature_rows = key_full.astype(jnp.bfloat16)
    value_per_head = values_b.reshape(row_total, HEADS, DH)
    value_part = jnp.einsum(
        "pgk,pgz->gkz", key_feature_rows, value_per_head, preferred_element_type=jnp.float32
    )
    total_part = jnp.sum(key_feature_rows, axis=0, dtype=jnp.float32)
    key_value_products, key_total = lax.psum((value_part, total_part), "seq")
    key_value_batched = key_value_products.astype(jnp.bfloat16)
    attention_numerator = jnp.einsum(
        "bli,lie->ble", query_feature_rows, key_value_batched, preferred_element_type=jnp.float32
    )
    denominator = jnp.sum(query_feature_rows.astype(jnp.float32) * key_total[None], axis=-1)
    attended_b = (
        (attention_numerator / denominator[:, :, None]).reshape(row_total, D).astype(jnp.bfloat16)
    )
    mixed = hidden_f + jnp.dot(attended_b, out_w, preferred_element_type=jnp.float32)
    normed_two_f, norm_two_pull = jax.vjp(layer_norm, mixed, gain_two, shift_two)
    normed_two_b = normed_two_f.astype(jnp.bfloat16)
    expanded = jnp.dot(normed_two_b, up_w, preferred_element_type=jnp.float32)
    activated_f, gelu_pull = jax.vjp(partial_gelu, expanded)
    activated_b = activated_f.astype(jnp.bfloat16)
    layer_out = (mixed + jnp.dot(activated_b, down_w, preferred_element_type=jnp.float32)) * valid[
        :, None
    ]
    grad_out = out_cotangent.reshape(row_total, D).astype(jnp.float32) * (valid * share)[:, None]
    grad_mlp = grad_out.astype(jnp.bfloat16)
    down_term = weight_term(activated_b, grad_mlp)
    grad_activated = jnp.dot(grad_mlp, down_w.T, preferred_element_type=jnp.float32)
    grad_up = gelu_pull(grad_activated)[0].astype(jnp.bfloat16)
    up_term = weight_term(normed_two_b, grad_up)
    grad_normed_two = jnp.dot(grad_up, up_w.T, preferred_element_type=jnp.float32)
    mixed_back, gain_two_term, shift_two_term = norm_two_pull(grad_normed_two)
    grad_mixed = grad_out + mixed_back
    grad_att = grad_mixed.astype(jnp.bfloat16)
    out_term = weight_term(attended_b, grad_att)
    grad_attended = jnp.dot(grad_att, out_w.T, preferred_element_type=jnp.float32).reshape(
        row_total, HEADS, DH
    )
    numerator_gradient = (grad_attended / denominator[:, :, None]).astype(jnp.bfloat16)
    grad_den = -jnp.sum(grad_attended * attention_numerator, axis=-1) / (denominator * denominator)
    value_grad_part = jnp.einsum(
        "pgk,pgz->gkz", query_feature_rows, numerator_gradient, preferred_element_type=jnp.float32
    )
    total_grad_part = jnp.sum(query_feature_rows.astype(jnp.float32) * grad_den[:, :, None], axis=0)
    grad_query_feat = (
        jnp.einsum(
            "pao,ajo->paj",
            numerator_gradient,
            key_value_batched,
            preferred_element_type=jnp.float32,
        )
        + grad_den[:, :, None] * key_total[None]
    ).astype(jnp.bfloat16)
    grad_kv, grad_total = lax.psum((value_grad_part, total_grad_part), "seq")
    key_value_gradient_batched = grad_kv.astype(jnp.bfloat16)
    grad_key_feat = (
        jnp.einsum(
            "pao,ajo->paj",
            value_per_head,
            key_value_gradient_batched,
            preferred_element_type=jnp.float32,
        )
        + grad_total[None]
    ).astype(jnp.bfloat16)
    grad_values = (
        jnp.einsum(
            "bli,lie->ble",
            key_feature_rows,
            key_value_gradient_batched,
            preferred_element_type=jnp.float32,
        )
        .reshape(row_total, D)
        .astype(jnp.bfloat16)
    )
    grad_queries = feature_grad(grad_query_feat, query_full, queries_b, random_features)
    grad_keys = feature_grad(grad_key_feat, key_full, keys_b, random_features)
    query_term = weight_term(normed_b, grad_queries)
    key_term = weight_term(normed_b, grad_keys)
    value_term = weight_term(normed_b, grad_values)
    grad_normed = jnp.dot(grad_queries, query_w.T, preferred_element_type=jnp.float32)
    grad_normed = grad_normed + jnp.dot(grad_keys, key_w.T, preferred_element_type=jnp.float32)
    grad_normed = grad_normed + jnp.dot(grad_values, value_w.T, preferred_element_type=jnp.float32)
    hidden_back, gain_one_term, shift_one_term = norm_one_pull(grad_normed)
    grad_hidden = (grad_mixed + hidden_back).astype(jnp.bfloat16)
    returned = lax.all_to_all(
        grad_hidden.reshape(cell_count, pair_rows, D),
        "grp",
        split_axis=0,
        concat_axis=0,
        tiled=True,
    )
    token_grad = jnp.take(returned.reshape(row_total, D), back_index, axis=0)
    encoded_grad = jnp.dot(token_grad, in_proj.T, preferred_element_type=jnp.float32).astype(
        jnp.bfloat16
    )
    in_term = weight_term(token_rows, token_grad)
    (
        in_sum,
        query_sum,
        key_sum,
        value_sum,
        out_sum,
        up_sum,
        down_sum,
        gain_one_sum,
        shift_one_sum,
        gain_two_sum,
        shift_two_sum,
    ) = lax.psum(
        (
            in_term,
            query_term,
            key_term,
            value_term,
            out_term,
            up_term,
            down_term,
            gain_one_term,
            shift_one_term,
            gain_two_term,
            shift_two_term,
        ),
        ("grp", "seq"),
    )
    return (
        layer_out.reshape(1, 1, row_total, D),
        encoded_grad.reshape(1, 1, tokens, D_IN),
        in_sum,
        gain_one_sum,
        shift_one_sum,
        query_sum,
        key_sum,
        value_sum,
        out_sum,
        gain_two_sum,
        shift_two_sum,
        up_sum,
        down_sum,
    )


def partial_gelu(values):
    return jax.nn.gelu(values, approximate=True)


def solution(mesh):
    in_specs = (
        P("grp", "seq", None, None),
        P(),
        P(),
        P(),
        P(),
        P(),
        P(),
        P(),
        P(),
        P(),
        P(),
        P(),
        P(),
        P(),
        P(),
        P("grp", "seq", None, None),
    )
    out_specs = (
        P("grp", "seq", None, None),
        P("grp", "seq", None, None),
        P(),
        P(),
        P(),
        P(),
        P(),
        P(),
        P(),
        P(),
        P(),
        P(),
        P(),
    )
    body = functools.partial(fused, mesh) if mesh.shape["grp"] <= FUSED_CELLS else plain
    return jax.shard_map(body, mesh=mesh, in_specs=in_specs, out_specs=out_specs, check_vma=False)
```
